32 devices in a mesh: dp: 8 (over y, x, core), rows: 4 (over z).
Axes of the slice: x: 2, y: 2, z: 4, core: 2. Of those that a mesh axis runs over, the one named last changes fastest.
Arguments:
- tokens: bfloat16 [16, 5, 32, 32, 512], P('dp', None, 'rows'), may hold values from -6 to 6
- video_flag: int32 [16], P('dp'), may hold values from 0 to 1, as said below
- frame_count: int32 [16], P('dp'), may hold values from 1 to 5, as said below
- norm_gain: float32 [4, 512], replicated, may hold values from 0.5 to 1.5
- norm_bias: float32 [4, 512], replicated, may hold values from -3 to 3
- w_qkv: bfloat16 [2, 512, 1536], replicated, may hold values from -0.25 to 0.25
- w_proj: bfloat16 [2, 512, 512], replicated, may hold values from -0.5 to 0.5
- w_up: bfloat16 [2, 512, 2048], replicated, may hold values from -0.25 to 0.25
- w_down: bfloat16 [2, 2048, 512], replicated, may hold values from -0.125 to 0.125
- out_bias: float32 [4, 512], replicated, may hold values from -3 to 3
- up_bias: float32 [2, 2048], replicated, may hold values from -3 to 3
- cotangent: bfloat16 [16, 5, 32, 32, 512], P('dp', None, 'rows'), may hold values from -6 to 6
Outputs:
- layer_out: bfloat16 [16, 5, 32, 32, 512], P('dp', None, 'rows')
- grad_tokens: bfloat16 [16, 5, 32, 32, 512], P('dp', None, 'rows')
- grad_norm_gain: float32 [4, 512], P(None, 'rows')
- grad_norm_bias: float32 [4, 512], P(None, 'rows')
- grad_qkv: float32 [2, 512, 1536], P(None, 'rows')
- grad_proj: float32 [2, 512, 512], P(None, 'rows')
- grad_up: float32 [2, 512, 2048], P(None, 'rows')
- grad_down: float32 [2, 2048, 512], P(None, 'rows')
- grad_out_bias: float32 [4, 512], P(None, 'rows')
- grad_up_bias: float32 [2, 2048], P(None, 'rows')
The draws below stay inside these ranges and needn't reach their ends.
Inputs may be any that keep to these rules, and one draw needn't show every extreme that they name: `video_flag`: 1 marks a video, 0 an image; at least one item is a video. `frame_count`: valid frame slots of the item: 1 for every image, 1 to 5 for a video, exactly 5 for at least one video in every draw.
All inputs are finite; a program needn't handle non-finite values.
Results may differ from the reference program's by a relative error of at most 0.02.
Values may be sent and summed in bfloat16 or wider, within the bound.
No kernel may reach another device: no remote copies, remote signals or barrier semaphores. Data moves between devices by JAX's collectives and lax.ppermute only.
A program may use at most 448 MiB of HBM per device.

```python
import jax
import jax.numpy as jnp
from jax import lax

D = 512
FF = 2048
HEADS = 8
HEAD_DIM = 64
WIN = 8
SHIFT = 4
W = 32
TG = 5
ITEMS = 16
H = 32


def item_kinds(key):
    flag_key, count_key, pick_key = jax.random.split(key, 3)
    flags = jax.random.randint(flag_key, (ITEMS,), 0, 2)
    frames = jax.random.randint(count_key, (ITEMS,), 1, TG + 1)
    chosen = jax.random.randint(pick_key, (), 0, ITEMS)
    flags = flags.at[chosen].set(1)
    frames = jnp.where(flags == 1, frames, 1).at[chosen].set(TG)
    return (flags.astype(jnp.int32), frames.astype(jnp.int32))


def draw_video_flag(key, part):
    return item_kinds(key)[0]


def draw_frame_count(key, part):
    return item_kinds(key)[1]


def shard_levels(key, shape, cuts, smallest, high):
    def one(dim, parts):
        steps = jax.random.uniform(jax.random.fold_in(jax.random.fold_in(key, 6), dim), (parts,), jnp.float32, smallest / len(cuts), high / len(cuts))
        return jnp.repeat(jnp.exp(steps), shape[dim] // parts).reshape((-1,) + (1,) * (len(shape) - dim - 1))

    level = one(*cuts[0])
    for cut in cuts[1:]:
        level = level * one(*cut)
    return level


def normal_values(stream_key, shape, deviation, limit, cuts=(), kind=jnp.bfloat16):
    factor_of = shard_levels(stream_key, shape, cuts, -0.22, 0.18) if cuts else 1.0
    values = jax.random.normal(stream_key, shape, jnp.float32) * deviation * factor_of
    return jnp.minimum(jnp.maximum(values, -limit), limit).astype(kind)


def setup_inputs(seed: int = 0) -> dict:
    seeds = jax.random.split(jax.random.key(seed), 13)
    return {
        "tokens": normal_values(seeds[0], (ITEMS, TG, H, W, D), 1.0, 6.0, ((0, 8), (2, 4))),
        "video_flag": draw_video_flag(jax.random.fold_in(seeds[12], 71), 0),
        "frame_count": draw_frame_count(jax.random.fold_in(seeds[12], 71), 0),
        "norm_gain": jnp.clip(1.0 + 0.1 * jax.random.normal(seeds[3], (4, D), jnp.float32), 0.5, 1.5),
        "norm_bias": normal_values(seeds[4], (4, D), 0.3, 3.0, (), jnp.float32),
        "w_qkv": normal_values(seeds[5], (2, D, 3 * D), D ** -0.5, 0.25),
        "w_proj": normal_values(seeds[6], (2, D, D), (D // 4) ** -0.5, 0.5),
        "w_up": normal_values(seeds[7], (2, D, FF), D ** -0.5, 0.25),
        "w_down": normal_values(seeds[8], (2, FF, D), FF ** -0.5, 0.125),
        "out_bias": normal_values(seeds[9], (4, D), 0.3, 3.0, (), jnp.float32),
        "up_bias": normal_values(seeds[10], (2, FF), 0.5, 3.0, (), jnp.float32),
        "cotangent": normal_values(seeds[11], (ITEMS, TG, H, W, D), 1.0, 6.0, ((0, 8), (2, 4))),
    }


EPS = 1e-05
NEG = -1e+30
HIGH = lax.Precision.HIGHEST

@jax.custom_vjp
def low(v):
    return lax.optimization_barrier(v.astype(jnp.bfloat16)).astype(jnp.float32)

@jax.custom_vjp
def low_back(v):
    return v

def low_keep(v):
    return (low(v), None)

def low_pass(kept, grad):
    return (grad,)

def back_keep(v):
    return (v, None)

def back_low(kept, grad):
    return (low(grad),)
low.defvjp(low_keep, low_pass)
low_back.defvjp(back_keep, back_low)

def norm_apply(hidden, gain, bias):
    center = hidden - lax.optimization_barrier(jnp.mean(hidden, axis=-1, keepdims=True))
    spread = lax.optimization_barrier(jnp.mean(center * center, axis=-1, keepdims=True))
    return center * lax.rsqrt(spread + EPS) * gain + bias

def region_label(index, extent):
    return jnp.where(index < extent - WIN, 0, jnp.where(index < extent - SHIFT, 1, 2))

def allowed_mask():
    row_label = region_label(jnp.arange(H), H).reshape(H // WIN, 1, WIN, 1)
    col_label = region_label(jnp.arange(W), W).reshape(1, W // WIN, 1, WIN)
    label = (row_label * 3 + col_label).reshape(H // WIN, W // WIN, WIN * WIN)
    return label[:, :, :, None] == label[:, :, None, :]

def soft_weights(scores, allowed):
    scores = jnp.where(allowed, low_back(scores), NEG)
    row_max = lax.optimization_barrier(jnp.max(scores, axis=-1, keepdims=True))
    exponent = jnp.exp(scores - row_max)
    return low(exponent / lax.optimization_barrier(jnp.sum(exponent, axis=-1, keepdims=True)))

def spatial_block(hidden, params, allowed):
    norm_gain, norm_bias, w_qkv, w_proj, w_up, w_down, out_bias, up_bias = params
    score_scale = HEAD_DIM ** (-0.5)
    normed = low(norm_apply(hidden, norm_gain[0], norm_bias[0]))
    rolled = jnp.roll(normed, (-SHIFT, -SHIFT), axis=(1, 2))
    tile_rows = rolled.reshape(TG, H // WIN, WIN, W // WIN, WIN, D).transpose(0, 1, 3, 2, 4, 5)
    tile_rows = tile_rows.reshape(TG, H // WIN, W // WIN, WIN * WIN, D)
    packed = low_back(low(jnp.dot(tile_rows, w_qkv[0], precision=HIGH)))
    packed = packed.reshape(TG, H // WIN, W // WIN, WIN * WIN, 3, HEADS, HEAD_DIM)
    queries, key_rows, values = (packed[..., 0, :, :], packed[..., 1, :, :], packed[..., 2, :, :])
    scores = jnp.einsum('tabqhe,tabkhe->tabhqk', queries, key_rows, precision=HIGH) * score_scale
    weights = soft_weights(scores, allowed[:, :, None])
    mixed_heads = jnp.einsum('tabhqk,tabkhe->tabqhe', weights, values, precision=HIGH)
    mixed_heads = low_back(low(mixed_heads.reshape(TG, H // WIN, W // WIN, WIN, WIN, D)))
    layout = mixed_heads.transpose(0, 1, 3, 2, 4, 5).reshape(TG, H, W, D)
    layout = jnp.roll(layout, (SHIFT, SHIFT), axis=(1, 2))
    branch = low_back(jnp.dot(layout, w_proj[0], precision=HIGH) + out_bias[0])
    return hidden + branch

def temporal_block(hidden, params, is_video):
    norm_gain, norm_bias, w_qkv, w_proj, w_up, w_down, out_bias, up_bias = params
    score_scale = HEAD_DIM ** (-0.5)
    normed = low(norm_apply(hidden, norm_gain[2], norm_bias[2]))
    packed = low_back(low(jnp.dot(normed, w_qkv[1], precision=HIGH)))
    packed = packed.reshape(TG, H * W, 3, HEADS, HEAD_DIM)
    queries, key_rows, values = (packed[:, :, 0], packed[:, :, 1], packed[:, :, 2])
    scores = jnp.einsum('tphe,uphe->phtu', queries, key_rows, precision=HIGH) * score_scale
    causal = jnp.arange(TG)[:, None] >= jnp.arange(TG)[None, :]
    weights = soft_weights(scores, causal)
    mixed_heads = jnp.einsum('phtu,uphe->tphe', weights, values, precision=HIGH)
    mixed_heads = low_back(low(mixed_heads.reshape(TG, H, W, D)))
    branch = low_back(jnp.dot(mixed_heads, w_proj[1], precision=HIGH) + out_bias[2])
    return hidden + is_video * branch

def feed_forward(hidden, params, block, norm_index, bias_index):
    norm_gain, norm_bias, w_qkv, w_proj, w_up, w_down, out_bias, up_bias = params
    normed = low(norm_apply(hidden, norm_gain[norm_index], norm_bias[norm_index]))
    pre_act = low_back(jnp.dot(normed, w_up[block], precision=HIGH) + up_bias[block])
    active = low(jax.nn.gelu(pre_act, approximate=False))
    branch = low_back(jnp.dot(active, w_down[block], precision=HIGH) + out_bias[bias_index])
    return hidden + branch

def item_forward(params, allowed, packed_item):
    hidden, is_video, frames = packed_item
    hidden = spatial_block(hidden, params, allowed)
    hidden = feed_forward(hidden, params, 0, 1, 1)
    hidden = temporal_block(hidden, params, is_video.astype(jnp.float32))
    hidden = feed_forward(hidden, params, 1, 3, 3)
    is_valid = (jnp.arange(TG) < frames).astype(jnp.float32)
    return hidden * is_valid[:, None, None, None]

def reference(tokens, video_flag, frame_count, norm_gain, norm_bias, w_qkv, w_proj, w_up, w_down, out_bias, up_bias, cotangent):
    allowed = allowed_mask()
    params = (norm_gain.astype(jnp.float32), norm_bias.astype(jnp.float32), w_qkv.astype(jnp.float32), w_proj.astype(jnp.float32), w_up.astype(jnp.float32), w_down.astype(jnp.float32), out_bias.astype(jnp.float32), up_bias.astype(jnp.float32))
    inputs = tokens.astype(jnp.float32)
    stepper = jax.checkpoint(item_forward)

    def forward(inputs, params):
        return lax.map(lambda packed_item: stepper(params, allowed, packed_item), (inputs, video_flag, frame_count))
    result, pullback = jax.vjp(forward, inputs, params)
    grad_inputs, grads = pullback(cotangent.astype(jnp.float32))
    return (result.astype(jnp.bfloat16), grad_inputs.astype(jnp.bfloat16), grads[0], grads[1], grads[2], grads[3], grads[4], grads[5], grads[6], grads[7])
```

```python
import functools

import jax
import jax.numpy as jnp
from jax import lax
from jax.experimental import pallas as pl
from jax.experimental.pallas import tpu as pltpu
from jax.sharding import PartitionSpec as P

HEADS = 8
HEAD_DIM = 64
WIN = 8
SHIFT = 4
EPS = 1e-05
NEG = -1e30
SCALE = HEAD_DIM ** (-0.5)
BF16 = jnp.bfloat16
F32 = jnp.float32
NN = (((1,), (0,)), ((), ()))
NT = (((1,), (1,)), ((), ()))
CHUNK = 512
MIB = 1 << 20


def mm(left, right, dims=NN):
    return lax.dot_general(left, right, dims, preferred_element_type=F32)


def wide(column, lanes):
    return jnp.concatenate([column] * (lanes // column.shape[1]), axis=1)


def lane_sum(x):
    total = x[:, :128]
    for k in range(1, x.shape[1] // 128):
        total = total + x[:, 128 * k : 128 * (k + 1)]
    return total


def half_mask(shape):
    return lax.rem(lax.broadcasted_iota(jnp.int32, shape, len(shape) - 1), 128) < 64


def load_frame(own_ref, halo_ref):
    grid = jnp.concatenate([own_ref[0, 0], halo_ref[0, 0]], axis=0).astype(F32)
    rows, cols, feats = grid.shape
    blocks = grid.reshape(rows, cols // WIN, WIN, feats)
    after = jnp.concatenate([blocks[:, 1:], blocks[:, :1]], axis=1)
    first = lax.broadcasted_iota(jnp.int32, blocks.shape, 2) < SHIFT
    tiles = jnp.where(first, after, blocks).transpose(1, 0, 2, 3)
    return tiles.reshape(rows * cols, feats).astype(BF16).T.astype(F32)


def store_frame(value, own_ref, halo_ref):
    rows = own_ref.shape[2] + halo_ref.shape[2]
    cols, feats = own_ref.shape[3], own_ref.shape[4]
    flat = value.astype(BF16).T.astype(F32)
    tiles = flat.reshape(cols // WIN, rows, WIN, feats).transpose(1, 0, 2, 3)
    before = jnp.concatenate([tiles[:, -1:], tiles[:, :-1]], axis=1)
    first = lax.broadcasted_iota(jnp.int32, tiles.shape, 2) < SHIFT
    grid = jnp.where(first, before, tiles).reshape(rows, cols, feats).astype(BF16)
    own_ref[0, 0] = grid[: own_ref.shape[2]]
    halo_ref[0, 0] = grid[own_ref.shape[2] :]


def norm(x, gain, bias):
    center = x - jnp.mean(x, axis=0, keepdims=True)
    spread = jnp.mean(center * center, axis=0, keepdims=True)
    rstd = lax.rsqrt(spread + EPS)
    xhat = center * rstd
    return xhat, rstd, (xhat * gain + bias).astype(BF16)


def norm_back(d_norm, xhat, rstd, gain):
    grad_gain = d_norm * xhat
    e_mean = jnp.mean(d_norm * gain, axis=0, keepdims=True)
    x_mean = jnp.mean(grad_gain * gain, axis=0, keepdims=True)
    d_hidden = (d_norm * gain - e_mean - xhat * x_mean) * rstd
    return d_hidden, lane_sum(grad_gain), lane_sum(d_norm)


def gelu_parts(pre):
    upper = 0.5 + 0.5 * lax.erf(pre * (0.5**0.5))
    density = jnp.exp(pre * pre * -0.5) * 0.3989422804014327
    return (pre * upper).astype(BF16), upper + pre * density


def head_sum(x):
    return jnp.sum(x.reshape(HEADS, HEAD_DIM, x.shape[1]), axis=1)


def head_spread(p):
    return jnp.broadcast_to(p[:, None, :], (HEADS, HEAD_DIM, p.shape[1])).reshape(
        HEADS * HEAD_DIM, p.shape[1]
    )


def head_pair(x):
    zero = jnp.zeros_like(x[:HEAD_DIM])
    return jnp.concatenate(
        [
            jnp.concatenate([x[:HEAD_DIM], zero], axis=1),
            jnp.concatenate([zero, x[HEAD_DIM:]], axis=1),
        ],
        axis=0,
    )


def window_blocks(p, left):
    zero = jnp.zeros_like(p)
    return jnp.concatenate([jnp.where(left, p, zero), jnp.where(left, zero, p)], axis=0)


def pack(info, pieces, keep_ref, send_ref):
    me, row = info[0], info[1]
    core, cell = lax.rem(me, 2), lax.div(me, 2)

    def step(i, carry):
        j, z = lax.div(i, 4), lax.rem(i, 4)
        for ref, side in ((keep_ref, core), (send_ref, 1 - core)):
            base = 0
            for acc_ref, depth in pieces:
                first = (z ^ row) * (8 * depth) + (side * 4 + (j ^ cell)) * depth
                part = acc_ref[pl.ds(pl.multiple_of(first, 16), depth), :].astype(BF16)
                for k in range(part.shape[1] // 512):
                    ref[j, z, base : base + depth, :] = part[:, 512 * k : 512 * (k + 1)]
                    base += depth
        return carry

    lax.fori_loop(0, 16, step, 0)


def row_sums(acc):
    return lax.dot_general(
        jnp.ones((8, 128), F32), acc, NT, precision=lax.Precision.HIGHEST, preferred_element_type=F32
    )


GAIN, BIAS, OUTB, UPB = 0, 2048, 4096, 6144

C1, XHAT1, ACT0, SLOPE0, A2, XHAT2, O2, R1_ROWS = 0, 512, 1024, 3072, 5120, 5632, 6144, 6656
A0, XHAT0, O0, QKV0, P0, R2_ROWS = 0, 512, 1024, 1536, 3072, 3584


def forward_kernel(
    info,
    own_ref,
    halo_ref,
    cot_own_ref,
    cot_halo_ref,
    mask_ref,
    vec_ref,
    wqkv_t_ref,
    wproj_t_ref,
    wup_t_ref,
    wdown_t_ref,
    wup_ref,
    wdown_ref,
    out_own_ref,
    out_halo_ref,
    r1_ref,
    r2_ref,
    qkv2_ref,
    p2_ref,
    stat_ref,
    g3_ref,
    keep_ref,
    send_ref,
    sums_ref,
    acc_up,
    acc_down,
    acc_vec,
    kv_ref,
):
    item, frame = pl.program_id(0), pl.program_id(1)
    items, frames = pl.num_programs(0), pl.num_programs(1)
    lanes = r1_ref.shape[2]
    feats = wqkv_t_ref.shape[2]

    def vec(base, index=0, size=512):
        return wide(vec_ref[base + 512 * index : base + 512 * index + size, :], lanes)

    @pl.when((item == 0) & (frame == 0))
    def _():
        acc_up[...] = jnp.zeros_like(acc_up)
        acc_down[...] = jnp.zeros_like(acc_down)
        acc_vec[...] = jnp.zeros_like(acc_vec)
        kv_ref[...] = jnp.zeros_like(kv_ref)

    x0 = load_frame(own_ref, halo_ref)
    xhat0, rstd0, a0 = norm(x0, vec(GAIN, 0), vec(BIAS, 0))
    r2_ref[0, A0 : A0 + 512, :] = a0
    r2_ref[0, XHAT0 : XHAT0 + 512, :] = xhat0.astype(BF16)
    qkv = mm(wqkv_t_ref[0], a0).astype(BF16)
    r2_ref[0, QKV0 : QKV0 + 1536, :] = qkv
    keys = qkv[512:1024].T
    left = half_mask((64, 256))
    left_one = left[:, :128]
    for pair in range(lanes // 128):
        cols = slice(128 * pair, 128 * pair + 128)
        allowed = mask_ref[pair] > 0.5
        for hp in range(HEADS // 2):
            dims = slice(128 * hp, 128 * hp + 128)
            scores = mm(keys[cols, dims], head_pair(qkv[dims, cols]))
            scores = jnp.where(left, scores[:64], scores[64:]) * SCALE
            scores = jnp.where(allowed, scores, NEG)
            exponent = jnp.exp(scores - jnp.max(scores, axis=0, keepdims=True))
            weights = exponent * (1.0 / jnp.sum(exponent, axis=0, keepdims=True))
            weights = weights.astype(BF16)
            r2_ref[0, P0 + 256 * pair + 64 * hp : P0 + 256 * pair + 64 * hp + 64, :] = weights
            for j in range(2):
                blocks = window_blocks(weights[:, 128 * j : 128 * j + 128], left_one)
                first = 128 * hp + 64 * j
                values = qkv[1024 + first : 1024 + first + 64, cols]
                r2_ref[0, O0 + first : O0 + first + 64, cols] = mm(values, blocks).astype(BF16)
    x1 = x0 + mm(wproj_t_ref[0], r2_ref[0, O0 : O0 + 512, :]) + vec(OUTB, 0)

    xhat1, rstd1, c1 = norm(x1, vec(GAIN, 1), vec(BIAS, 1))
    r1_ref[0, C1 : C1 + 512, :] = c1
    r1_ref[0, XHAT1 : XHAT1 + 512, :] = xhat1.astype(BF16)
    x2 = x1 + vec(OUTB, 1)
    for k in range(wup_t_ref.shape[1] // CHUNK):
        part = slice(CHUNK * k, CHUNK * (k + 1))
        pre = mm(wup_t_ref[0, part, :], c1) + vec(UPB, k)
        act, slope = gelu_parts(pre)
        r1_ref[0, ACT0 + CHUNK * k : ACT0 + CHUNK * (k + 1), :] = act
        r1_ref[0, SLOPE0 + CHUNK * k : SLOPE0 + CHUNK * (k + 1), :] = slope.astype(BF16)
        x2 = x2 + mm(wdown_t_ref[0, :, part], act)

    xhat2, rstd2, a2 = norm(x2, vec(GAIN, 2), vec(BIAS, 2))
    r1_ref[0, A2 : A2 + 512, :] = a2
    r1_ref[0, XHAT2 : XHAT2 + 512, :] = xhat2.astype(BF16)
    qkv = mm(wqkv_t_ref[1], a2).astype(BF16)
    qkv2_ref[0] = qkv
    kv_ref[frame] = qkv[512:]
    query = qkv[:512].astype(F32) * SCALE
    scores = []
    for u in range(kv_ref.shape[0]):
        score = head_sum(query * kv_ref[u, :512, :].astype(F32))
        scores.append(jnp.where(u <= frame, score, NEG))
    top = functools.reduce(jnp.maximum, scores)
    exponents = [jnp.exp(s - top) for s in scores]
    scale = 1.0 / sum(exponents)
    mixed = jnp.zeros((feats, lanes), F32)
    for u in range(kv_ref.shape[0]):
        weight = exponents[u] * scale
        p2_ref[0, u] = weight
        weight = weight.astype(BF16).astype(F32)
        mixed = mixed + head_spread(weight) * kv_ref[u, 512:, :].astype(F32)
    o2 = mixed.astype(BF16)
    r1_ref[0, O2 : O2 + 512, :] = o2
    is_video = info[2 + item].astype(F32)
    x3 = x2 + is_video * (mm(wproj_t_ref[1], o2) + vec(OUTB, 2))

    is_valid = jnp.where(frame < info[2 + items + item], 1.0, 0.0)
    g4 = load_frame(cot_own_ref, cot_halo_ref) * is_valid
    grad_low = g4.astype(BF16)
    xhat3, rstd3, c3 = norm(x3, vec(GAIN, 3), vec(BIAS, 3))
    x4 = x3 + vec(OUTB, 3)
    d_norm = jnp.zeros((feats, lanes), F32)
    for k in range(wup_t_ref.shape[1] // CHUNK):
        part = slice(CHUNK * k, CHUNK * (k + 1))
        pre = mm(wup_t_ref[1, part, :], c3) + vec(UPB, 4 + k)
        act, slope = gelu_parts(pre)
        x4 = x4 + mm(wdown_t_ref[1, :, part], act)
        d_pre = (mm(wdown_ref[0, part, :], grad_low) * slope).astype(BF16)
        d_norm = d_norm + mm(wup_ref[0, :, part], d_pre)
        acc_up[:, part] += mm(c3, d_pre, NT)
        acc_down[part, :] += mm(act, grad_low, NT)
        acc_vec[1536 + CHUNK * k : 1536 + CHUNK * (k + 1), :] += lane_sum(d_pre.astype(F32))
    store_frame(x4 * is_valid, out_own_ref, out_halo_ref)
    d_hidden, gain_part, bias_part = norm_back(d_norm, xhat3, rstd3, vec(GAIN, 3))
    acc_vec[0:512, :] += gain_part
    acc_vec[512:1024, :] += bias_part
    acc_vec[1024:1536, :] += lane_sum(g4)
    g3_ref[0] = g4 + d_hidden
    stat_ref[0] = jnp.concatenate([rstd0, rstd1, rstd2, jnp.zeros((5, lanes), F32)], axis=0)

    @pl.when((item == items - 1) & (frame == frames - 1))
    def _():
        pack(info, [(acc_up, 16), (acc_down, 64)], keep_ref, send_ref)
        sums_ref[...] = row_sums(acc_vec[...])


def middle_kernel(
    info,
    g3_ref,
    r1_ref,
    qkv2_ref,
    p2_ref,
    stat_ref,
    vec_ref,
    wqkv_ref,
    wproj_ref,
    wup_ref,
    wdown_ref,
    g1_ref,
    keep_ref,
    send_ref,
    sums_ref,
    acc_up,
    acc_down,
    acc_qkv,
    acc_proj,
    acc_vec,
    dkv_ref,
):
    item, step = pl.program_id(0), pl.program_id(1)
    items, frames = pl.num_programs(0), pl.num_programs(1)
    frame = frames - 1 - step
    lanes = r1_ref.shape[2]
    feats = wqkv_ref.shape[1]

    def vec(base, index=0, size=512):
        return wide(vec_ref[base + 512 * index : base + 512 * index + size, :], lanes)

    @pl.when((item == 0) & (step == 0))
    def _():
        for acc in (acc_up, acc_down, acc_qkv, acc_proj, acc_vec):
            acc[...] = jnp.zeros_like(acc)

    @pl.when(step == 0)
    def _():
        dkv_ref[...] = jnp.zeros_like(dkv_ref)

    g3 = g3_ref[0]
    is_video = info[2 + item].astype(F32)
    d_attn = (g3 * is_video).astype(BF16)
    acc_proj[...] += mm(r1_ref[0, O2 : O2 + 512, :], d_attn, NT)
    acc_vec[0:512, :] += lane_sum(d_attn.astype(F32))
    d_mixed = mm(wproj_ref[0], d_attn).astype(BF16).astype(F32)
    query = qkv2_ref[frame, :512, :].astype(F32) * SCALE
    count = qkv2_ref.shape[0]
    weights = [p2_ref[0, u] for u in range(count)]
    d_weights = []
    for u in range(count):
        d_weights.append(head_sum(d_mixed * qkv2_ref[u, 1024:, :].astype(F32)))
    inner = sum(w * d for w, d in zip(weights, d_weights))
    d_query = jnp.zeros((feats, lanes), F32)
    for u in range(count):
        d_score = (weights[u] * (d_weights[u] - inner)).astype(BF16).astype(F32)
        spread = head_spread(d_score)
        d_query = d_query + spread * qkv2_ref[u, 512:1024, :].astype(F32)
        dkv_ref[u, :512, :] += spread * query
        dkv_ref[u, 512:, :] += head_spread(weights[u].astype(BF16).astype(F32)) * d_mixed
    d_qkv = jnp.concatenate(
        [(d_query * SCALE).astype(BF16), dkv_ref[frame].astype(BF16)], axis=0
    )
    acc_qkv[...] += mm(r1_ref[0, A2 : A2 + 512, :], d_qkv, NT)
    d_norm = mm(wqkv_ref[0], d_qkv)
    xhat = r1_ref[0, XHAT2 : XHAT2 + 512, :].astype(F32)
    d_hidden, gain_part, bias_part = norm_back(d_norm, xhat, stat_ref[0, 2:3, :], vec(GAIN, 2))
    acc_vec[512:1024, :] += gain_part
    acc_vec[1024:1536, :] += bias_part
    g2 = g3 + d_hidden

    grad_low = g2.astype(BF16)
    acc_vec[1536:2048, :] += lane_sum(grad_low.astype(F32))
    c1 = r1_ref[0, C1 : C1 + 512, :]
    d_norm = jnp.zeros((feats, lanes), F32)
    for k in range(wup_ref.shape[2] // CHUNK):
        part = slice(CHUNK * k, CHUNK * (k + 1))
        slope = r1_ref[0, SLOPE0 + CHUNK * k : SLOPE0 + CHUNK * (k + 1), :].astype(F32)
        d_pre = (mm(wdown_ref[0, part, :], grad_low) * slope).astype(BF16)
        d_norm = d_norm + mm(wup_ref[0, :, part], d_pre)
        acc_up[:, part] += mm(c1, d_pre, NT)
        acc_down[part, :] += mm(
            r1_ref[0, ACT0 + CHUNK * k : ACT0 + CHUNK * (k + 1), :], grad_low, NT
        )
        acc_vec[3072 + CHUNK * k : 3072 + CHUNK * (k + 1), :] += lane_sum(d_pre.astype(F32))
    xhat = r1_ref[0, XHAT1 : XHAT1 + 512, :].astype(F32)
    d_hidden, gain_part, bias_part = norm_back(d_norm, xhat, stat_ref[0, 1:2, :], vec(GAIN, 1))
    acc_vec[2048:2560, :] += gain_part
    acc_vec[2560:3072, :] += bias_part
    g1_ref[0] = g2 + d_hidden

    @pl.when((item == items - 1) & (step == frames - 1))
    def _():
        pieces = [(acc_up, 16), (acc_down, 64), (acc_qkv, 16), (acc_proj, 16)]
        pack(info, pieces, keep_ref, send_ref)
        sums_ref[...] = row_sums(acc_vec[...])


def space_kernel(
    info,
    g1_ref,
    r2_ref,
    stat_ref,
    vec_ref,
    wqkv_ref,
    wproj_ref,
    out_own_ref,
    out_halo_ref,
    keep_ref,
    send_ref,
    sums_ref,
    acc_qkv,
    acc_proj,
    acc_vec,
    dqkv_ref,
):
    item, frame = pl.program_id(0), pl.program_id(1)
    items, frames = pl.num_programs(0), pl.num_programs(1)
    lanes = r2_ref.shape[2]

    @pl.when((item == 0) & (frame == 0))
    def _():
        for acc in (acc_qkv, acc_proj, acc_vec):
            acc[...] = jnp.zeros_like(acc)

    g1 = g1_ref[0]
    d_attn = g1.astype(BF16)
    acc_proj[...] += mm(r2_ref[0, O0 : O0 + 512, :], d_attn, NT)
    acc_vec[0:512, :] += lane_sum(d_attn.astype(F32))
    d_mixed = mm(wproj_ref[0], d_attn).astype(BF16)
    values = r2_ref[0, QKV0 + 1024 : QKV0 + 1536, :].T
    left = half_mask((64, 256))
    left_one = left[:, :128]
    for pair in range(lanes // 128):
        cols = slice(128 * pair, 128 * pair + 128)
        for hp in range(HEADS // 2):
            dims = slice(128 * hp, 128 * hp + 128)
            d_weights = mm(values[cols, dims], head_pair(d_mixed[dims, cols]))
            d_weights = jnp.where(left, d_weights[:64], d_weights[64:])
            low = r2_ref[0, P0 + 256 * pair + 64 * hp : P0 + 256 * pair + 64 * hp + 64, :]
            weights = low.astype(F32)
            inner = jnp.sum(weights * d_weights, axis=0, keepdims=True)
            d_scores = (weights * (d_weights - inner)).astype(BF16)
            for j in range(2):
                one = slice(128 * j, 128 * j + 128)
                first = 128 * hp + 64 * j
                soft = window_blocks(low[:, one], left_one)
                slope = window_blocks(d_scores[:, one], left_one)
                query = r2_ref[0, QKV0 + first : QKV0 + first + 64, cols]
                key = r2_ref[0, QKV0 + 512 + first : QKV0 + 512 + first + 64, cols]
                dqkv_ref[first : first + 64, cols] = (mm(key, slope) * SCALE).astype(BF16)
                dqkv_ref[512 + first : 512 + first + 64, cols] = (
                    mm(query, slope, NT) * SCALE
                ).astype(BF16)
                dqkv_ref[1024 + first : 1024 + first + 64, cols] = mm(
                    d_mixed[first : first + 64, cols], soft, NT
                ).astype(BF16)
    d_qkv = dqkv_ref[...]
    acc_qkv[...] += mm(r2_ref[0, A0 : A0 + 512, :], d_qkv, NT)
    d_norm = mm(wqkv_ref[0], d_qkv)
    xhat = r2_ref[0, XHAT0 : XHAT0 + 512, :].astype(F32)
    gain = wide(vec_ref[GAIN : GAIN + 512, :], lanes)
    d_hidden, gain_part, bias_part = norm_back(d_norm, xhat, stat_ref[0, 0:1, :], gain)
    acc_vec[512:1024, :] += gain_part
    acc_vec[1024:1536, :] += bias_part
    store_frame(g1 + d_hidden, out_own_ref, out_halo_ref)

    @pl.when((item == items - 1) & (frame == frames - 1))
    def _():
        pack(info, [(acc_qkv, 16), (acc_proj, 16)], keep_ref, send_ref)
        sums_ref[...] = row_sums(acc_vec[...])


def unpack_kernel(info, ff1_ref, mid_ref, space_ref, qkv_ref, proj_ref, up_ref, down_ref):
    def put(out_ref, slot, source_ref, base, depth, width):
        for k in range(width // 512):
            rows = source_ref[0, base + depth * k : base + depth * (k + 1), :]
            out_ref[slot, :, 512 * k : 512 * (k + 1)] = rows.astype(F32)

    put(up_ref, 1, ff1_ref, 0, 16, 2048)
    put(down_ref, 1, ff1_ref, 64, 64, 512)
    put(up_ref, 0, mid_ref, 0, 16, 2048)
    put(down_ref, 0, mid_ref, 64, 64, 512)
    put(qkv_ref, 1, mid_ref, 128, 16, 1536)
    put(proj_ref, 1, mid_ref, 176, 16, 512)
    put(qkv_ref, 0, space_ref, 0, 16, 1536)
    put(proj_ref, 0, space_ref, 48, 16, 512)


def whole_spec(shape, single=True):
    mode = pl.Buffered(1) if single else None
    return pl.BlockSpec(shape, lambda *_: (0,) * len(shape), pipeline_mode=mode)


def part_spec(shape, index):
    def place(i, t, info):
        return (index,) + (0,) * (len(shape) - 1)

    return pl.BlockSpec((1,) + tuple(shape[1:]), place, pipeline_mode=pl.Buffered(1))


def params(limit=60 * MIB):
    return pltpu.CompilerParams(
        dimension_semantics=("arbitrary",) * 2, vmem_limit_bytes=limit
    )


def sds(shape, dtype):
    return jax.ShapeDtypeStruct(shape, dtype)


def run_forward(info, tokens, halo, cotangent, cot_halo, mask, vecs, weights):
    wqkv_t, wproj_t, wup_t, wdown_t, wup, wdown = weights
    items, frames, grid_rows, cols, feats = tokens.shape
    lanes = grid_rows * cols
    planes = items * frames
    half = (1, 1, SHIFT, cols, feats)
    own_spec = pl.BlockSpec(half, lambda i, t, info: (i, t, 1, 0, 0))
    halo_spec = pl.BlockSpec(half, lambda i, t, info: (i, t, 0, 0, 0))

    def plane_spec(*shape):
        return pl.BlockSpec(
            (1,) + shape, lambda i, t, info: (i * frames + t,) + (0,) * len(shape)
        )

    hidden = wup.shape[2]
    return pl.pallas_call(
        forward_kernel,
        grid_spec=pltpu.PrefetchScalarGridSpec(
            num_scalar_prefetch=1,
            grid=(items, frames),
            in_specs=[
                own_spec,
                halo_spec,
                own_spec,
                halo_spec,
                whole_spec(mask.shape),
                whole_spec(vecs.shape),
                whole_spec(wqkv_t.shape),
                whole_spec(wproj_t.shape),
                whole_spec(wup_t.shape),
                whole_spec(wdown_t.shape),
                part_spec(wup.shape, 1),
                part_spec(wdown.shape, 1),
            ],
            out_specs=[
                own_spec,
                halo_spec,
                plane_spec(R1_ROWS, lanes),
                plane_spec(R2_ROWS, lanes),
                plane_spec(3 * feats, lanes),
                plane_spec(frames, HEADS, lanes),
                plane_spec(8, lanes),
                plane_spec(feats, lanes),
                whole_spec((4, 4, 128, 512)),
                whole_spec((4, 4, 128, 512)),
                whole_spec((8, 3584)),
            ],
            scratch_shapes=[
                pltpu.VMEM((feats, hidden), F32),
                pltpu.VMEM((hidden, feats), F32),
                pltpu.VMEM((3584, 128), F32),
                pltpu.VMEM((frames, 2 * feats, lanes), BF16),
            ],
        ),
        out_shape=[
            sds(tokens.shape, BF16),
            sds(halo.shape, BF16),
            sds((planes, R1_ROWS, lanes), BF16),
            sds((planes, R2_ROWS, lanes), BF16),
            sds((planes, 3 * feats, lanes), BF16),
            sds((planes, frames, HEADS, lanes), F32),
            sds((planes, 8, lanes), F32),
            sds((planes, feats, lanes), F32),
            sds((4, 4, 128, 512), BF16),
            sds((4, 4, 128, 512), BF16),
            sds((8, 3584), F32),
        ],
        compiler_params=params(),
        cost_estimate=pl.CostEstimate(
            flops=55_000_000_000, bytes_accessed=100_000_000, transcendentals=20_000_000
        ),
        name="forward",
    )(info, tokens, halo, cotangent, cot_halo, mask, vecs, wqkv_t, wproj_t, wup_t, wdown_t, wup, wdown)


def run_middle(info, g3, r1, qkv2, p2, stats, vecs, weights, items):
    wqkv, wproj, wup, wdown = weights
    planes, feats, lanes = g3.shape
    frames = planes // items
    hidden = wup.shape[2]

    def plane_spec(*shape):
        return pl.BlockSpec(
            (1,) + shape,
            lambda i, s, info: (i * frames + frames - 1 - s,) + (0,) * len(shape),
        )

    return pl.pallas_call(
        middle_kernel,
        grid_spec=pltpu.PrefetchScalarGridSpec(
            num_scalar_prefetch=1,
            grid=(items, frames),
            in_specs=[
                plane_spec(feats, lanes),
                plane_spec(R1_ROWS, lanes),
                pl.BlockSpec((frames, 3 * feats, lanes), lambda i, s, info: (i, 0, 0)),
                plane_spec(frames, HEADS, lanes),
                plane_spec(8, lanes),
                whole_spec(vecs.shape),
                part_spec(wqkv.shape, 1),
                part_spec(wproj.shape, 1),
                part_spec(wup.shape, 0),
                part_spec(wdown.shape, 0),
            ],
            out_specs=[
                plane_spec(feats, lanes),
                whole_spec((4, 4, 192, 512)),
                whole_spec((4, 4, 192, 512)),
                whole_spec((8, 5120)),
            ],
            scratch_shapes=[
                pltpu.VMEM((feats, hidden), F32),
                pltpu.VMEM((hidden, feats), F32),
                pltpu.VMEM((feats, 3 * feats), F32),
                pltpu.VMEM((feats, feats), F32),
                pltpu.VMEM((5120, 128), F32),
                pltpu.VMEM((frames, 2 * feats, lanes), F32),
            ],
        ),
        out_shape=[
            sds((planes, feats, lanes), F32),
            sds((4, 4, 192, 512), BF16),
            sds((4, 4, 192, 512), BF16),
            sds((8, 5120), F32),
        ],
        compiler_params=params(),
        cost_estimate=pl.CostEstimate(
            flops=33_000_000_000, bytes_accessed=70_000_000, transcendentals=1_000_000
        ),
        name="middle",
    )(info, g3, r1, qkv2, p2, stats, vecs, wqkv, wproj, wup, wdown)


def run_space(info, g1, r2, stats, vecs, weights, shape):
    wqkv, wproj = weights
    items, frames, grid_rows, cols, feats = shape
    planes, _, lanes = g1.shape
    half = (1, 1, SHIFT, cols, feats)

    def plane_spec(*tail):
        return pl.BlockSpec(
            (1,) + tail, lambda i, t, info: (i * frames + t,) + (0,) * len(tail)
        )

    return pl.pallas_call(
        space_kernel,
        grid_spec=pltpu.PrefetchScalarGridSpec(
            num_scalar_prefetch=1,
            grid=(items, frames),
            in_specs=[
                plane_spec(feats, lanes),
                plane_spec(R2_ROWS, lanes),
                plane_spec(8, lanes),
                whole_spec((512, 128)),
                part_spec(wqkv.shape, 0),
                part_spec(wproj.shape, 0),
            ],
            out_specs=[
                pl.BlockSpec(half, lambda i, t, info: (i, t, 1, 0, 0)),
                pl.BlockSpec(half, lambda i, t, info: (i, t, 0, 0, 0)),
                whole_spec((4, 4, 64, 512)),
                whole_spec((4, 4, 64, 512)),
                whole_spec((8, 1536)),
            ],
            scratch_shapes=[
                pltpu.VMEM((feats, 3 * feats), F32),
                pltpu.VMEM((feats, feats), F32),
                pltpu.VMEM((1536, 128), F32),
                pltpu.VMEM((3 * feats, lanes), BF16),
            ],
        ),
        out_shape=[
            sds(shape, BF16),
            sds((items, frames, SHIFT, cols, feats), BF16),
            sds((4, 4, 64, 512), BF16),
            sds((4, 4, 64, 512), BF16),
            sds((8, 1536), F32),
        ],
        compiler_params=params(),
        cost_estimate=pl.CostEstimate(
            flops=14_000_000_000, bytes_accessed=40_000_000, transcendentals=1_000_000
        ),
        name="space",
    )(info, g1, r2, stats, vecs, wqkv, wproj)


def run_unpack(info, ff1, mid, space):
    def piece(array):
        return pl.BlockSpec((1,) + array.shape[1:], lambda q, info: (q ^ info[0], 0, 0))

    def out(depth, width):
        return pl.BlockSpec((2, depth, width), lambda q, info: (0, q, 0))

    return pl.pallas_call(
        unpack_kernel,
        grid_spec=pltpu.PrefetchScalarGridSpec(
            num_scalar_prefetch=1,
            grid=(8,),
            in_specs=[piece(ff1), piece(mid), piece(space)],
            out_specs=[out(16, 1536), out(16, 512), out(16, 2048), out(64, 512)],
        ),
        out_shape=[
            sds((2, 128, 1536), F32),
            sds((2, 128, 512), F32),
            sds((2, 128, 2048), F32),
            sds((2, 512, 512), F32),
        ],
        name="unpack",
    )(info, ff1, mid, space)


def shift(block, axis, distance):
    size = lax.axis_size(axis)
    return lax.ppermute(block, axis, [(i, (i + distance) % size) for i in range(size)])


def swap(block, axis, bits):
    return lax.ppermute(block, axis, [(i, i ^ bits) for i in range(lax.axis_size(axis))])


def add(*terms):
    return functools.reduce(jnp.add, [t.astype(F32) for t in terms])


def upper_bits(total):
    bit = 8
    while bit < lax.axis_size("dp"):
        total = add(total, swap(total, "dp", bit))
        bit *= 2
    return total


def reduce_pieces(keep, send):
    taken = swap(send, "dp", 1)
    parts = [add(keep[j], taken[j]).astype(BF16) for j in range(4)]
    across = [swap(parts[j], "dp", 2 * j) for j in range(1, 4)]
    rows = add(parts[0], *across).astype(BF16)
    along = [swap(rows[z], "rows", z) for z in range(1, 4)]
    return upper_bits(add(rows[0], *along)).astype(BF16)


def gather_pieces(mine):
    chip = jnp.stack([mine] + [swap(mine, "dp", 2 * j) for j in range(1, 4)])
    return jnp.concatenate([chip, swap(chip, "dp", 1)])


def reduce_vector(vector):
    total = add(vector, swap(vector, "dp", 1))
    total = add(total, *[swap(total, "dp", 2 * j) for j in range(1, 4)])
    total = upper_bits(total)
    return add(total, *[swap(total, "rows", z) for z in range(1, 4)])


def region_label(index, extent):
    return jnp.where(index < extent - WIN, 0, jnp.where(index < extent - SHIFT, 1, 2))


def tile_mask(cols):
    height = lax.axis_size("rows") * WIN
    row_label = region_label(lax.axis_index("rows") * WIN + jnp.arange(WIN), height)
    place = (jnp.arange(WIN) + SHIFT) % WIN
    col_label = region_label(jnp.arange(0, cols, WIN)[:, None] + place, cols)
    label = (row_label[None, :, None] * 3 + col_label[:, None, :]).reshape(-1, WIN * WIN)
    same = (label[:, :, None] == label[:, None, :]).astype(F32)
    pairs = same.reshape(-1, 2, WIN * WIN, WIN * WIN).transpose(0, 2, 1, 3)
    pairs = pairs.reshape(-1, WIN * WIN, 2 * WIN * WIN)
    return jnp.concatenate([pairs, pairs], axis=2)


def on_device(
    tokens,
    video_flag,
    frame_count,
    norm_gain,
    norm_bias,
    w_qkv,
    w_proj,
    w_up,
    w_down,
    out_bias,
    up_bias,
    cotangent,
):
    items, frames, grid_rows, cols, feats = tokens.shape
    place = lax.rem(lax.axis_index("dp"), 8)
    row = lax.axis_index("rows")
    info = jnp.concatenate([jnp.stack([place, row]), video_flag, frame_count]).astype(jnp.int32)
    unpack_info = jnp.stack([lax.rem(place, 2) * 4 + lax.div(place, 2)]).astype(jnp.int32)

    halo = shift(tokens[:, :, :SHIFT], "rows", -1)
    cot_halo = shift(cotangent[:, :, :SHIFT], "rows", -1)
    mask = tile_mask(cols)
    vecs = jnp.concatenate([v.reshape(-1) for v in (norm_gain, norm_bias, out_bias, up_bias)])
    vecs = jnp.broadcast_to(vecs[:, None], (vecs.shape[0], 128))
    flipped = [jnp.swapaxes(w, 1, 2) for w in (w_qkv, w_proj, w_up, w_down)]

    (out_own, out_halo, r1, r2, qkv2, p2, stats, g3, keep1, send1, sums1) = run_forward(
        info, tokens, halo, cotangent, cot_halo, mask, vecs, flipped + [w_up, w_down]
    )
    layer_out = lax.dynamic_update_slice(out_own, shift(out_halo, "rows", 1), (0,) * 5)
    g1, keep0, send0, sums0 = run_middle(
        info, g3, r1, qkv2, p2, stats, vecs, (w_qkv, w_proj, w_up, w_down), items
    )
    grad_own, grad_halo, keeps, sends, sumss = run_space(
        info, g1, r2, stats, vecs, (w_qkv, w_proj), tokens.shape
    )
    grad_tokens = lax.dynamic_update_slice(grad_own, shift(grad_halo, "rows", 1), (0,) * 5)

    ff1 = gather_pieces(reduce_pieces(keep1, send1))
    mid = gather_pieces(reduce_pieces(keep0, send0))
    space = gather_pieces(reduce_pieces(keeps, sends))
    grad_qkv, grad_proj, grad_up, grad_down = run_unpack(unpack_info, ff1, mid, space)

    a, b, c = sums1[0], sums0[0], sumss[0]
    gains = jnp.stack([c[512:1024], b[2048:2560], b[512:1024], a[0:512]])
    biases = jnp.stack([c[1024:1536], b[2560:3072], b[1024:1536], a[512:1024]])
    outer = jnp.stack([c[0:512], b[1536:2048], b[0:512], a[1024:1536]])
    upper = jnp.stack([b[3072:5120], a[1536:3584]])
    vector = jnp.concatenate([gains, biases, outer, upper.reshape(8, 512)])
    total = reduce_vector(vector)

    def share(values, width):
        return lax.dynamic_slice_in_dim(values, row * width, width, axis=1)

    narrow = share(total[:12], feats // lax.axis_size("rows"))
    up_sum = share(total[12:].reshape(2, -1), up_bias.shape[1] // lax.axis_size("rows"))
    return (
        layer_out,
        grad_tokens,
        narrow[0:4],
        narrow[4:8],
        grad_qkv,
        grad_proj,
        grad_up,
        grad_down,
        narrow[8:12],
        up_sum,
    )


def solution(mesh):
    split = P("dp", None, "rows", None, None)
    in_specs = (split, P("dp"), P("dp")) + (P(),) * 8 + (split,)
    out_specs = (
        split,
        split,
        P(None, "rows"),
        P(None, "rows"),
        P(None, "rows", None),
        P(None, "rows", None),
        P(None, "rows", None),
        P(None, "rows", None),
        P(None, "rows"),
        P(None, "rows"),
    )
    return jax.shard_map(
        on_device, mesh=mesh, in_specs=in_specs, out_specs=out_specs, check_vma=False
    )
```

```python
import functools

import jax
import jax.numpy as jnp
from jax import lax
from jax.experimental import pallas as pl
from jax.experimental.pallas import tpu as pltpu
from jax.sharding import PartitionSpec as P

HEADS = 8
HEAD_DIM = 64
WIN = 8
SHIFT = 4
EPS = 1e-05
NEG = -1e30
SCALE = HEAD_DIM ** (-0.5)
BF16 = jnp.bfloat16
F32 = jnp.float32
NN = (((1,), (0,)), ((), ()))
NT = (((1,), (1,)), ((), ()))
CHUNK = 512
MIB = 1 << 20


def mm(left, right, dims=NN):
    return lax.dot_general(left, right, dims, preferred_element_type=F32)


def wide(column, lanes):
    return jnp.concatenate([column] * (lanes // column.shape[1]), axis=1)


def lane_sum(x):
    total = x[:, :128]
    for k in range(1, x.shape[1] // 128):
        total = total + x[:, 128 * k : 128 * (k + 1)]
    return total


def half_mask(shape):
    return lax.rem(lax.broadcasted_iota(jnp.int32, shape, len(shape) - 1), 128) < 64


def load_frame(own, halo):
    grid = jnp.concatenate([own, halo], axis=0).astype(F32)
    rows, cols, feats = grid.shape
    blocks = grid.reshape(rows, cols // WIN, WIN, feats)
    after = jnp.concatenate([blocks[:, 1:], blocks[:, :1]], axis=1)
    first = lax.broadcasted_iota(jnp.int32, blocks.shape, 2) < SHIFT
    tiles = jnp.where(first, after, blocks).transpose(1, 0, 2, 3)
    return tiles.reshape(rows * cols, feats).astype(BF16).T.astype(F32)


def store_frame(value, own_ref, halo_ref):
    rows = own_ref.shape[2] + halo_ref.shape[2]
    cols, feats = own_ref.shape[3], own_ref.shape[4]
    flat = value.astype(BF16).T.astype(F32)
    tiles = flat.reshape(cols // WIN, rows, WIN, feats).transpose(1, 0, 2, 3)
    before = jnp.concatenate([tiles[:, -1:], tiles[:, :-1]], axis=1)
    first = lax.broadcasted_iota(jnp.int32, tiles.shape, 2) < SHIFT
    grid = jnp.where(first, before, tiles).reshape(rows, cols, feats).astype(BF16)
    own_ref[0, 0] = grid[: own_ref.shape[2]]
    halo_ref[0, 0] = grid[own_ref.shape[2] :]


def norm(x, gain, bias):
    center = x - jnp.mean(x, axis=0, keepdims=True)
    spread = jnp.mean(center * center, axis=0, keepdims=True)
    rstd = lax.rsqrt(spread + EPS)
    xhat = center * rstd
    return xhat, rstd, (xhat * gain + bias).astype(BF16)


def norm_back(d_norm, xhat, rstd, gain):
    grad_gain = d_norm * xhat
    e_mean = jnp.mean(d_norm * gain, axis=0, keepdims=True)
    x_mean = jnp.mean(grad_gain * gain, axis=0, keepdims=True)
    d_hidden = (d_norm * gain - e_mean - xhat * x_mean) * rstd
    return d_hidden, lane_sum(grad_gain), lane_sum(d_norm)


def gelu_parts(pre):
    upper = 0.5 + 0.5 * lax.erf(pre * (0.5**0.5))
    density = jnp.exp(pre * pre * -0.5) * 0.3989422804014327
    return (pre * upper).astype(BF16), upper + pre * density


def head_sum(x):
    return jnp.sum(x.reshape(HEADS, HEAD_DIM, x.shape[1]), axis=1)


def head_spread(p):
    return jnp.broadcast_to(p[:, None, :], (HEADS, HEAD_DIM, p.shape[1])).reshape(
        HEADS * HEAD_DIM, p.shape[1]
    )


def blocks_of(x, left, places):
    zero = jnp.zeros((HEAD_DIM, 128), x.dtype)
    halves = (x[:, :128], x[:, 128:])
    rows = []
    for place in places:
        half = halves[place // 2]
        kept = jnp.where(left, zero, half) if place % 2 else jnp.where(left, half, zero)
        rows.append(jnp.concatenate([zero, kept] if place // 2 else [kept, zero], axis=1))
    return jnp.concatenate(rows, axis=0)


BY_LANES = (0, 1, 2, 3)
BY_ROWS = (0, 2, 1, 3)


def unit_lanes(x, pair, hp):
    cols = slice(128 * pair, 128 * pair + 128)
    first = 128 * hp
    return jnp.concatenate([x[first : first + 64, cols], x[first + 64 : first + 128, cols]], axis=1)


def unit_rows(x, pair, hp):
    dims = slice(128 * hp, 128 * hp + 128)
    first = 128 * pair
    return jnp.concatenate([x[first : first + 64, dims], x[first + 64 : first + 128, dims]], axis=1)


def put_unit(ref, base, pair, hp, value):
    cols = slice(128 * pair, 128 * pair + 128)
    first = base + 128 * hp
    ref[first : first + 64, cols] = value[:, :128]
    ref[first + 64 : first + 128, cols] = value[:, 128:]


def spread_vectors(pieces_ref, space, feed, time, last):
    pieces_ref[...] = jnp.zeros_like(pieces_ref)
    starts = (512, 1024, 0)
    sources = [
        (part, first)
        for kind, first in enumerate(starts)
        for part, first in (
            (space, first),
            (feed, first),
            (time, first),
            (last, (0, 512, 1024)[kind]),
        )
    ]
    for z in range(4):
        rows = [part[0:1, first + 128 * z : first + 128 * z + 128] for part, first in sources]
        for part in (feed, last):
            for m in range(4):
                first = 1536 + 512 * z + 128 * m
                rows.append(part[0:1, first : first + 128])
        for r, row in enumerate(rows):
            pieces_ref[8 * z + r // 3, r % 3 : r % 3 + 1, :] = row


def pack(info, pieces, place, vectors=None):
    me, row = info[0], info[1]
    core, cell = lax.rem(me, 2), lax.div(me, 2)

    def step(i, carry):
        c, z = lax.div(i, 4), lax.rem(i, 4)
        for j in range(4):
            base = 0
            for acc_ref, depth in pieces:
                first = (z ^ row) * (8 * depth) + ((core ^ c) * 4 + (cell ^ j)) * depth
                part = acc_ref[pl.ds(pl.multiple_of(first, 16), depth), :].astype(BF16)
                for k in range(part.shape[1] // 512):
                    place(j, c, z, slice(base, base + depth), part[:, 512 * k : 512 * (k + 1)])
                    base += depth
            if vectors is not None:
                part = vectors[(z ^ row) * 8 + (core ^ c) * 4 + (cell ^ j)].astype(BF16)
                part = jnp.concatenate([part, jnp.zeros((16, 384), BF16)], axis=1)
                place(j, c, z, slice(base, base + 16), part)
        return carry

    lax.fori_loop(0, 8, step, 0)


def row_sums(acc):
    return lax.dot_general(
        jnp.ones((8, 128), F32), acc, NT, precision=lax.Precision.HIGHEST, preferred_element_type=F32
    )


A2, XHAT2, O2, R1_ROWS = 0, 512, 1024, 1536
C1, XHAT1, ACT0, SLOPE0, R3_ROWS = 0, 512, 1024, 3072, 5120
A0, XHAT0, O0, QKV0, P0, R2_ROWS = 0, 512, 1024, 1536, 3072, 3584


def state_kernel(
    info,
    own_ref,
    halo_ref,
    mask_ref,
    vec_ref,
    wqkv_t_ref,
    wproj_t_ref,
    wup_t_ref,
    wdown_t_ref,
    *refs,
    item,
):
    r1_ref, r2_ref, r3_ref, qkv2_ref, p2_ref, stat_ref, x3_ref, kv_ref, scores_ref = refs[-9:]
    frame = pl.program_id(0)
    lanes = r1_ref.shape[2]
    feats = wqkv_t_ref.shape[2]

    def vec(index, size=512):
        return wide(vec_ref[512 * index : 512 * index + size, :], lanes)

    @pl.when(frame == 0)
    def _():
        kv_ref[...] = jnp.zeros_like(kv_ref)

    x0 = load_frame(own_ref[0, 0], halo_ref[0, 0])
    xhat0, rstd0, a0 = norm(x0, vec(0), vec(1))
    r2_ref[0, A0 : A0 + 512, :] = a0
    r2_ref[0, XHAT0 : XHAT0 + 512, :] = xhat0.astype(BF16)
    qkv = mm(wqkv_t_ref[0], a0).astype(BF16)
    r2_ref[0, QKV0 : QKV0 + 1536, :] = qkv
    keys = qkv[512:1024].T
    left = half_mask((64, 128))
    units = [(pair, hp) for pair in range(lanes // 128) for hp in range(HEADS // 2)]
    for n, (pair, hp) in enumerate(units):
        query = blocks_of(unit_lanes(qkv[:512], pair, hp), left, BY_ROWS)
        scores = mm(unit_rows(keys, pair, hp), query) * SCALE
        scores_ref[n] = jnp.where(mask_ref[pair] > 0.5, scores, NEG)
    for n, (pair, hp) in enumerate(units):
        scores = scores_ref[n]
        exponent = jnp.exp(scores - jnp.max(scores, axis=0, keepdims=True))
        weights = exponent * (1.0 / jnp.sum(exponent, axis=0, keepdims=True))
        r2_ref[0, P0 + 64 * n : P0 + 64 * n + 64, :] = weights.astype(BF16)
    for n, (pair, hp) in enumerate(units):
        weights = blocks_of(r2_ref[0, P0 + 64 * n : P0 + 64 * n + 64, :], left, BY_LANES)
        mixed = mm(unit_lanes(qkv[1024:], pair, hp), weights).astype(BF16)
        put_unit(r2_ref.at[0], O0, pair, hp, mixed)
    x1 = x0 + mm(wproj_t_ref[0], r2_ref[0, O0 : O0 + 512, :]) + vec(2)

    xhat1, rstd1, c1 = norm(x1, vec(3), vec(4))
    r3_ref[0, C1 : C1 + 512, :] = c1
    r3_ref[0, XHAT1 : XHAT1 + 512, :] = xhat1.astype(BF16)
    x2 = x1 + vec(5)
    for k in range(wup_t_ref.shape[1] // CHUNK):
        part = slice(CHUNK * k, CHUNK * (k + 1))
        pre = mm(wup_t_ref[0, part, :], c1) + vec(9 + k)
        act, slope = gelu_parts(pre)
        r3_ref[0, ACT0 + CHUNK * k : ACT0 + CHUNK * (k + 1), :] = act
        r3_ref[0, SLOPE0 + CHUNK * k : SLOPE0 + CHUNK * (k + 1), :] = slope.astype(BF16)
        x2 = x2 + mm(wdown_t_ref[0, :, part], act)

    xhat2, rstd2, a2 = norm(x2, vec(6), vec(7))
    r1_ref[0, A2 : A2 + 512, :] = a2
    r1_ref[0, XHAT2 : XHAT2 + 512, :] = xhat2.astype(BF16)
    qkv = mm(wqkv_t_ref[1], a2).astype(BF16)
    qkv2_ref[0] = qkv
    kv_ref[frame] = qkv[512:]
    query = qkv[:512].astype(F32) * SCALE
    scores = []
    for u in range(kv_ref.shape[0]):
        score = head_sum(query * kv_ref[u, :512, :].astype(F32))
        scores.append(jnp.where(u <= frame, score, NEG))
    top = functools.reduce(jnp.maximum, scores)
    exponents = [jnp.exp(s - top) for s in scores]
    scale = 1.0 / sum(exponents)
    mixed = jnp.zeros((feats, lanes), F32)
    for u in range(kv_ref.shape[0]):
        weight = exponents[u] * scale
        p2_ref[0, u] = weight
        weight = weight.astype(BF16).astype(F32)
        mixed = mixed + head_spread(weight) * kv_ref[u, 512:, :].astype(F32)
    o2 = mixed.astype(BF16)
    r1_ref[0, O2 : O2 + 512, :] = o2
    is_video = info[2 + item].astype(F32)
    x3_ref[0] = x2 + is_video * (mm(wproj_t_ref[1], o2) + vec(8))
    stat_ref[0] = jnp.concatenate([rstd0, rstd1, rstd2, jnp.zeros((5, lanes), F32)], axis=0)


def last_kernel(info, items, *refs):
    x3_ref, cot_own_ref, *refs = refs
    cot_halo_refs, refs = refs[:items], refs[items:]
    vec_ref, wup_t_ref, wdown_t_ref, wup_ref, wdown_ref, *refs = refs
    out_own_ref, out_halo_ref, g3_ref, *refs = refs
    keep_ref, send_ref, sums_ref, acc_up, acc_down, acc_vec = refs
    item, frame = pl.program_id(0), pl.program_id(1)
    frames = pl.num_programs(1)
    feats, lanes = g3_ref.shape[1:]

    def vec(index, size=512):
        return wide(vec_ref[512 * index : 512 * index + size, :], lanes)

    @pl.when((item == 0) & (frame == 0))
    def _():
        for acc in (acc_up, acc_down, acc_vec):
            acc[...] = jnp.zeros_like(acc)

    is_valid = jnp.where(frame < info[2 + items + item], 1.0, 0.0)
    halo = cot_halo_refs[0][0, 0]
    for i in range(1, items):
        halo = jnp.where(item == i, cot_halo_refs[i][0, 0], halo)
    g4 = load_frame(cot_own_ref[0, 0], halo) * is_valid
    grad_low = g4.astype(BF16)
    x3 = x3_ref[0]
    xhat3, rstd3, c3 = norm(x3, vec(0), vec(1))
    x4 = x3 + vec(2)
    d_norm = jnp.zeros((feats, lanes), F32)
    for k in range(wup_t_ref.shape[1] // CHUNK):
        part = slice(CHUNK * k, CHUNK * (k + 1))
        pre = mm(wup_t_ref[0, part, :], c3) + vec(3 + k)
        act, slope = gelu_parts(pre)
        x4 = x4 + mm(wdown_t_ref[0, :, part], act)
        d_pre = (mm(wdown_ref[0, part, :], grad_low) * slope).astype(BF16)
        d_norm = d_norm + mm(wup_ref[0, :, part], d_pre)
        acc_up[:, part] += mm(c3, d_pre, NT)
        acc_down[part, :] += mm(act, grad_low, NT)
        acc_vec[1536 + CHUNK * k : 1536 + CHUNK * (k + 1), :] += lane_sum(d_pre.astype(F32))
    store_frame(x4 * is_valid, out_own_ref, out_halo_ref)
    d_hidden, gain_part, bias_part = norm_back(d_norm, xhat3, rstd3, vec(0))
    acc_vec[0:512, :] += gain_part
    acc_vec[512:1024, :] += bias_part
    acc_vec[1024:1536, :] += lane_sum(g4)
    g3_ref[0] = g4 + d_hidden

    @pl.when((item == items - 1) & (frame == frames - 1))
    def _():
        pack(info, [(acc_up, 16), (acc_down, 64)], core_first(keep_ref, send_ref))
        sums_ref[...] = row_sums(acc_vec[...])


def core_first(keep_ref, send_ref):
    def place(j, c, z, rows, value):
        @pl.when(c == 0)
        def _():
            keep_ref[j, z, rows, :] = value

        @pl.when(c == 1)
        def _():
            send_ref[j, z, rows, :] = value

    return place


def time_kernel(
    info,
    g3_ref,
    r1_ref,
    qkv2_ref,
    p2_ref,
    stat_ref,
    vec_ref,
    wqkv_ref,
    wproj_ref,
    g2_ref,
    keep_ref,
    send_ref,
    sums_ref,
    acc_qkv,
    acc_proj,
    acc_vec,
    dkv_ref,
):
    item, step = pl.program_id(0), pl.program_id(1)
    items, frames = pl.num_programs(0), pl.num_programs(1)
    frame = frames - 1 - step
    feats, lanes = g2_ref.shape[1:]

    @pl.when((item == 0) & (step == 0))
    def _():
        for acc in (acc_qkv, acc_proj, acc_vec):
            acc[...] = jnp.zeros_like(acc)

    @pl.when(step == 0)
    def _():
        dkv_ref[...] = jnp.zeros_like(dkv_ref)

    g3 = g3_ref[0]
    is_video = info[2 + item].astype(F32)
    d_attn = (g3 * is_video).astype(BF16)
    acc_proj[...] += mm(r1_ref[0, O2 : O2 + 512, :], d_attn, NT)
    acc_vec[0:512, :] += lane_sum(d_attn.astype(F32))
    d_mixed = mm(wproj_ref[0], d_attn).astype(BF16).astype(F32)
    query = qkv2_ref[frame, :512, :].astype(F32) * SCALE
    count = qkv2_ref.shape[0]
    weights = [p2_ref[0, u] for u in range(count)]
    d_weights = []
    for u in range(count):
        d_weights.append(head_sum(d_mixed * qkv2_ref[u, 1024:, :].astype(F32)))
    inner = sum(w * d for w, d in zip(weights, d_weights))
    d_query = jnp.zeros((feats, lanes), F32)
    for u in range(count):
        d_score = (weights[u] * (d_weights[u] - inner)).astype(BF16).astype(F32)
        spread = head_spread(d_score)
        d_query = d_query + spread * qkv2_ref[u, 512:1024, :].astype(F32)
        dkv_ref[u, :512, :] += spread * query
        dkv_ref[u, 512:, :] += head_spread(weights[u].astype(BF16).astype(F32)) * d_mixed
    d_qkv = jnp.concatenate(
        [(d_query * SCALE).astype(BF16), dkv_ref[frame].astype(BF16)], axis=0
    )
    acc_qkv[...] += mm(r1_ref[0, A2 : A2 + 512, :], d_qkv, NT)
    d_norm = mm(wqkv_ref[0], d_qkv)
    xhat = r1_ref[0, XHAT2 : XHAT2 + 512, :].astype(F32)
    gain = wide(vec_ref[...], lanes)
    d_hidden, gain_part, bias_part = norm_back(d_norm, xhat, stat_ref[0, 2:3, :], gain)
    acc_vec[512:1024, :] += gain_part
    acc_vec[1024:1536, :] += bias_part
    g2_ref[0] = g3 + d_hidden

    @pl.when((item == items - 1) & (step == frames - 1))
    def _():
        pack(info, [(acc_qkv, 16), (acc_proj, 16)], core_first(keep_ref, send_ref))
        sums_ref[...] = row_sums(acc_vec[...])


def feed_kernel(info, g2_ref, r3_ref, stat_ref, vec_ref, wup_ref, wdown_ref, *refs, passes):
    g1_ref, keep_ref, send_ref, sums_ref = refs[passes : passes + 4]
    acc_up, acc_down, acc_vec = refs[-3:]
    plane, planes = pl.program_id(0), pl.num_programs(0)
    feats, lanes = g1_ref.shape[1:]

    @pl.when(plane == 0)
    def _():
        for acc in (acc_up, acc_down, acc_vec):
            acc[...] = jnp.zeros_like(acc)

    g2 = g2_ref[0]
    grad_low = g2.astype(BF16)
    acc_vec[0:512, :] += lane_sum(grad_low.astype(F32))
    c1 = r3_ref[0, C1 : C1 + 512, :]
    d_norm = jnp.zeros((feats, lanes), F32)
    for k in range(wup_ref.shape[2] // CHUNK):
        part = slice(CHUNK * k, CHUNK * (k + 1))
        slope = r3_ref[0, SLOPE0 + CHUNK * k : SLOPE0 + CHUNK * (k + 1), :].astype(F32)
        d_pre = (mm(wdown_ref[0, part, :], grad_low) * slope).astype(BF16)
        d_norm = d_norm + mm(wup_ref[0, :, part], d_pre)
        acc_up[:, part] += mm(c1, d_pre, NT)
        acc_down[part, :] += mm(
            r3_ref[0, ACT0 + CHUNK * k : ACT0 + CHUNK * (k + 1), :], grad_low, NT
        )
        acc_vec[1536 + CHUNK * k : 1536 + CHUNK * (k + 1), :] += lane_sum(d_pre.astype(F32))
    xhat = r3_ref[0, XHAT1 : XHAT1 + 512, :].astype(F32)
    gain = wide(vec_ref[...], lanes)
    d_hidden, gain_part, bias_part = norm_back(d_norm, xhat, stat_ref[0, 1:2, :], gain)
    acc_vec[512:1024, :] += gain_part
    acc_vec[1024:1536, :] += bias_part
    g1_ref[0] = g2 + d_hidden

    @pl.when(plane == planes - 1)
    def _():
        pack(info, [(acc_up, 16), (acc_down, 64)], core_first(keep_ref, send_ref))
        sums_ref[...] = row_sums(acc_vec[...])


def core_first(keep_ref, send_ref):
    def place(j, c, z, rows, value):
        @pl.when(c == 0)
        def _():
            keep_ref[j, z, rows, :] = value

        @pl.when(c == 1)
        def _():
            send_ref[j, z, rows, :] = value

    return place


def middle_kernel(
    info,
    g3_ref,
    r1_ref,
    qkv2_ref,
    p2_ref,
    stat_ref,
    vec_ref,
    wqkv_ref,
    wproj_ref,
    wup_ref,
    wdown_ref,
    g1_ref,
    keep_ref,
    send_ref,
    sums_ref,
    acc_up,
    acc_down,
    acc_qkv,
    acc_proj,
    acc_vec,
    dkv_ref,
):
    item, step = pl.program_id(0), pl.program_id(1)
    items, frames = pl.num_programs(0), pl.num_programs(1)
    frame = frames - 1 - step
    lanes = r1_ref.shape[2]
    feats = wqkv_ref.shape[1]

    def vec(index, size=512):
        return wide(vec_ref[512 * index : 512 * index + size, :], lanes)

    @pl.when((item == 0) & (step == 0))
    def _():
        for acc in (acc_up, acc_down, acc_qkv, acc_proj, acc_vec):
            acc[...] = jnp.zeros_like(acc)

    @pl.when(step == 0)
    def _():
        dkv_ref[...] = jnp.zeros_like(dkv_ref)

    g3 = g3_ref[0]
    is_video = info[2 + item].astype(F32)
    d_attn = (g3 * is_video).astype(BF16)
    acc_proj[...] += mm(r1_ref[0, O2 : O2 + 512, :], d_attn, NT)
    acc_vec[0:512, :] += lane_sum(d_attn.astype(F32))
    d_mixed = mm(wproj_ref[0], d_attn).astype(BF16).astype(F32)
    query = qkv2_ref[frame, :512, :].astype(F32) * SCALE
    count = qkv2_ref.shape[0]
    weights = [p2_ref[0, u] for u in range(count)]
    d_weights = []
    for u in range(count):
        d_weights.append(head_sum(d_mixed * qkv2_ref[u, 1024:, :].astype(F32)))
    inner = sum(w * d for w, d in zip(weights, d_weights))
    d_query = jnp.zeros((feats, lanes), F32)
    for u in range(count):
        d_score = (weights[u] * (d_weights[u] - inner)).astype(BF16).astype(F32)
        spread = head_spread(d_score)
        d_query = d_query + spread * qkv2_ref[u, 512:1024, :].astype(F32)
        dkv_ref[u, :512, :] += spread * query
        dkv_ref[u, 512:, :] += head_spread(weights[u].astype(BF16).astype(F32)) * d_mixed
    d_qkv = jnp.concatenate(
        [(d_query * SCALE).astype(BF16), dkv_ref[frame].astype(BF16)], axis=0
    )
    acc_qkv[...] += mm(r1_ref[0, A2 : A2 + 512, :], d_qkv, NT)
    d_norm = mm(wqkv_ref[0], d_qkv)
    xhat = r1_ref[0, XHAT2 : XHAT2 + 512, :].astype(F32)
    d_hidden, gain_part, bias_part = norm_back(d_norm, xhat, stat_ref[0, 2:3, :], vec(1))
    acc_vec[512:1024, :] += gain_part
    acc_vec[1024:1536, :] += bias_part
    g2 = g3 + d_hidden

    grad_low = g2.astype(BF16)
    acc_vec[1536:2048, :] += lane_sum(grad_low.astype(F32))
    c1 = r1_ref[0, C1 : C1 + 512, :]
    d_norm = jnp.zeros((feats, lanes), F32)
    for k in range(wup_ref.shape[2] // CHUNK):
        part = slice(CHUNK * k, CHUNK * (k + 1))
        slope = r1_ref[0, SLOPE0 + CHUNK * k : SLOPE0 + CHUNK * (k + 1), :].astype(F32)
        d_pre = (mm(wdown_ref[0, part, :], grad_low) * slope).astype(BF16)
        d_norm = d_norm + mm(wup_ref[0, :, part], d_pre)
        acc_up[:, part] += mm(c1, d_pre, NT)
        acc_down[part, :] += mm(
            r1_ref[0, ACT0 + CHUNK * k : ACT0 + CHUNK * (k + 1), :], grad_low, NT
        )
        acc_vec[3072 + CHUNK * k : 3072 + CHUNK * (k + 1), :] += lane_sum(d_pre.astype(F32))
    xhat = r1_ref[0, XHAT1 : XHAT1 + 512, :].astype(F32)
    d_hidden, gain_part, bias_part = norm_back(d_norm, xhat, stat_ref[0, 1:2, :], vec(0))
    acc_vec[2048:2560, :] += gain_part
    acc_vec[2560:3072, :] += bias_part
    g1_ref[0] = g2 + d_hidden

    @pl.when((item == items - 1) & (step == frames - 1))
    def _():
        pieces = [(acc_up, 16), (acc_down, 64), (acc_qkv, 16), (acc_proj, 16)]
        pack(info, pieces, core_first(keep_ref, send_ref))
        sums_ref[...] = row_sums(acc_vec[...])


def space_kernel(info, g1_ref, r2_ref, stat_ref, vec_ref, wqkv_ref, wproj_ref, *refs, first, last, passes):
    dqkv_ref, refs = refs[-1], refs[:-1]
    if not first:
        (qkv_in, proj_in, vec_in, _), refs = refs[:4], refs[4:]
    if last:
        (last_sums, time_sums, feed_sums), refs = refs[:3], refs[3:]
    out_own_ref, out_halo_ref, *refs = refs[passes:]
    if last:
        keep_ref, send_ref, *refs = refs
        *refs, vec_pieces = refs[passes:]
    acc_qkv, acc_proj, acc_vec = refs[:3]
    frame = pl.program_id(0)
    frames = pl.num_programs(0)
    lanes = r2_ref.shape[2]

    @pl.when(frame == 0)
    def _():
        for k, acc in enumerate((acc_qkv, acc_proj, acc_vec)):
            acc[...] = jnp.zeros_like(acc) if first else (qkv_in, proj_in, vec_in)[k][...]

    g1 = g1_ref[0]
    d_attn = g1.astype(BF16)
    acc_proj[...] += mm(r2_ref[0, O0 : O0 + 512, :], d_attn, NT)
    acc_vec[0:512, :] += lane_sum(d_attn.astype(F32))
    d_mixed = mm(wproj_ref[0], d_attn).astype(BF16)
    values = r2_ref[0, QKV0 + 1024 : QKV0 + 1536, :].T
    left = half_mask((64, 128))
    units = [(pair, hp) for pair in range(lanes // 128) for hp in range(HEADS // 2)]
    for n, (pair, hp) in enumerate(units):
        grad = unit_lanes(d_mixed, pair, hp)
        d_weights = mm(unit_rows(values, pair, hp), blocks_of(grad, left, BY_ROWS))
        low = r2_ref[0, P0 + 64 * n : P0 + 64 * n + 64, :]
        weights = low.astype(F32)
        inner = jnp.sum(weights * d_weights, axis=0, keepdims=True)
        d_scores = (weights * (d_weights - inner)).astype(BF16)
        slope = blocks_of(d_scores, left, BY_LANES)
        soft = blocks_of(low, left, BY_LANES)
        query = unit_lanes(r2_ref[0, QKV0 : QKV0 + 512, :], pair, hp)
        key = unit_lanes(r2_ref[0, QKV0 + 512 : QKV0 + 1024, :], pair, hp)
        put_unit(dqkv_ref, 0, pair, hp, (mm(key, slope) * SCALE).astype(BF16))
        put_unit(dqkv_ref, 512, pair, hp, (mm(query, slope, NT) * SCALE).astype(BF16))
        put_unit(dqkv_ref, 1024, pair, hp, mm(grad, soft, NT).astype(BF16))
    d_qkv = dqkv_ref[...]
    acc_qkv[...] += mm(r2_ref[0, A0 : A0 + 512, :], d_qkv, NT)
    d_norm = mm(wqkv_ref[0], d_qkv)
    xhat = r2_ref[0, XHAT0 : XHAT0 + 512, :].astype(F32)
    gain = wide(vec_ref[...], lanes)
    d_hidden, gain_part, bias_part = norm_back(d_norm, xhat, stat_ref[0, 0:1, :], gain)
    acc_vec[512:1024, :] += gain_part
    acc_vec[1024:1536, :] += bias_part
    store_frame(g1 + d_hidden, out_own_ref, out_halo_ref)

    if last:

        @pl.when(frame == frames - 1)
        def _():
            spread_vectors(
                vec_pieces, row_sums(acc_vec[...]), feed_sums[...], time_sums[...], last_sums[...]
            )
            place = core_first(keep_ref, send_ref)
            pack(info, [(acc_qkv, 16), (acc_proj, 16)], place, vec_pieces)


def put_rows(out_ref, slot, pieces, base, depth):
    for k in range(out_ref.shape[2] // 512):
        rows = pieces[base + depth * k : base + depth * (k + 1), :]
        out_ref[slot, :, 512 * k : 512 * (k + 1)] = rows.astype(F32)


EARLY_ROWS, LATE_ROWS = 192, 208


def unpack_early_kernel(info, mine_ref, other_ref, up_ref, down_ref, qkv_ref, proj_ref):
    pieces = jnp.where(pl.program_id(0) // 4 == info[0], mine_ref[0], other_ref[0])
    put_rows(up_ref, 0, pieces, 0, 16)
    put_rows(down_ref, 0, pieces, 64, 64)
    put_rows(qkv_ref, 0, pieces, 128, 16)
    put_rows(proj_ref, 0, pieces, 176, 16)


def unpack_late_kernel(info, mine_ref, other_ref, *refs):
    up_ref, down_ref, qkv_ref, proj_ref, gain_ref, bias_ref, outb_ref, upb_ref, vec_ref = refs[-9:]
    place = pl.program_id(0)
    pieces = jnp.where(place // 4 == info[0], mine_ref[0], other_ref[0])
    put_rows(up_ref, 0, pieces, 0, 16)
    put_rows(down_ref, 0, pieces, 64, 64)
    put_rows(qkv_ref, 0, pieces, 128, 16)
    put_rows(proj_ref, 0, pieces, 176, 16)
    vec_ref[place] = pieces[192:208, :128].astype(F32)

    @pl.when(place == 7)
    def _():
        for k, ref in enumerate((gain_ref, bias_ref, outb_ref)):
            for n in range(4):
                r = 4 * k + n
                ref[n : n + 1, :] = vec_ref[r // 3, r % 3 : r % 3 + 1, :]
        for k in range(2):
            for m in range(4):
                r = 12 + 4 * k + m
                upb_ref[k : k + 1, 128 * m : 128 * m + 128] = vec_ref[r // 3, r % 3 : r % 3 + 1, :]


def split_sum_kernel(groups, *refs):
    counts = [(len(g), g[0].shape[0]) for g in groups]
    ins, outs = refs[: sum(c for c, _ in counts)], refs[sum(c for c, _ in counts) :]
    for count, pieces in counts:
        for k in range(pieces):
            total = ins[0][k].astype(F32)
            for ref in ins[1:count]:
                total = total + ref[k].astype(F32)
            outs[k][...] = total.astype(BF16)
        ins, outs = ins[count:], outs[pieces:]


def join_sum_kernel(counts, *refs):
    base = 0
    for count in counts:
        total = refs[0][...].astype(F32)
        for ref in refs[1:count]:
            total = total + ref[...].astype(F32)
        refs[-1][base : base + total.shape[0], :] = total.astype(BF16)
        base += total.shape[0]
        refs = refs[count:]


def stack_kernel(*refs):
    for k, ref in enumerate(refs[:-1]):
        refs[-1][k] = ref[...]


def whole_spec(shape, single=True):
    mode = pl.Buffered(1) if single else None
    return pl.BlockSpec(shape, lambda *_: (0,) * len(shape), pipeline_mode=mode)


def part_spec(shape, index):
    def place(*_):
        return (index,) + (0,) * (len(shape) - 1)

    return pl.BlockSpec((1,) + tuple(shape[1:]), place, pipeline_mode=pl.Buffered(1))


def params(axes, limit=56 * MIB):
    return pltpu.CompilerParams(
        dimension_semantics=("arbitrary",) * axes, vmem_limit_bytes=limit
    )


def cost(flops, moved):
    return pl.CostEstimate(flops=int(flops), bytes_accessed=int(moved), transcendentals=0)


def sds(shape, dtype):
    return jax.ShapeDtypeStruct(shape, dtype)


ANY = pl.BlockSpec(memory_space=pl.ANY)


def run_state(info, item, tokens, halo, mask, vecs, weights, before):
    wqkv_t, wproj_t, wup_t, wdown_t = weights
    items, frames, grid_rows, cols, feats = tokens.shape
    lanes = grid_rows * cols
    planes = items * frames
    half = (1, 1, SHIFT, cols, feats)

    def plane_spec(*shape):
        return pl.BlockSpec(
            (1,) + shape, lambda t, info: (item * frames + t,) + (0,) * len(shape)
        )

    shapes = [
        (R1_ROWS, lanes, BF16),
        (R2_ROWS, lanes, BF16),
        (R3_ROWS, lanes, BF16),
        (3 * feats, lanes, BF16),
        (frames, HEADS, lanes, F32),
        (8, lanes, F32),
        (feats, lanes, F32),
    ]
    operands = [info, tokens, halo, mask, vecs, wqkv_t, wproj_t, wup_t, wdown_t]
    start = len(operands)
    return pl.pallas_call(
        functools.partial(state_kernel, item=item),
        grid_spec=pltpu.PrefetchScalarGridSpec(
            num_scalar_prefetch=1,
            grid=(frames,),
            in_specs=[
                pl.BlockSpec(half, lambda t, info: (item, t, 1, 0, 0)),
                pl.BlockSpec(half, lambda t, info: (0, t, 0, 0, 0)),
                whole_spec(mask.shape),
                whole_spec(vecs.shape),
                whole_spec(wqkv_t.shape),
                whole_spec(wproj_t.shape),
                part_spec(wup_t.shape, 0),
                part_spec(wdown_t.shape, 0),
            ]
            + [ANY] * len(before),
            out_specs=[plane_spec(*s[:-1]) for s in shapes],
            scratch_shapes=[
                pltpu.VMEM((frames, 2 * feats, lanes), BF16),
                pltpu.VMEM((lanes // 128 * (HEADS // 2), 64, 256), F32),
            ],
        ),
        out_shape=[sds((planes,) + s[:-1], s[-1]) for s in shapes],
        input_output_aliases={start + k: k for k in range(len(before))},
        compiler_params=params(1, 40 * MIB),
        cost_estimate=cost(11e9 * 2, 50e6),
        name="state",
    )(*operands, *before)


def run_last(info, x3, cotangent, cot_halos, vecs, weights):
    wup_t, wdown_t, wup, wdown = weights
    items, frames, grid_rows, cols, feats = cotangent.shape
    planes, _, lanes = x3.shape
    hidden = wup.shape[2]
    half = (1, 1, SHIFT, cols, feats)
    own_spec = pl.BlockSpec(half, lambda i, t, info: (i, t, 1, 0, 0))
    halo_spec = pl.BlockSpec(half, lambda i, t, info: (i, t, 0, 0, 0))

    def item_halo(k):
        def place(i, t, info):
            return (0, jnp.where(i == k, t, jnp.where(i < k, 0, frames - 1)), 0, 0, 0)

        return pl.BlockSpec(half, place)

    plane = pl.BlockSpec((1, feats, lanes), lambda i, t, info: (i * frames + t, 0, 0))
    return pl.pallas_call(
        lambda info, *refs: last_kernel(info, items, *refs),
        grid_spec=pltpu.PrefetchScalarGridSpec(
            num_scalar_prefetch=1,
            grid=(items, frames),
            in_specs=[plane, own_spec]
            + [item_halo(k) for k in range(items)]
            + [
                whole_spec(vecs.shape),
                part_spec(wup_t.shape, 1),
                part_spec(wdown_t.shape, 1),
                part_spec(wup.shape, 1),
                part_spec(wdown.shape, 1),
            ],
            out_specs=[own_spec, halo_spec, plane]
            + [whole_spec((4, 4, 128, 512))] * 2
            + [whole_spec((8, 3584))],
            scratch_shapes=[
                pltpu.VMEM((feats, hidden), F32),
                pltpu.VMEM((hidden, feats), F32),
                pltpu.VMEM((3584, 128), F32),
            ],
        ),
        out_shape=[
            sds(cotangent.shape, BF16),
            sds((items, frames, SHIFT, cols, feats), BF16),
            sds((planes, feats, lanes), F32),
        ]
        + [sds((4, 4, 128, 512), BF16)] * 2
        + [sds((8, 3584), F32)],
        compiler_params=params(2, 44 * MIB),
        cost_estimate=cost(32e9 * 1.2, 40e6),
        name="last",
    )(info, x3, cotangent, *cot_halos, vecs, wup_t, wdown_t, wup, wdown)


def run_time(info, g3, r1, qkv2, p2, stats, vecs, weights, items):
    wqkv, wproj = weights
    planes, feats, lanes = g3.shape
    frames = planes // items

    def plane_spec(*shape):
        return pl.BlockSpec(
            (1,) + shape,
            lambda i, s, info: (i * frames + frames - 1 - s,) + (0,) * len(shape),
        )

    return pl.pallas_call(
        time_kernel,
        grid_spec=pltpu.PrefetchScalarGridSpec(
            num_scalar_prefetch=1,
            grid=(items, frames),
            in_specs=[
                plane_spec(feats, lanes),
                plane_spec(R1_ROWS, lanes),
                pl.BlockSpec((frames, 3 * feats, lanes), lambda i, s, info: (i, 0, 0)),
                plane_spec(frames, HEADS, lanes),
                plane_spec(8, lanes),
                whole_spec(vecs.shape),
                part_spec(wqkv.shape, 1),
                part_spec(wproj.shape, 1),
            ],
            out_specs=[
                plane_spec(feats, lanes),
                whole_spec((4, 4, 64, 512)),
                whole_spec((4, 4, 64, 512)),
                whole_spec((8, 1536)),
            ],
            scratch_shapes=[
                pltpu.VMEM((feats, 3 * feats), F32),
                pltpu.VMEM((feats, feats), F32),
                pltpu.VMEM((1536, 128), F32),
                pltpu.VMEM((frames, 2 * feats, lanes), F32),
            ],
        ),
        out_shape=[
            sds((planes, feats, lanes), F32),
            sds((4, 4, 64, 512), BF16),
            sds((4, 4, 64, 512), BF16),
            sds((8, 1536), F32),
        ],
        compiler_params=params(2, 40 * MIB),
        cost_estimate=cost(30e9, 40e6),
        name="time",
    )(info, g3, r1, qkv2, p2, stats, vecs, wqkv, wproj)


def run_feed(info, g2, r3, stats, vecs, weights, passes):
    wup, wdown = weights
    planes, feats, lanes = g2.shape
    hidden = wup.shape[2]

    def plane_spec(*shape):
        return pl.BlockSpec((1,) + shape, lambda n, info: (n,) + (0,) * len(shape))

    return pl.pallas_call(
        functools.partial(feed_kernel, passes=len(passes)),
        grid_spec=pltpu.PrefetchScalarGridSpec(
            num_scalar_prefetch=1,
            grid=(planes,),
            in_specs=[
                plane_spec(feats, lanes),
                plane_spec(R3_ROWS, lanes),
                plane_spec(8, lanes),
                whole_spec(vecs.shape),
                part_spec(wup.shape, 0),
                part_spec(wdown.shape, 0),
            ]
            + [ANY] * len(passes),
            out_specs=[
                plane_spec(feats, lanes),
                whole_spec((4, 4, 128, 512)),
                whole_spec((4, 4, 128, 512)),
                whole_spec((8, 3584)),
            ]
            + [ANY] * len(passes),
            scratch_shapes=[
                pltpu.VMEM((feats, hidden), F32),
                pltpu.VMEM((hidden, feats), F32),
                pltpu.VMEM((3584, 128), F32),
            ],
        ),
        out_shape=[
            sds((planes, feats, lanes), F32),
            sds((4, 4, 128, 512), BF16),
            sds((4, 4, 128, 512), BF16),
            sds((8, 3584), F32),
        ]
        + [sds(p.shape, p.dtype) for p in passes],
        input_output_aliases={7 + k: 4 + k for k in range(len(passes))},
        compiler_params=params(1, 44 * MIB),
        cost_estimate=cost(30e9, 40e6),
        name="feed",
    )(info, g2, r3, stats, vecs, wup, wdown, *passes)


def run_space(info, item, g1, r2, stats, vecs, weights, shape, before, sums, passes):
    wqkv, wproj = weights
    items, frames, grid_rows, cols, feats = shape
    planes, _, lanes = g1.shape
    half = (1, 1, SHIFT, cols, feats)
    first, last = item == 0, item == items - 1

    def plane_spec(*tail):
        return pl.BlockSpec(
            (1,) + tail, lambda t, info: (item * frames + t,) + (0,) * len(tail)
        )

    accs = [(feats, 3 * feats), (feats, feats), (1536, 128)]
    halves = [(4, 4, 80, 512), (4, 4, 80, 512)]
    in_specs = [
        plane_spec(feats, lanes),
        plane_spec(R2_ROWS, lanes),
        plane_spec(8, lanes),
        whole_spec(vecs.shape),
        part_spec(wqkv.shape, 0),
        part_spec(wproj.shape, 0),
    ]
    operands = [info, g1, r2, stats, vecs, wqkv, wproj]
    aliases = {}
    if not first:
        in_specs += [whole_spec(a) for a in accs] + [ANY]
        aliases = {len(operands) + 3: 0}
    in_specs += [whole_spec(v.shape) for v in sums]
    start = len(in_specs) + 1
    in_specs += [ANY] * len(passes)
    out_specs = [
        pl.BlockSpec(half, lambda t, info: (item, t, 1, 0, 0)),
        pl.BlockSpec(half, lambda t, info: (0, t, 0, 0, 0)),
    ]
    out_shape = [sds(shape, BF16), sds((1, frames, SHIFT, cols, feats), BF16)]
    scratch = []
    if last:
        out_specs += [whole_spec(h) for h in halves]
        out_shape += [sds(h, BF16) for h in halves]
        scratch += [pltpu.VMEM(a, F32) for a in accs] + [pltpu.VMEM((32, 16, 128), F32)]
    else:
        out_specs += [whole_spec(a) for a in accs]
        out_shape += [sds(a, F32) for a in accs]
    aliases.update({start + k: len(out_specs) + k for k in range(len(passes))})
    out_specs += [ANY] * len(passes)
    out_shape += [sds(p.shape, p.dtype) for p in passes]
    return pl.pallas_call(
        functools.partial(space_kernel, first=first, last=last, passes=len(passes)),
        grid_spec=pltpu.PrefetchScalarGridSpec(
            num_scalar_prefetch=1,
            grid=(frames,),
            in_specs=in_specs,
            out_specs=out_specs,
            scratch_shapes=scratch + [pltpu.VMEM((3 * feats, lanes), BF16)],
        ),
        out_shape=out_shape,
        input_output_aliases=aliases,
        compiler_params=params(1, 32 * MIB),
        cost_estimate=cost(7e9 * 2, 30e6),
        name="space",
    )(*operands, *before, *sums, *passes)


def run_unpack(info, chip, other, outs):
    rows = chip.shape[1]
    slot = 0 if outs else 1

    def out(depth, width):
        return pl.BlockSpec((1, depth, width), lambda q, info: (slot, q, 0))

    def piece(q, info):
        return (lax.rem(q, 4) ^ info[1], 0, 0)

    shapes = [(2, 128, 2048), (2, 512, 512), (2, 128, 1536), (2, 128, 512)]
    specs = [out(16, 2048), out(64, 512), out(16, 1536), out(16, 512)]
    small = [(4, 128), (4, 128), (4, 128), (2, 512)] if outs else []
    return pl.pallas_call(
        unpack_late_kernel if outs else unpack_early_kernel,
        grid_spec=pltpu.PrefetchScalarGridSpec(
            num_scalar_prefetch=1,
            grid=(8,),
            in_specs=[pl.BlockSpec((1, rows, 512), piece)] * 2 + [ANY] * len(outs),
            out_specs=specs + [whole_spec(a) for a in small],
            scratch_shapes=[pltpu.VMEM((8, 16, 128), F32)] if outs else [],
        ),
        out_shape=[sds(a, F32) for a in shapes + small],
        input_output_aliases={3 + k: k for k in range(len(outs))},
        compiler_params=params(1, 16 * MIB),
        cost_estimate=cost(0, 6e6),
        name="unpack",
    )(info, chip, other, *outs)


def split_sum(*groups):
    size = sum(a.size for g in groups for a in g)
    depths = [g[0].shape[-2] for g in groups]
    steps = next(n for n in (5, 4, 1) if all(d % (16 * n) == 0 for d in depths))

    def spec(shape):
        block = shape[:-2] + (shape[-2] // steps, shape[-1])
        return pl.BlockSpec(block, lambda i: (0,) * (len(shape) - 2) + (i, 0))

    ins = [a for g in groups for a in g]
    outs = [g[0].shape[1:] for g in groups for _ in range(g[0].shape[0])]
    flat = pl.pallas_call(
        functools.partial(split_sum_kernel, groups),
        grid=(steps,),
        in_specs=[spec(a.shape) for a in ins],
        out_specs=[spec(o) for o in outs],
        out_shape=[sds(o, BF16) for o in outs],
        compiler_params=params(1, 24 * MIB),
        cost_estimate=cost(size, 3 * size),
        name="split_sum",
    )(*ins)
    result = []
    for g in groups:
        result.append(flat[: g[0].shape[0]])
        flat = flat[g[0].shape[0] :]
    return result


def join_sum(*groups):
    ins = [a for g in groups for a in g]
    rows = sum(g[0].shape[0] for g in groups)
    return pl.pallas_call(
        functools.partial(join_sum_kernel, [len(g) for g in groups]),
        out_shape=sds((rows, 512), BF16),
        compiler_params=params(0, 16 * MIB),
        name="join_sum",
    )(*ins)


def run_stack(*arrays):
    shape = (len(arrays),) + arrays[0].shape
    return pl.pallas_call(
        stack_kernel, out_shape=sds(shape, BF16), compiler_params=params(0, 16 * MIB), name="stack"
    )(*arrays)


def after(values, *others):
    count = len(values)
    return pl.pallas_call(
        lambda *refs: None,
        in_specs=[ANY] * (count + len(others)),
        out_specs=[ANY] * count,
        out_shape=[sds(v.shape, v.dtype) for v in values],
        input_output_aliases={k: k for k in range(count)},
        compiler_params=params(0, 1 * MIB),
        name="after",
    )(*values, *others)


def shift(block, axis, distance):
    size = lax.axis_size(axis)
    return lax.ppermute(block, axis, [(i, (i + distance) % size) for i in range(size)])


def swap(block, axis, bits):
    return lax.ppermute(block, axis, [(i, i ^ bits) for i in range(lax.axis_size(axis))])


def upper_bits(total):
    bit = 8
    while bit < lax.axis_size("dp"):
        total = (total.astype(F32) + swap(total, "dp", bit).astype(F32)).astype(BF16)
        bit *= 2
    return total


def region_label(index, extent):
    return jnp.where(index < extent - WIN, 0, jnp.where(index < extent - SHIFT, 1, 2))


def tile_mask(cols):
    height = lax.axis_size("rows") * WIN
    row_label = region_label(lax.axis_index("rows") * WIN + jnp.arange(WIN), height)
    place = (jnp.arange(WIN) + SHIFT) % WIN
    col_label = region_label(jnp.arange(0, cols, WIN)[:, None] + place, cols)
    label = (row_label[None, :, None] * 3 + col_label[:, None, :]).reshape(-1, WIN * WIN)
    same = (label[:, :, None] == label[:, None, :]).astype(F32)
    pairs = same.reshape(-1, 2, WIN * WIN, WIN * WIN).transpose(0, 2, 1, 3)
    pairs = pairs.reshape(-1, WIN * WIN, 2 * WIN * WIN)
    return jnp.concatenate([pairs, pairs], axis=2)


def gather(mine):
    chip = run_stack(mine, *[swap(mine, "dp", 2 * j) for j in range(1, 4)])
    return chip, swap(chip, "dp", 1)


def on_device(
    tokens,
    video_flag,
    frame_count,
    norm_gain,
    norm_bias,
    w_qkv,
    w_proj,
    w_up,
    w_down,
    out_bias,
    up_bias,
    cotangent,
):
    items, frames, grid_rows, cols, feats = tokens.shape
    place = lax.rem(lax.axis_index("dp"), 8)
    row = lax.axis_index("rows")
    info = jnp.concatenate([jnp.stack([place, row]), video_flag, frame_count]).astype(jnp.int32)
    unpack_info = jnp.stack([lax.rem(place, 2), lax.div(place, 2)]).astype(jnp.int32)

    def column(*parts):
        flat = jnp.concatenate([p.reshape(-1) for p in parts])
        return jnp.broadcast_to(flat[:, None], (flat.shape[0], 128))

    halos = [shift(tokens[:1, :, :SHIFT], "rows", -1)]
    cot_halos = []
    mask = tile_mask(cols)
    state_vecs = column(
        *[v[n] for n in range(3) for v in (norm_gain, norm_bias, out_bias)], up_bias[0]
    )
    last_vecs = column(norm_gain[3], norm_bias[3], out_bias[3], up_bias[1])
    time_vecs = column(norm_gain[2])
    feed_vecs = column(norm_gain[1])
    space_vecs = column(norm_gain[0])
    wqkv_t, wproj_t, wup_t, wdown_t = [jnp.swapaxes(w, 1, 2) for w in (w_qkv, w_proj, w_up, w_down)]
    kept = ()
    for i in range(items):
        ahead = [cotangent[i : i + 1, :, :SHIFT]]
        if i + 1 < items:
            ahead.append(tokens[i + 1 : i + 2, :, :SHIFT])
        ahead = after(ahead, halos[i])
        cot_halos.append(shift(ahead[0], "rows", -1))
        if i + 1 < items:
            halos.append(shift(ahead[1], "rows", -1))
        kept = run_state(
            info, i, tokens, halos[i], mask, state_vecs, (wqkv_t, wproj_t, wup_t, wdown_t), kept
        )
    r1, r2, r3, qkv2, p2, stats, x3 = kept
    out_own, out_halo, g3, keep1, send1, sums1 = run_last(
        info, x3, cotangent, cot_halos, last_vecs, (wup_t, wdown_t, w_up, w_down)
    )

    def cells(array, *taken):
        return split_sum([array, *taken])[0]

    def halves(array):
        return array.reshape((2, 2) + array.shape[1:])

    out_back = shift(out_halo, "rows", 1)
    core1 = swap(send1, "dp", 1)
    g2, keept, sendt, sumst = run_time(
        info, g3, r1, qkv2, p2, stats, time_vecs, (w_qkv, w_proj), items
    )
    cells1 = cells(keep1, core1)
    layer_out = lax.dynamic_update_slice(out_own, out_back, (0,) * 5)
    (sendt,) = after([sendt], cells1[0], layer_out)

    across1 = [swap(cells1[j], "dp", 2 * j) for j in range(1, 4)]
    coret = swap(sendt, "dp", 1)
    g1, keep0, send0, sums0, mine1, layer_out = run_feed(
        info, g2, r3, stats, feed_vecs, (w_up, w_down), [cells1[0], layer_out]
    )
    rows1, cellst = split_sum([halves(mine1), *[halves(a) for a in across1]], [keept, coret])
    (send0,) = after([send0], rows1[0], cellst[0])

    along1 = swap(rows1[1], "rows", 2)
    acrosst = [swap(cellst[j], "dp", 2 * j) for j in range(1, 4)]
    core0 = swap(send0, "dp", 1)
    grad_own, back0, *accs, mine1, minet = run_space(
        info, 0, g1, r2, stats, space_vecs, (w_qkv, w_proj), tokens.shape, (), (),
        [rows1[0], cellst[0]],
    )
    rows1, rowst, cells0 = split_sum(
        [mine1, along1], [halves(minet), *[halves(a) for a in acrosst]], [keep0, core0]
    )
    (back0,) = after([back0], rows1[0], rowst[0], cells0[0])

    alongt = swap(rowst[1], "rows", 2)
    across0 = [swap(cells0[j], "dp", 2 * j) for j in range(1, 4)]
    backs = [shift(back0, "rows", 1)]
    grad_own, back1, keeps, sends, mine1, minet, mine0 = run_space(
        info, 1, g1, r2, stats, space_vecs, (w_qkv, w_proj), tokens.shape,
        accs + [grad_own], (sums1, sumst, sums0), [rows1[0], rowst[0], cells0[0]],
    )
    rowst, rows0 = split_sum([minet, alongt], [mine0, *across0])
    sends, back1, near1 = after([sends, back1, rows1[1]], rowst[0], rows0[0])

    cores = swap(sends, "dp", 1)
    along0 = [swap(rows0[z], "rows", z) for z in range(1, 4)]
    near1 = swap(near1, "rows", 1)
    neart = swap(rowst[1], "rows", 1)
    cellss = cells(keeps, cores)
    acrosss = [swap(cellss[j], "dp", 2 * j) for j in range(1, 4)]
    early = upper_bits(join_sum([mine1, near1], [rowst[0], neart]))
    early_chip, early_other = gather(early)
    rowss = cells(cellss[0], *acrosss)
    backs.append(shift(back1, "rows", 1))
    alongs = [swap(rowss[z], "rows", z) for z in range(1, 4)]
    outs = run_unpack(unpack_info, early_chip, early_other, ())
    grad_tokens = grad_own
    for i in range(items):
        grad_tokens = lax.dynamic_update_slice(grad_tokens, backs[i], (i, 0, 0, 0, 0))
    late = join_sum([rows0[0], *along0], [rowss[0], *alongs])
    late_chip, late_other = gather(upper_bits(late))
    up, down, qkv, proj, gain, bias, outb, upb = run_unpack(
        unpack_info, late_chip, late_other, outs
    )
    return layer_out, grad_tokens, gain, bias, qkv, proj, up, down, outb, upb


def solution(mesh):
    split = P("dp", None, "rows", None, None)
    in_specs = (split, P("dp"), P("dp")) + (P(),) * 8 + (split,)
    out_specs = (
        split,
        split,
        P(None, "rows"),
        P(None, "rows"),
        P(None, "rows", None),
        P(None, "rows", None),
        P(None, "rows", None),
        P(None, "rows", None),
        P(None, "rows"),
        P(None, "rows"),
    )
    return jax.shard_map(
        on_device, mesh=mesh, in_specs=in_specs, out_specs=out_specs, check_vma=False
    )
```

```python
import functools
import math

import jax
import jax.numpy as jnp
from jax import lax
from jax.experimental import pallas as pl
from jax.experimental.pallas import tpu as pltpu
from jax.sharding import PartitionSpec as P

HEADS = 8
HEAD_DIM = 64
WIN = 8
SHIFT = 4
EPS = 1e-05
NEG = -1e30
SCALE = HEAD_DIM ** (-0.5)
BF16 = jnp.bfloat16
F32 = jnp.float32
NN = (((1,), (0,)), ((), ()))
NT = (((1,), (1,)), ((), ()))
TN = (((0,), (0,)), ((), ()))
CHUNK = 256
MIB = 1 << 20


def mm(left, right, dims=NN):
    return lax.dot_general(left, right, dims, preferred_element_type=F32)


def wide(column, lanes):
    return jnp.concatenate([column] * (lanes // column.shape[1]), axis=1)


def lane_sum(x):
    total = x[:, :128]
    for k in range(1, x.shape[1] // 128):
        total = total + x[:, 128 * k : 128 * (k + 1)]
    return total


def half_mask(shape):
    return lax.rem(lax.broadcasted_iota(jnp.int32, shape, len(shape) - 1), 128) < 64


def load_frame(own_ref, halo_ref):
    items = []
    for i in range(own_ref.shape[0]):
        grid = jnp.concatenate([own_ref[i, 0], halo_ref[i, 0]], axis=0).astype(F32)
        rows, cols, feats = grid.shape
        blocks = grid.reshape(rows, cols // WIN, WIN, feats)
        after = jnp.concatenate([blocks[:, 1:], blocks[:, :1]], axis=1)
        first = lax.broadcasted_iota(jnp.int32, blocks.shape, 2) < SHIFT
        tiles = jnp.where(first, after, blocks).transpose(1, 0, 2, 3)
        items.append(tiles.reshape(rows * cols, feats).astype(BF16).T)
    return jnp.concatenate(items, axis=1).astype(F32)


def store_frame(value, own_ref, halo_ref):
    count, _, half, cols, feats = own_ref.shape
    rows = 2 * half
    for i in range(count):
        part = value[:, rows * cols * i : rows * cols * (i + 1)]
        flat = part.astype(BF16).T.astype(F32)
        tiles = flat.reshape(cols // WIN, rows, WIN, feats).transpose(1, 0, 2, 3)
        before = jnp.concatenate([tiles[:, -1:], tiles[:, :-1]], axis=1)
        first = lax.broadcasted_iota(jnp.int32, tiles.shape, 2) < SHIFT
        grid = jnp.where(first, before, tiles).reshape(rows, cols, feats).astype(BF16)
        own_ref[i, 0] = grid[:half]
        halo_ref[i, 0] = grid[half:]


def item_row(values, lanes):
    size = lanes // len(values)
    return jnp.concatenate([jnp.full((1, size), v, F32) for v in values], axis=1)


def norm(x, gain, bias):
    center = x - jnp.mean(x, axis=0, keepdims=True)
    spread = jnp.mean(center * center, axis=0, keepdims=True)
    rstd = lax.rsqrt(spread + EPS)
    xhat = center * rstd
    return xhat, rstd, (xhat * gain + bias).astype(BF16)


def norm_back(d_norm, xhat, rstd, gain):
    grad_gain = d_norm * xhat
    e_mean = jnp.mean(d_norm * gain, axis=0, keepdims=True)
    x_mean = jnp.mean(grad_gain * gain, axis=0, keepdims=True)
    d_hidden = (d_norm * gain - e_mean - xhat * x_mean) * rstd
    return d_hidden, lane_sum(grad_gain), lane_sum(d_norm)


def gelu_parts(pre):
    upper = 0.5 + 0.5 * lax.erf(pre * (0.5**0.5))
    act = (pre * upper).astype(BF16)
    low = pre.astype(BF16)
    density = jnp.exp2(low * low * BF16(-0.5 / math.log(2))) * BF16(0.3989422804014327)
    return act, upper.astype(BF16) + low * density


def head_rows(feats):
    row = lax.broadcasted_iota(jnp.int32, (16, feats), 0)
    head = lax.div(lax.broadcasted_iota(jnp.int32, (16, feats), 1), HEAD_DIM)
    return jnp.where(row == head, 1.0, 0.0).astype(BF16)


def head_spread(p):
    rows = []
    for h in range(HEADS):
        row = jnp.broadcast_to(p[h : h + 1, :], (16, p.shape[1])).astype(BF16)
        rows += [row] * (HEAD_DIM // 16)
    return jnp.concatenate(rows, axis=0)


def blocks_of(x, left, places):
    zero = jnp.zeros((HEAD_DIM, 128), x.dtype)
    halves = (x[:, :128], x[:, 128:])
    rows = []
    for place in places:
        half = halves[place // 2]
        kept = jnp.where(left, zero, half) if place % 2 else jnp.where(left, half, zero)
        rows.append(jnp.concatenate([zero, kept] if place // 2 else [kept, zero], axis=1))
    return jnp.concatenate(rows, axis=0)


BY_LANES = (0, 1, 2, 3)
BY_ROWS = (0, 2, 1, 3)


def unit_lanes(x, pair, hp):
    cols = slice(128 * pair, 128 * pair + 128)
    first = 128 * hp
    return jnp.concatenate([x[first : first + 64, cols], x[first + 64 : first + 128, cols]], axis=1)


def unit_rows(x, pair, hp):
    dims = slice(128 * hp, 128 * hp + 128)
    first = 128 * pair
    return jnp.concatenate([x[first : first + 64, dims], x[first + 64 : first + 128, dims]], axis=1)


def unit_slot(n):
    return slice(P0 + 64 * (n // 2), P0 + 64 * (n // 2) + 64), slice(256 * (n % 2), 256 * (n % 2) + 256)


def put_unit(ref, base, pair, hp, value):
    cols = slice(128 * pair, 128 * pair + 128)
    first = base + 128 * hp
    ref[first : first + 64, cols] = value[:, :128]
    ref[first + 64 : first + 128, cols] = value[:, 128:]


def spread_vectors(pieces_ref, space, feed, time, last):
    pieces_ref[...] = jnp.zeros_like(pieces_ref)
    starts = (512, 1024, 0)
    sources = [
        (part, first)
        for kind, first in enumerate(starts)
        for part, first in (
            (space, first),
            (feed, first),
            (time, first),
            (last, (0, 512, 1024)[kind]),
        )
    ]
    for z in range(4):
        rows = [part[0:1, first + 128 * z : first + 128 * z + 128] for part, first in sources]
        for part in (feed, last):
            for m in range(4):
                first = 1536 + 512 * z + 128 * m
                rows.append(part[0:1, first : first + 128])
        for r, row in enumerate(rows):
            pieces_ref[8 * z + r // 3, r % 3 : r % 3 + 1, :] = row


def pack(info, pieces, place, vectors=None):
    me, row = info[0], info[1]
    core, cell = lax.rem(me, 2), lax.div(me, 2)

    def step(z, carry):
        for c in range(2):
            for j in range(4):
                side = (core ^ c) * 4 + (cell ^ j)
                base = 0
                for acc_ref, depth in pieces:
                    first = pl.multiple_of((z ^ row) * (8 * depth) + side * depth, 16)
                    for k in range(acc_ref.shape[1] // 512):
                        part = acc_ref[pl.ds(first, depth), 512 * k : 512 * (k + 1)]
                        place(j, c, z, slice(base, base + depth), part.astype(BF16))
                        base += depth
                if vectors is not None:
                    part = vectors[(z ^ row) * 8 + side].astype(BF16)
                    part = jnp.concatenate([part, jnp.zeros((16, 384), BF16)], axis=1)
                    place(j, c, z, slice(base, base + 16), part)
        return carry

    lax.fori_loop(0, 4, step, 0)


def row_sums(acc):
    return lax.dot_general(
        jnp.ones((8, 128), F32), acc, NT, precision=lax.Precision.HIGHEST, preferred_element_type=F32
    )


A2, XHAT2, O2, R1_ROWS = 0, 512, 1024, 1536
C1, XHAT1, ACT0, SLOPE0, R3_ROWS = 0, 512, 1024, 3072, 5120
A0, XHAT0, O0, QKV0, P0, R2_ROWS = 0, 512, 1024, 1536, 3072, 3584


def state_kernel(
    info, own_ref, halo_ref, mask_ref, vec_ref, wqkv_ref, wproj_ref, wup_ref, wdown_ref, *refs, start, items
):
    r1_ref, r2_ref, r3_ref, qkv2_ref, p2_ref, stat_ref, x3_ref, kv_ref, scores_ref, sem = refs[-10:]
    step = pl.program_id(0)
    frame = start + step
    lanes = r1_ref.shape[2]
    feats = wqkv_ref.shape[1]

    def vec(index, size=512):
        return wide(vec_ref[512 * index : 512 * index + size, :], lanes)

    def earlier():
        return pltpu.make_async_copy(
            refs[3].at[pl.ds(0, start), pl.ds(512, 1024)], kv_ref.at[pl.ds(0, start)], sem
        )

    @pl.when(step == 0)
    def _():
        kv_ref[start:] = jnp.zeros_like(kv_ref[start:])
        if start:
            earlier().start()

    x0 = load_frame(own_ref, halo_ref)
    xhat0, rstd0, a0 = norm(x0, vec(0), vec(1))
    r2_ref[0, A0 : A0 + 512, :] = a0
    r2_ref[0, XHAT0 : XHAT0 + 512, :] = xhat0.astype(BF16)
    qkv = mm(wqkv_ref[0], a0, TN).astype(BF16)
    r2_ref[0, QKV0 : QKV0 + 1536, :] = qkv
    keys = qkv[512:1024].T
    left = half_mask((64, 128))
    units = [(pair, hp) for pair in range(lanes // 128) for hp in range(HEADS // 2)]
    for n, (pair, hp) in enumerate(units):
        query = blocks_of(unit_lanes(qkv[:512], pair, hp), left, BY_ROWS)
        scores = mm(unit_rows(keys, pair, hp), query) * SCALE
        scores_ref[n] = jnp.where(mask_ref[pair % mask_ref.shape[0]] > 0.5, scores, NEG)
    for n in range(len(units)):
        scores = scores_ref[n]
        exponent = jnp.exp(scores - jnp.max(scores, axis=0, keepdims=True))
        weights = exponent * (1.0 / jnp.sum(exponent, axis=0, keepdims=True))
        r2_ref[(0, *unit_slot(n))] = weights.astype(BF16)
    for n, (pair, hp) in enumerate(units):
        weights = blocks_of(r2_ref[(0, *unit_slot(n))], left, BY_LANES)
        mixed = mm(unit_lanes(qkv[1024:], pair, hp), weights).astype(BF16)
        put_unit(r2_ref.at[0], O0, pair, hp, mixed)
    x1 = x0 + mm(wproj_ref[0], r2_ref[0, O0 : O0 + 512, :], TN) + vec(2)

    xhat1, rstd1, c1 = norm(x1, vec(3), vec(4))
    r3_ref[0, C1 : C1 + 512, :] = c1
    r3_ref[0, XHAT1 : XHAT1 + 512, :] = xhat1.astype(BF16)
    for k in range(wup_ref.shape[2] // CHUNK):
        pre = mm(wup_ref[0, :, CHUNK * k : CHUNK * (k + 1)], c1, TN)
        pre = pre + wide(vec_ref[512 * 9 + CHUNK * k : 512 * 9 + CHUNK * (k + 1), :], lanes)
        act, slope = gelu_parts(pre)
        r3_ref[0, ACT0 + CHUNK * k : ACT0 + CHUNK * (k + 1), :] = act
        r3_ref[0, SLOPE0 + CHUNK * k : SLOPE0 + CHUNK * (k + 1), :] = slope
    x2 = x1 + vec(5) + mm(wdown_ref[0], r3_ref[0, ACT0:SLOPE0, :], TN)

    xhat2, rstd2, a2 = norm(x2, vec(6), vec(7))
    r1_ref[0, A2 : A2 + 512, :] = a2
    r1_ref[0, XHAT2 : XHAT2 + 512, :] = xhat2.astype(BF16)
    qkv = mm(wqkv_ref[1], a2, TN).astype(BF16)
    qkv2_ref[0] = qkv
    kv_ref[frame] = qkv[512:]
    if start:

        @pl.when(step == 0)
        def _():
            earlier().wait()

    query = qkv[:512] * BF16(SCALE)
    count = kv_ref.shape[0]
    products = jnp.concatenate([query * kv_ref[u, :512, :] for u in range(count)], axis=1)
    products = mm(head_rows(feats), products)
    scores = []
    for u in range(count):
        score = products[:HEADS, lanes * u : lanes * (u + 1)]
        scores.append(jnp.where(u <= frame, score, NEG))
    top = functools.reduce(jnp.maximum, scores)
    exponents = [jnp.exp(s - top) for s in scores]
    scale = 1.0 / sum(exponents)
    o2 = jnp.zeros((feats, lanes), BF16)
    for u in range(count):
        weight = exponents[u] * scale
        p2_ref[0, u] = weight
        o2 = o2 + head_spread(weight) * kv_ref[u, 512:, :]
    r1_ref[0, O2 : O2 + 512, :] = o2
    is_video = item_row([info[2 + i].astype(F32) for i in range(items)], lanes)
    x3_ref[0] = x2 + is_video * (mm(wproj_ref[1], o2, TN) + vec(8))
    stat_ref[0] = jnp.concatenate([rstd0, rstd1, rstd2, jnp.zeros((5, lanes), F32)], axis=0)


def last_kernel(
    info,
    x3_ref,
    cot_own_ref,
    cot_halo_ref,
    vec_ref,
    wup_ref,
    wdown_ref,
    out_own_ref,
    out_halo_ref,
    g3_ref,
    keep_ref,
    send_ref,
    sums_ref,
    acc_up,
    acc_down,
    acc_vec,
    act_ref,
    slope_ref,
    *,
    items,
):
    frame, frames = pl.program_id(0), pl.num_programs(0)
    feats, lanes = g3_ref.shape[1:]

    def vec(index, size=512):
        return wide(vec_ref[512 * index : 512 * index + size, :], lanes)

    @pl.when(frame == 0)
    def _():
        for acc in (acc_up, acc_down, acc_vec):
            acc[...] = jnp.zeros_like(acc)

    counts = [info[2 + items + i] for i in range(items)]
    is_valid = item_row([jnp.where(frame < c, 1.0, 0.0) for c in counts], lanes)
    g4 = load_frame(cot_own_ref, cot_halo_ref) * is_valid
    grad_low = g4.astype(BF16)
    x3 = x3_ref[0]
    xhat3, rstd3, c3 = norm(x3, vec(0), vec(1))
    chunks = [slice(CHUNK * k, CHUNK * (k + 1)) for k in range(wup_ref.shape[2] // CHUNK)]
    for part in chunks:
        pre = mm(wup_ref[0, :, part], c3, TN)
        pre = pre + wide(vec_ref[1536 + part.start : 1536 + part.stop, :], lanes)
        act_ref[part, :], slope_ref[part, :] = gelu_parts(pre)
    x4 = x3 + vec(2) + mm(wdown_ref[0], act_ref[...], TN)
    store_frame(x4 * is_valid, out_own_ref, out_halo_ref)
    for part in chunks:
        d_pre = (mm(wdown_ref[0, part, :], grad_low) * slope_ref[part, :]).astype(BF16)
        slope_ref[part, :] = d_pre
        rows = slice(1536 + part.start, 1536 + part.stop)
        acc_vec[rows, :] += lane_sum(d_pre.astype(F32))
    d_norm = mm(wup_ref[0], slope_ref[...])
    acc_up[...] += mm(c3, slope_ref[...], NT)
    acc_down[...] += mm(act_ref[...], grad_low, NT)
    d_hidden, gain_part, bias_part = norm_back(d_norm, xhat3, rstd3, vec(0))
    acc_vec[0:512, :] += gain_part
    acc_vec[512:1024, :] += bias_part
    acc_vec[1024:1536, :] += lane_sum(g4)
    g3_ref[0] = g4 + d_hidden

    @pl.when(frame == frames - 1)
    def _():
        pack(info, [(acc_up, 16), (acc_down, 64)], core_first(keep_ref, send_ref))
        sums_ref[...] = row_sums(acc_vec[...])


def time_step(t, qkv2_ref, p2_ref, grad_ref, weight_ref, score_ref, dqkv_ref):
    frames, _, lanes = qkv2_ref.shape
    feats = grad_ref.shape[1]
    grad = grad_ref[t]
    products = jnp.concatenate([grad * qkv2_ref[u, 1024:, :] for u in range(t + 1)], axis=1)
    products = mm(head_rows(feats), products)
    weights = [p2_ref[0, u] for u in range(t + 1)]
    d_weights = [products[:HEADS, lanes * u : lanes * (u + 1)] for u in range(t + 1)]
    inner = sum(w * d for w, d in zip(weights, d_weights))
    d_query = jnp.zeros((feats, lanes), BF16)
    for u in range(t + 1):
        d_score = (weights[u] * (d_weights[u] - inner)).astype(BF16).astype(F32)
        score_ref[t, u] = d_score
        weight_ref[t, u] = weights[u]
        d_query = d_query + head_spread(d_score) * qkv2_ref[u, 512:1024, :]
    dqkv_ref[:512, :] = d_query * BF16(SCALE)
    d_key = jnp.zeros((feats, lanes), BF16)
    d_value = jnp.zeros((feats, lanes), BF16)
    for v in range(t, frames):
        d_key = d_key + head_spread(score_ref[v, t]) * qkv2_ref[v, :512, :]
        d_value = d_value + head_spread(weight_ref[v, t]) * grad_ref[v]
    dqkv_ref[512:1024, :] = d_key * BF16(SCALE)
    dqkv_ref[1024:, :] = d_value


def time_kernel(
    info,
    g3_ref,
    r1_ref,
    qkv2_ref,
    p2_ref,
    stat_ref,
    vec_ref,
    wqkv_ref,
    wproj_ref,
    g2_ref,
    keep_ref,
    send_ref,
    sums_ref,
    acc_qkv,
    acc_proj,
    acc_vec,
    grad_ref,
    weight_ref,
    score_ref,
    dqkv_ref,
    *,
    items,
):
    step, frames = pl.program_id(0), pl.num_programs(0)
    frame = frames - 1 - step
    feats, lanes = g2_ref.shape[1:]

    @pl.when(step == 0)
    def _():
        for acc in (acc_qkv, acc_proj, acc_vec):
            acc[...] = jnp.zeros_like(acc)

    g3 = g3_ref[0]
    is_video = item_row([info[2 + i].astype(F32) for i in range(items)], lanes)
    d_attn = (g3 * is_video).astype(BF16)
    acc_proj[...] += mm(r1_ref[0, O2 : O2 + 512, :], d_attn, NT)
    acc_vec[0:512, :] += lane_sum(d_attn.astype(F32))
    grad_ref[frame] = mm(wproj_ref[0], d_attn).astype(BF16)
    for t in range(qkv2_ref.shape[0]):

        @pl.when(frame == t)
        def _():
            time_step(t, qkv2_ref, p2_ref, grad_ref, weight_ref, score_ref, dqkv_ref)

    d_qkv = dqkv_ref[...]
    acc_qkv[...] += mm(r1_ref[0, A2 : A2 + 512, :], d_qkv, NT)
    d_norm = mm(wqkv_ref[0], d_qkv)
    xhat = r1_ref[0, XHAT2 : XHAT2 + 512, :].astype(F32)
    gain = wide(vec_ref[...], lanes)
    d_hidden, gain_part, bias_part = norm_back(d_norm, xhat, stat_ref[0, 2:3, :], gain)
    acc_vec[512:1024, :] += gain_part
    acc_vec[1024:1536, :] += bias_part
    g2_ref[0] = g3 + d_hidden

    @pl.when(step == frames - 1)
    def _():
        pack(info, [(acc_qkv, 16), (acc_proj, 16)], core_first(keep_ref, send_ref))
        sums_ref[...] = row_sums(acc_vec[...])


def feed_kernel(info, g2_ref, r3_ref, stat_ref, vec_ref, wup_ref, wdown_ref, *refs, passes):
    g1_ref, keep_ref, send_ref, sums_ref = refs[passes : passes + 4]
    acc_up, acc_down, acc_vec = refs[-3:]
    step, steps = pl.program_id(0), pl.num_programs(0)
    lanes = g1_ref.shape[2]

    @pl.when(step == 0)
    def _():
        for acc in (acc_up, acc_down, acc_vec):
            acc[...] = jnp.zeros_like(acc)

    g2 = g2_ref[0]
    grad_low = g2.astype(BF16)
    acc_vec[0:512, :] += lane_sum(grad_low.astype(F32))
    c1 = r3_ref[0, C1 : C1 + 512, :]
    d_norm = jnp.zeros(g2.shape, F32)
    size = 1024
    for k in range(wup_ref.shape[2] // size):
        part = slice(size * k, size * (k + 1))
        d_pre = mm(wdown_ref[0, part, :], grad_low)
        d_pre = (d_pre * r3_ref[0, SLOPE0 + size * k : SLOPE0 + size * (k + 1), :]).astype(BF16)
        d_norm = d_norm + mm(wup_ref[0, :, part], d_pre)
        acc_up[:, part] += mm(c1, d_pre, NT)
        acc_down[part, :] += mm(
            r3_ref[0, ACT0 + size * k : ACT0 + size * (k + 1), :], grad_low, NT
        )
        acc_vec[1536 + size * k : 1536 + size * (k + 1), :] += lane_sum(d_pre.astype(F32))
    xhat = r3_ref[0, XHAT1 : XHAT1 + 512, :].astype(F32)
    gain = wide(vec_ref[...], lanes)
    d_hidden, gain_part, bias_part = norm_back(d_norm, xhat, stat_ref[0, 1:2, :], gain)
    acc_vec[512:1024, :] += gain_part
    acc_vec[1024:1536, :] += bias_part
    g1_ref[0] = g2 + d_hidden

    @pl.when(step == steps - 1)
    def _():
        pack(info, [(acc_up, 16), (acc_down, 64)], core_first(keep_ref, send_ref))
        sums_ref[...] = row_sums(acc_vec[...])


def core_first(keep_ref, send_ref):
    def place(j, c, z, rows, value):
        (send_ref if c else keep_ref)[j, z, rows, :] = value

    return place


def space_kernel(info, g1_ref, r2_ref, stat_ref, vec_ref, wqkv_ref, wproj_ref, *refs, first, last, passes):
    *refs, dqkv_ref, scores_ref, slope_ref = refs
    if not first:
        (qkv_in, proj_in, vec_in, _), refs = refs[:4], refs[4:]
    if last:
        (last_sums, time_sums, feed_sums), refs = refs[:3], refs[3:]
    out_own_ref, out_halo_ref, *refs = refs[passes:]
    if last:
        keep_ref, send_ref, *refs = refs
        *refs, vec_pieces = refs[passes:]
    acc_qkv, acc_proj, acc_vec = refs[:3]
    frame = pl.program_id(0)
    frames = pl.num_programs(0)
    lanes = r2_ref.shape[2]

    @pl.when(frame == 0)
    def _():
        for k, acc in enumerate((acc_qkv, acc_proj, acc_vec)):
            acc[...] = jnp.zeros_like(acc) if first else (qkv_in, proj_in, vec_in)[k][...]

    g1 = g1_ref[0]
    d_attn = g1.astype(BF16)
    acc_proj[...] += mm(r2_ref[0, O0 : O0 + 512, :], d_attn, NT)
    acc_vec[0:512, :] += lane_sum(d_attn.astype(F32))
    d_mixed = mm(wproj_ref[0], d_attn).astype(BF16)
    values = r2_ref[0, QKV0 + 1024 : QKV0 + 1536, :].T
    left = half_mask((64, 128))
    units = [(pair, hp) for pair in range(lanes // 128) for hp in range(HEADS // 2)]
    for n, (pair, hp) in enumerate(units):
        grad = blocks_of(unit_lanes(d_mixed, pair, hp), left, BY_ROWS)
        scores_ref[n] = mm(unit_rows(values, pair, hp), grad)
    for n, (pair, hp) in enumerate(units):
        d_weights = scores_ref[n]
        weights = r2_ref[(0, *unit_slot(n))].astype(F32)
        inner = jnp.sum(weights * d_weights, axis=0, keepdims=True)
        slope_ref[n] = (weights * (d_weights - inner)).astype(BF16)
    for n, (pair, hp) in enumerate(units):
        slope = blocks_of(slope_ref[n], left, BY_LANES)
        soft = blocks_of(r2_ref[(0, *unit_slot(n))], left, BY_LANES)
        grad = unit_lanes(d_mixed, pair, hp)
        query = unit_lanes(r2_ref[0, QKV0 : QKV0 + 512, :], pair, hp)
        key = unit_lanes(r2_ref[0, QKV0 + 512 : QKV0 + 1024, :], pair, hp)
        put_unit(dqkv_ref, 0, pair, hp, (mm(key, slope) * SCALE).astype(BF16))
        put_unit(dqkv_ref, 512, pair, hp, (mm(query, slope, NT) * SCALE).astype(BF16))
        put_unit(dqkv_ref, 1024, pair, hp, mm(grad, soft, NT).astype(BF16))
    d_qkv = dqkv_ref[...]
    acc_qkv[...] += mm(r2_ref[0, A0 : A0 + 512, :], d_qkv, NT)
    d_norm = mm(wqkv_ref[0], d_qkv)
    xhat = r2_ref[0, XHAT0 : XHAT0 + 512, :].astype(F32)
    gain = wide(vec_ref[...], lanes)
    d_hidden, gain_part, bias_part = norm_back(d_norm, xhat, stat_ref[0, 0:1, :], gain)
    acc_vec[512:1024, :] += gain_part
    acc_vec[1024:1536, :] += bias_part
    store_frame(g1 + d_hidden, out_own_ref, out_halo_ref)

    if last:

        @pl.when(frame == frames - 1)
        def _():
            spread_vectors(
                vec_pieces, row_sums(acc_vec[...]), feed_sums[...], time_sums[...], last_sums[...]
            )
            place = core_first(keep_ref, send_ref)
            pack(info, [(acc_qkv, 16), (acc_proj, 16)], place, vec_pieces)


def put_rows(out_ref, slot, pieces, base, depth):
    for k in range(out_ref.shape[2] // 512):
        rows = pieces[base + depth * k : base + depth * (k + 1), :]
        out_ref[slot, :, 512 * k : 512 * (k + 1)] = rows.astype(F32)


EARLY_ROWS, LATE_ROWS = 192, 208


def unpack_early_kernel(info, mine_ref, other_ref, up_ref, down_ref, qkv_ref, proj_ref):
    pieces = jnp.where(pl.program_id(0) // 4 == info[0], mine_ref[0], other_ref[0])
    put_rows(up_ref, 0, pieces, 0, 16)
    put_rows(down_ref, 0, pieces, 64, 64)
    put_rows(qkv_ref, 0, pieces, 128, 16)
    put_rows(proj_ref, 0, pieces, 176, 16)


def unpack_late_kernel(info, mine_ref, other_ref, *refs):
    up_ref, down_ref, qkv_ref, proj_ref, gain_ref, bias_ref, outb_ref, upb_ref, vec_ref = refs[-9:]
    place = pl.program_id(0)
    pieces = jnp.where(place // 4 == info[0], mine_ref[0], other_ref[0])
    put_rows(up_ref, 0, pieces, 0, 16)
    put_rows(down_ref, 0, pieces, 64, 64)
    put_rows(qkv_ref, 0, pieces, 128, 16)
    put_rows(proj_ref, 0, pieces, 176, 16)
    vec_ref[place] = pieces[192:208, :128].astype(F32)

    @pl.when(place == 7)
    def _():
        for k, ref in enumerate((gain_ref, bias_ref, outb_ref)):
            for n in range(4):
                r = 4 * k + n
                ref[n : n + 1, :] = vec_ref[r // 3, r % 3 : r % 3 + 1, :]
        for k in range(2):
            for m in range(4):
                r = 12 + 4 * k + m
                upb_ref[k : k + 1, 128 * m : 128 * m + 128] = vec_ref[r // 3, r % 3 : r % 3 + 1, :]


def split_sum_kernel(groups, *refs):
    counts = [(len(g), g[0].shape[0]) for g in groups]
    ins, outs = refs[: sum(c for c, _ in counts)], refs[sum(c for c, _ in counts) :]
    for count, pieces in counts:
        for k in range(pieces):
            total = ins[0][k].astype(F32)
            for ref in ins[1:count]:
                total = total + ref[k].astype(F32)
            outs[k][...] = total.astype(BF16)
        ins, outs = ins[count:], outs[pieces:]


def join_sum_kernel(counts, *refs):
    base = 0
    for count in counts:
        total = refs[0][...].astype(F32)
        for ref in refs[1:count]:
            total = total + ref[...].astype(F32)
        refs[-1][base : base + total.shape[0], :] = total.astype(BF16)
        base += total.shape[0]
        refs = refs[count:]


def stack_kernel(*refs):
    for k, ref in enumerate(refs[:-1]):
        refs[-1][k] = ref[...]


def whole_spec(shape, single=True):
    mode = pl.Buffered(1) if single else None
    return pl.BlockSpec(shape, lambda *_: (0,) * len(shape), pipeline_mode=mode)


def part_spec(shape, index):
    def place(*_):
        return (index,) + (0,) * (len(shape) - 1)

    return pl.BlockSpec((1,) + tuple(shape[1:]), place, pipeline_mode=pl.Buffered(1))


def params(axes, limit=56 * MIB):
    return pltpu.CompilerParams(
        dimension_semantics=("arbitrary",) * axes, vmem_limit_bytes=limit
    )


def cost(flops, moved):
    return pl.CostEstimate(flops=int(flops), bytes_accessed=int(moved), transcendentals=0)


def sds(shape, dtype):
    return jax.ShapeDtypeStruct(shape, dtype)


ANY = pl.BlockSpec(memory_space=pl.ANY)


def run_state(info, start, tokens, halo, mask, vecs, weights, before):
    wqkv, wproj, wup, wdown = weights
    items, frames, grid_rows, cols, feats = tokens.shape
    lanes = items * grid_rows * cols
    half = (items, 1, SHIFT, cols, feats)

    def plane_spec(*shape):
        return pl.BlockSpec((1,) + shape, lambda t, info: (start + t,) + (0,) * len(shape))

    shapes = [
        (R1_ROWS, lanes, BF16),
        (R2_ROWS, lanes, BF16),
        (R3_ROWS, lanes, BF16),
        (3 * feats, lanes, BF16),
        (frames, HEADS, lanes, F32),
        (8, lanes, F32),
        (feats, lanes, F32),
    ]
    operands = [info, tokens, halo, mask, vecs, wqkv, wproj, wup, wdown]
    return pl.pallas_call(
        functools.partial(state_kernel, start=start, items=items),
        grid_spec=pltpu.PrefetchScalarGridSpec(
            num_scalar_prefetch=1,
            grid=(halo.shape[1],),
            in_specs=[
                pl.BlockSpec(half, lambda t, info: (0, start + t, 1, 0, 0)),
                pl.BlockSpec(half, lambda t, info: (0, t, 0, 0, 0)),
                whole_spec(mask.shape),
                whole_spec(vecs.shape),
                whole_spec(wqkv.shape),
                whole_spec(wproj.shape),
                part_spec(wup.shape, 0),
                part_spec(wdown.shape, 0),
            ]
            + [ANY] * len(before),
            out_specs=[plane_spec(*s[:-1]) for s in shapes],
            scratch_shapes=[
                pltpu.VMEM((frames, 2 * feats, lanes), BF16),
                pltpu.VMEM((lanes // 128 * (HEADS // 2), 64, 256), F32),
                pltpu.SemaphoreType.DMA(()),
            ],
        ),
        out_shape=[sds((frames,) + s[:-1], s[-1]) for s in shapes],
        input_output_aliases={len(operands) + k: k for k in range(len(before))},
        compiler_params=params(1, 60 * MIB),
        cost_estimate=cost(4.5e9 * 2 * halo.shape[1], 20e6 * halo.shape[1]),
        name="state",
    )(*operands, *before)


def run_last(info, x3, cotangent, cot_halo, vecs, weights):
    wup, wdown = weights
    items, frames, grid_rows, cols, feats = cotangent.shape
    lanes = x3.shape[2]
    hidden = wup.shape[2]
    half = (items, 1, SHIFT, cols, feats)
    own_spec = pl.BlockSpec(half, lambda t, info: (0, t, 1, 0, 0))
    halo_spec = pl.BlockSpec(half, lambda t, info: (0, t, 0, 0, 0))
    plane = pl.BlockSpec((1, feats, lanes), lambda t, info: (t, 0, 0))
    return pl.pallas_call(
        functools.partial(last_kernel, items=items),
        grid_spec=pltpu.PrefetchScalarGridSpec(
            num_scalar_prefetch=1,
            grid=(frames,),
            in_specs=[
                plane,
                own_spec,
                halo_spec,
                whole_spec(vecs.shape),
                part_spec(wup.shape, 1),
                part_spec(wdown.shape, 1),
            ],
            out_specs=[own_spec, halo_spec, plane]
            + [whole_spec((4, 4, 128, 512))] * 2
            + [whole_spec((8, 3584))],
            scratch_shapes=[
                pltpu.VMEM((feats, hidden), F32),
                pltpu.VMEM((hidden, feats), F32),
                pltpu.VMEM((3584, 128), F32),
                pltpu.VMEM((hidden, lanes), BF16),
                pltpu.VMEM((hidden, lanes), BF16),
            ],
        ),
        out_shape=[
            sds(cotangent.shape, BF16),
            sds(cot_halo.shape, BF16),
            sds((frames, feats, lanes), F32),
        ]
        + [sds((4, 4, 128, 512), BF16)] * 2
        + [sds((8, 3584), F32)],
        compiler_params=params(1, 50 * MIB),
        cost_estimate=cost(32e9 * 1.2, 40e6),
        name="last",
    )(info, x3, cotangent, cot_halo, vecs, wup, wdown)


def run_time(info, g3, r1, qkv2, p2, stats, vecs, weights, items):
    wqkv, wproj = weights
    frames, feats, lanes = g3.shape

    def plane_spec(*shape):
        return pl.BlockSpec(
            (1,) + shape,
            lambda s, info: (frames - 1 - s,) + (0,) * len(shape),
        )

    return pl.pallas_call(
        functools.partial(time_kernel, items=items),
        grid_spec=pltpu.PrefetchScalarGridSpec(
            num_scalar_prefetch=1,
            grid=(frames,),
            in_specs=[
                plane_spec(feats, lanes),
                plane_spec(R1_ROWS, lanes),
                whole_spec(qkv2.shape),
                plane_spec(frames, HEADS, lanes),
                plane_spec(8, lanes),
                whole_spec(vecs.shape),
                part_spec(wqkv.shape, 1),
                part_spec(wproj.shape, 1),
            ],
            out_specs=[
                plane_spec(feats, lanes),
                whole_spec((4, 4, 64, 512)),
                whole_spec((4, 4, 64, 512)),
                whole_spec((8, 1536)),
            ],
            scratch_shapes=[
                pltpu.VMEM((feats, 3 * feats), F32),
                pltpu.VMEM((feats, feats), F32),
                pltpu.VMEM((1536, 128), F32),
                pltpu.VMEM((frames, feats, lanes), BF16),
                pltpu.VMEM((frames, frames, HEADS, lanes), F32),
                pltpu.VMEM((frames, frames, HEADS, lanes), F32),
                pltpu.VMEM((3 * feats, lanes), BF16),
            ],
        ),
        out_shape=[
            sds((frames, feats, lanes), F32),
            sds((4, 4, 64, 512), BF16),
            sds((4, 4, 64, 512), BF16),
            sds((8, 1536), F32),
        ],
        compiler_params=params(1, 50 * MIB),
        cost_estimate=cost(30e9, 40e6),
        name="time",
    )(info, g3, r1, qkv2, p2, stats, vecs, wqkv, wproj)


def run_feed(info, g2, r3, stats, vecs, weights, passes):
    wup, wdown = weights
    planes, feats, lanes = g2.shape
    hidden = wup.shape[2]

    def plane_spec(*shape):
        return pl.BlockSpec((1,) + shape, lambda n, info: (n,) + (0,) * len(shape))

    return pl.pallas_call(
        functools.partial(feed_kernel, passes=len(passes)),
        grid_spec=pltpu.PrefetchScalarGridSpec(
            num_scalar_prefetch=1,
            grid=(planes,),
            in_specs=[
                plane_spec(feats, lanes),
                plane_spec(R3_ROWS, lanes),
                plane_spec(8, lanes),
                whole_spec(vecs.shape),
                part_spec(wup.shape, 0),
                part_spec(wdown.shape, 0),
            ]
            + [ANY] * len(passes),
            out_specs=[
                plane_spec(feats, lanes),
                whole_spec((4, 4, 128, 512)),
                whole_spec((4, 4, 128, 512)),
                whole_spec((8, 3584)),
            ]
            + [ANY] * len(passes),
            scratch_shapes=[
                pltpu.VMEM((feats, hidden), F32),
                pltpu.VMEM((hidden, feats), F32),
                pltpu.VMEM((3584, 128), F32),
            ],
        ),
        out_shape=[
            sds((planes, feats, lanes), F32),
            sds((4, 4, 128, 512), BF16),
            sds((4, 4, 128, 512), BF16),
            sds((8, 3584), F32),
        ]
        + [sds(p.shape, p.dtype) for p in passes],
        input_output_aliases={7 + k: 4 + k for k in range(len(passes))},
        compiler_params=params(1, 44 * MIB),
        cost_estimate=cost(30e9, 40e6),
        name="feed",
    )(info, g2, r3, stats, vecs, wup, wdown, *passes)


def run_space(info, start, count, g1, r2, stats, vecs, weights, shape, before, sums, passes):
    wqkv, wproj = weights
    items, frames, grid_rows, cols, feats = shape
    lanes = g1.shape[2]
    half = (items, 1, SHIFT, cols, feats)
    first, last = start == 0, start + count == frames

    def plane_spec(*tail):
        return pl.BlockSpec(
            (1,) + tail, lambda t, info: (start + t,) + (0,) * len(tail)
        )

    accs = [(feats, 3 * feats), (feats, feats), (1536, 128)]
    halves = [(4, 4, 80, 512), (4, 4, 80, 512)]
    in_specs = [
        plane_spec(feats, lanes),
        plane_spec(R2_ROWS, lanes),
        plane_spec(8, lanes),
        whole_spec(vecs.shape),
        part_spec(wqkv.shape, 0),
        part_spec(wproj.shape, 0),
    ]
    operands = [info, g1, r2, stats, vecs, wqkv, wproj]
    aliases = {}
    if not first:
        in_specs += [whole_spec(a) for a in accs] + [ANY]
        aliases = {len(operands) + 3: 0}
    in_specs += [whole_spec(v.shape) for v in sums]
    base = len(in_specs) + 1
    in_specs += [ANY] * len(passes)
    out_specs = [
        pl.BlockSpec(half, lambda t, info: (0, start + t, 1, 0, 0)),
        pl.BlockSpec(half, lambda t, info: (0, t, 0, 0, 0)),
    ]
    out_shape = [sds(shape, BF16), sds((items, count, SHIFT, cols, feats), BF16)]
    scratch = []
    if last:
        out_specs += [whole_spec(h) for h in halves]
        out_shape += [sds(h, BF16) for h in halves]
        scratch += [pltpu.VMEM(a, F32) for a in accs] + [pltpu.VMEM((32, 16, 128), F32)]
    else:
        out_specs += [whole_spec(a) for a in accs]
        out_shape += [sds(a, F32) for a in accs]
    aliases.update({base + k: len(out_specs) + k for k in range(len(passes))})
    out_specs += [ANY] * len(passes)
    out_shape += [sds(p.shape, p.dtype) for p in passes]
    return pl.pallas_call(
        functools.partial(space_kernel, first=first, last=last, passes=len(passes)),
        grid_spec=pltpu.PrefetchScalarGridSpec(
            num_scalar_prefetch=1,
            grid=(count,),
            in_specs=in_specs,
            out_specs=out_specs,
            scratch_shapes=scratch
            + [
                pltpu.VMEM((3 * feats, lanes), BF16),
                pltpu.VMEM((lanes // 128 * (HEADS // 2), 64, 256), F32),
                pltpu.VMEM((lanes // 128 * (HEADS // 2), 64, 256), BF16),
            ],
        ),
        out_shape=out_shape,
        input_output_aliases=aliases,
        compiler_params=params(1, 44 * MIB),
        cost_estimate=cost(7e9 * 2, 30e6),
        name="space",
    )(*operands, *before, *sums, *passes)


def run_unpack(info, chip, other, outs):
    rows = chip.shape[1]
    slot = 0 if outs else 1

    def out(depth, width):
        return pl.BlockSpec((1, depth, width), lambda q, info: (slot, q, 0))

    def piece(q, info):
        return (lax.rem(q, 4) ^ info[1], 0, 0)

    shapes = [(2, 128, 2048), (2, 512, 512), (2, 128, 1536), (2, 128, 512)]
    specs = [out(16, 2048), out(64, 512), out(16, 1536), out(16, 512)]
    small = [(4, 128), (4, 128), (4, 128), (2, 512)] if outs else []
    return pl.pallas_call(
        unpack_late_kernel if outs else unpack_early_kernel,
        grid_spec=pltpu.PrefetchScalarGridSpec(
            num_scalar_prefetch=1,
            grid=(8,),
            in_specs=[pl.BlockSpec((1, rows, 512), piece)] * 2 + [ANY] * len(outs),
            out_specs=specs + [whole_spec(a) for a in small],
            scratch_shapes=[pltpu.VMEM((8, 16, 128), F32)] if outs else [],
        ),
        out_shape=[sds(a, F32) for a in shapes + small],
        input_output_aliases={3 + k: k for k in range(len(outs))},
        compiler_params=params(1, 16 * MIB),
        cost_estimate=cost(0, 6e6),
        name="unpack",
    )(info, chip, other, *outs)


def split_sum(*groups):
    size = sum(a.size for g in groups for a in g)
    depths = [g[0].shape[-2] for g in groups]
    steps = next(n for n in (5, 4, 1) if all(d % (16 * n) == 0 for d in depths))

    def spec(shape):
        block = shape[:-2] + (shape[-2] // steps, shape[-1])
        return pl.BlockSpec(block, lambda i: (0,) * (len(shape) - 2) + (i, 0))

    ins = [a for g in groups for a in g]
    outs = [g[0].shape[1:] for g in groups for _ in range(g[0].shape[0])]
    flat = pl.pallas_call(
        functools.partial(split_sum_kernel, groups),
        grid=(steps,),
        in_specs=[spec(a.shape) for a in ins],
        out_specs=[spec(o) for o in outs],
        out_shape=[sds(o, BF16) for o in outs],
        compiler_params=params(1, 24 * MIB),
        cost_estimate=cost(size, 3 * size),
        name="split_sum",
    )(*ins)
    result = []
    for g in groups:
        result.append(flat[: g[0].shape[0]])
        flat = flat[g[0].shape[0] :]
    return result


def join_sum(*groups):
    ins = [a for g in groups for a in g]
    rows = sum(g[0].shape[0] for g in groups)
    return pl.pallas_call(
        functools.partial(join_sum_kernel, [len(g) for g in groups]),
        out_shape=sds((rows, 512), BF16),
        compiler_params=params(0, 16 * MIB),
        name="join_sum",
    )(*ins)


def run_stack(*arrays):
    shape = (len(arrays),) + arrays[0].shape
    return pl.pallas_call(
        stack_kernel, out_shape=sds(shape, BF16), compiler_params=params(0, 16 * MIB), name="stack"
    )(*arrays)


def after(values, *others):
    count = len(values)
    return pl.pallas_call(
        lambda *refs: None,
        in_specs=[ANY] * (count + len(others)),
        out_specs=[ANY] * count,
        out_shape=[sds(v.shape, v.dtype) for v in values],
        input_output_aliases={k: k for k in range(count)},
        compiler_params=params(0, 1 * MIB),
        name="after",
    )(*values, *others)


def shift(block, axis, distance):
    size = lax.axis_size(axis)
    return lax.ppermute(block, axis, [(i, (i + distance) % size) for i in range(size)])


def swap(block, axis, bits):
    return lax.ppermute(block, axis, [(i, i ^ bits) for i in range(lax.axis_size(axis))])


def upper_bits(total):
    bit = 8
    while bit < lax.axis_size("dp"):
        total = (total.astype(F32) + swap(total, "dp", bit).astype(F32)).astype(BF16)
        bit *= 2
    return total


def region_label(index, extent):
    return jnp.where(index < extent - WIN, 0, jnp.where(index < extent - SHIFT, 1, 2))


def tile_mask(cols):
    height = lax.axis_size("rows") * WIN
    row_label = region_label(lax.axis_index("rows") * WIN + jnp.arange(WIN), height)
    place = (jnp.arange(WIN) + SHIFT) % WIN
    col_label = region_label(jnp.arange(0, cols, WIN)[:, None] + place, cols)
    label = (row_label[None, :, None] * 3 + col_label[:, None, :]).reshape(-1, WIN * WIN)
    same = (label[:, :, None] == label[:, None, :]).astype(F32)
    pairs = same.reshape(-1, 2, WIN * WIN, WIN * WIN).transpose(0, 2, 1, 3)
    pairs = pairs.reshape(-1, WIN * WIN, 2 * WIN * WIN)
    return jnp.concatenate([pairs, pairs], axis=2)


def gather(mine):
    chip = run_stack(mine, *[swap(mine, "dp", 2 * j) for j in range(1, 4)])
    return chip, swap(chip, "dp", 1)


def on_device(
    tokens,
    video_flag,
    frame_count,
    norm_gain,
    norm_bias,
    w_qkv,
    w_proj,
    w_up,
    w_down,
    out_bias,
    up_bias,
    cotangent,
):
    items, frames, grid_rows, cols, feats = tokens.shape
    place = lax.rem(lax.axis_index("dp"), 8)
    row = lax.axis_index("rows")
    info = jnp.concatenate([jnp.stack([place, row]), video_flag, frame_count]).astype(jnp.int32)
    unpack_info = jnp.stack([lax.rem(place, 2), lax.div(place, 2)]).astype(jnp.int32)

    def column(*parts):
        flat = jnp.concatenate([p.reshape(-1) for p in parts])
        return jnp.broadcast_to(flat[:, None], (flat.shape[0], 128))

    early = (frames - 1) // 2
    halo = shift(tokens[:, :early, :SHIFT], "rows", -1)
    mask = tile_mask(cols)
    state_vecs = column(
        *[v[n] for n in range(3) for v in (norm_gain, norm_bias, out_bias)], up_bias[0]
    )
    last_vecs = column(norm_gain[3], norm_bias[3], out_bias[3], up_bias[1])
    time_vecs = column(norm_gain[2])
    feed_vecs = column(norm_gain[1])
    space_vecs = column(norm_gain[0])
    weights = (w_qkv, w_proj, w_up, w_down)
    (ahead,) = after([tokens[:, early:, :SHIFT]], halo)
    late_halo = shift(ahead, "rows", -1)
    kept = run_state(info, 0, tokens, halo, mask, state_vecs, weights, ())
    (ahead,) = after([cotangent[:, :, :SHIFT]], late_halo)
    cot_halo = shift(ahead, "rows", -1)
    kept = run_state(info, early, tokens, late_halo, mask, state_vecs, weights, kept)
    r1, r2, r3, qkv2, p2, stats, x3 = kept
    out_own, out_halo, g3, keep1, send1, sums1 = run_last(
        info, x3, cotangent, cot_halo, last_vecs, (w_up, w_down)
    )

    def cells(array, *taken):
        return split_sum([array, *taken])[0]

    def halves(array):
        return array.reshape((2, 2) + array.shape[1:])

    out_back = shift(out_halo, "rows", 1)
    core1 = swap(send1, "dp", 1)
    g2, keept, sendt, sumst = run_time(
        info, g3, r1, qkv2, p2, stats, time_vecs, (w_qkv, w_proj), items
    )
    cells1 = cells(keep1, core1)
    layer_out = lax.dynamic_update_slice(out_own, out_back, (0,) * 5)
    (sendt,) = after([sendt], cells1[0], layer_out)

    across1 = [swap(cells1[j], "dp", 2 * j) for j in range(1, 4)]
    coret = swap(sendt, "dp", 1)
    g1, keep0, send0, sums0, mine1, layer_out = run_feed(
        info, g2, r3, stats, feed_vecs, (w_up, w_down), [cells1[0], layer_out]
    )
    rows1, cellst = split_sum([halves(mine1), *[halves(a) for a in across1]], [keept, coret])
    (send0,) = after([send0], rows1[0], cellst[0])

    along1 = swap(rows1[1], "rows", 2)
    acrosst = [swap(cellst[j], "dp", 2 * j) for j in range(1, 4)]
    core0 = swap(send0, "dp", 1)
    grad_own, back0, *accs, mine1, minet = run_space(
        info, 0, early, g1, r2, stats, space_vecs, (w_qkv, w_proj), tokens.shape, (), (),
        [rows1[0], cellst[0]],
    )
    rows1, rowst, cells0 = split_sum(
        [mine1, along1], [halves(minet), *[halves(a) for a in acrosst]], [keep0, core0]
    )
    (back0,) = after([back0], rows1[0], rowst[0], cells0[0])

    alongt = swap(rowst[1], "rows", 2)
    across0 = [swap(cells0[j], "dp", 2 * j) for j in range(1, 4)]
    backs = [shift(back0, "rows", 1)]
    grad_own, back1, keeps, sends, mine1, minet, mine0 = run_space(
        info, early, frames - early, g1, r2, stats, space_vecs, (w_qkv, w_proj), tokens.shape,
        accs + [grad_own], (sums1, sumst, sums0), [rows1[0], rowst[0], cells0[0]],
    )
    rowst, rows0 = split_sum([minet, alongt], [mine0, *across0])
    grad_tokens = lax.dynamic_update_slice(grad_own, backs[0], (0, 0, 0, 0, 0))
    sends, back1, near1 = after([sends, back1, rows1[1]], rowst[0], rows0[0], grad_tokens)

    cores = swap(sends, "dp", 1)
    along0 = [swap(rows0[z], "rows", z) for z in range(1, 4)]
    near1 = swap(near1, "rows", 1)
    neart = swap(rowst[1], "rows", 1)
    cellss = cells(keeps, cores)
    acrosss = [swap(cellss[j], "dp", 2 * j) for j in range(1, 4)]
    sums_early = upper_bits(join_sum([mine1, near1], [rowst[0], neart]))
    early_chip, early_other = gather(sums_early)
    rowss = cells(cellss[0], *acrosss)
    back1 = shift(back1, "rows", 1)
    grad_tokens = lax.dynamic_update_slice(grad_tokens, back1, (0, early, 0, 0, 0))
    alongs = [swap(rowss[z], "rows", z) for z in range(1, 4)]
    outs = run_unpack(unpack_info, early_chip, early_other, ())
    along0[0], grad_tokens = after([along0[0], grad_tokens])
    late = join_sum([rows0[0], *along0], [rowss[0], *alongs])
    late_chip, late_other = gather(upper_bits(late))
    up, down, qkv, proj, gain, bias, outb, upb = run_unpack(
        unpack_info, late_chip, late_other, outs
    )
    return layer_out, grad_tokens, gain, bias, qkv, proj, up, down, outb, upb


def solution(mesh):
    split = P("dp", None, "rows", None, None)
    in_specs = (split, P("dp"), P("dp")) + (P(),) * 8 + (split,)
    out_specs = (
        split,
        split,
        P(None, "rows"),
        P(None, "rows"),
        P(None, "rows", None),
        P(None, "rows", None),
        P(None, "rows", None),
        P(None, "rows", None),
        P(None, "rows"),
        P(None, "rows"),
    )
    return jax.shard_map(
        on_device, mesh=mesh, in_specs=in_specs, out_specs=out_specs, check_vma=False
    )
```

```python
import functools
import math

import jax
import jax.numpy as jnp
from jax import lax
from jax.experimental import pallas as pl
from jax.experimental.pallas import tpu as pltpu
from jax.sharding import PartitionSpec as P

HEADS = 8
HEAD_DIM = 64
WIN = 8
SHIFT = 4
EPS = 1e-05
NEG = -1e30
SCALE = HEAD_DIM ** (-0.5)
BF16 = jnp.bfloat16
F32 = jnp.float32
NN = (((1,), (0,)), ((), ()))
NT = (((1,), (1,)), ((), ()))
TN = (((0,), (0,)), ((), ()))
CHUNK = 512
MIB = 1 << 20


def mm(left, right, dims=NN):
    return lax.dot_general(left, right, dims, preferred_element_type=F32)


def wide(column, lanes):
    return jnp.concatenate([column] * (lanes // column.shape[1]), axis=1)


def lane_sum(x):
    total = x[:, :128]
    for k in range(1, x.shape[1] // 128):
        total = total + x[:, 128 * k : 128 * (k + 1)]
    return total


def half_mask(shape):
    return lax.rem(lax.broadcasted_iota(jnp.int32, shape, len(shape) - 1), 128) < 64


def load_frame(own_ref, halo_ref):
    items = []
    for i in range(own_ref.shape[0]):
        grid = jnp.concatenate([own_ref[i, 0], halo_ref[i, 0]], axis=0).astype(F32)
        rows, cols, feats = grid.shape
        blocks = grid.reshape(rows, cols // WIN, WIN, feats)
        after = jnp.concatenate([blocks[:, 1:], blocks[:, :1]], axis=1)
        first = lax.broadcasted_iota(jnp.int32, blocks.shape, 2) < SHIFT
        tiles = jnp.where(first, after, blocks).transpose(1, 0, 2, 3)
        items.append(tiles.reshape(rows * cols, feats).astype(BF16).T)
    return jnp.concatenate(items, axis=1).astype(F32)


def store_frame(value, own_ref, halo_ref):
    count, _, half, cols, feats = own_ref.shape
    rows = 2 * half
    for i in range(count):
        part = value[:, rows * cols * i : rows * cols * (i + 1)]
        flat = part.astype(BF16).T.astype(F32)
        tiles = flat.reshape(cols // WIN, rows, WIN, feats).transpose(1, 0, 2, 3)
        before = jnp.concatenate([tiles[:, -1:], tiles[:, :-1]], axis=1)
        first = lax.broadcasted_iota(jnp.int32, tiles.shape, 2) < SHIFT
        grid = jnp.where(first, before, tiles).reshape(rows, cols, feats).astype(BF16)
        own_ref[i, 0] = grid[:half]
        halo_ref[i, 0] = grid[half:]


def item_row(values, lanes):
    size = lanes // len(values)
    return jnp.concatenate([jnp.full((1, size), v, F32) for v in values], axis=1)


def norm(x, gain, bias):
    center = x - jnp.mean(x, axis=0, keepdims=True)
    spread = jnp.mean(center * center, axis=0, keepdims=True)
    rstd = lax.rsqrt(spread + EPS)
    xhat = center * rstd
    return xhat, rstd, (xhat * gain + bias).astype(BF16)


def norm_back(d_norm, xhat, rstd, gain):
    grad_gain = d_norm * xhat
    e_mean = jnp.mean(d_norm * gain, axis=0, keepdims=True)
    x_mean = jnp.mean(grad_gain * gain, axis=0, keepdims=True)
    d_hidden = (d_norm * gain - e_mean - xhat * x_mean) * rstd
    return d_hidden, lane_sum(grad_gain), lane_sum(d_norm)


def gelu_parts(pre):
    upper = 0.5 + 0.5 * lax.erf(pre * (0.5**0.5))
    act = (pre * upper).astype(BF16)
    low = pre.astype(BF16)
    density = jnp.exp2(low * low * BF16(-0.5 / math.log(2))) * BF16(0.3989422804014327)
    return act, upper.astype(BF16) + low * density


def head_rows(feats):
    row = lax.broadcasted_iota(jnp.int32, (16, feats), 0)
    head = lax.div(lax.broadcasted_iota(jnp.int32, (16, feats), 1), HEAD_DIM)
    return jnp.where(row == head, 1.0, 0.0).astype(BF16)


def head_spread(p):
    rows = []
    for h in range(HEADS):
        row = jnp.broadcast_to(p[h : h + 1, :], (16, p.shape[1])).astype(BF16)
        rows += [row] * (HEAD_DIM // 16)
    return jnp.concatenate(rows, axis=0)


def blocks_of(x, left, places):
    zero = jnp.zeros((HEAD_DIM, 128), x.dtype)
    halves = (x[:, :128], x[:, 128:])
    rows = []
    for place in places:
        half = halves[place // 2]
        kept = jnp.where(left, zero, half) if place % 2 else jnp.where(left, half, zero)
        rows.append(jnp.concatenate([zero, kept] if place // 2 else [kept, zero], axis=1))
    return jnp.concatenate(rows, axis=0)


BY_LANES = (0, 1, 2, 3)
BY_ROWS = (0, 2, 1, 3)


def unit_lanes(x, pair, hp):
    cols = slice(128 * pair, 128 * pair + 128)
    first = 128 * hp
    return jnp.concatenate([x[first : first + 64, cols], x[first + 64 : first + 128, cols]], axis=1)


def unit_rows(x, pair, hp):
    dims = slice(128 * hp, 128 * hp + 128)
    first = 128 * pair
    return jnp.concatenate([x[first : first + 64, dims], x[first + 64 : first + 128, dims]], axis=1)


def unit_slot(n):
    return slice(P0 + 64 * (n // 2), P0 + 64 * (n // 2) + 64), slice(256 * (n % 2), 256 * (n % 2) + 256)


def put_unit(ref, base, pair, hp, value):
    cols = slice(128 * pair, 128 * pair + 128)
    first = base + 128 * hp
    ref[first : first + 64, cols] = value[:, :128]
    ref[first + 64 : first + 128, cols] = value[:, 128:]


def spread_vectors(pieces_ref, space, feed, time, last):
    pieces_ref[...] = jnp.zeros_like(pieces_ref)
    starts = (512, 1024, 0)
    sources = [
        (part, first)
        for kind, first in enumerate(starts)
        for part, first in (
            (space, first),
            (feed, first),
            (time, first),
            (last, (0, 512, 1024)[kind]),
        )
    ]
    for z in range(4):
        rows = [part[0:1, first + 128 * z : first + 128 * z + 128] for part, first in sources]
        for part in (feed, last):
            for m in range(4):
                first = 1536 + 512 * z + 128 * m
                rows.append(part[0:1, first : first + 128])
        for r, row in enumerate(rows):
            pieces_ref[8 * z + r // 3, r % 3 : r % 3 + 1, :] = row


def pack(info, pieces, place, vectors=None):
    me, row = info[0], info[1]
    core, cell = lax.rem(me, 2), lax.div(me, 2)

    def step(z, carry):
        for c in range(2):
            for j in range(4):
                side = (core ^ c) * 4 + (cell ^ j)
                base = 0
                for acc_ref, depth in pieces:
                    first = pl.multiple_of((z ^ row) * (8 * depth) + side * depth, 16)
                    for k in range(acc_ref.shape[1] // 512):
                        part = acc_ref[pl.ds(first, depth), 512 * k : 512 * (k + 1)]
                        place(j, c, z, slice(base, base + depth), part.astype(BF16))
                        base += depth
                if vectors is not None:
                    part = vectors[(z ^ row) * 8 + side].astype(BF16)
                    part = jnp.concatenate([part, jnp.zeros((16, 384), BF16)], axis=1)
                    place(j, c, z, slice(base, base + 16), part)
        return carry

    lax.fori_loop(0, 4, step, 0)


def row_sums(acc):
    return lax.dot_general(
        jnp.ones((8, 128), F32), acc, NT, precision=lax.Precision.HIGHEST, preferred_element_type=F32
    )


A2, XHAT2, O2, R1_ROWS = 0, 512, 1024, 1536
C1, XHAT1, ACT0, SLOPE0, R3_ROWS = 0, 512, 1024, 3072, 5120
A0, XHAT0, O0, QKV0, P0, R2_ROWS = 0, 512, 1024, 1536, 3072, 3584


def state_kernel(
    info, own_ref, halo_ref, mask_ref, vec_ref, wqkv_ref, wproj_ref, wup_ref, wdown_ref, *refs, start, items
):
    r1_ref, r2_ref, r3_ref, qkv2_ref, p2_ref, stat_ref, x3_ref, kv_ref, scores_ref, sem = refs[-10:]
    step = pl.program_id(0)
    frame = start + step
    lanes = r1_ref.shape[2]
    feats = wqkv_ref.shape[1]

    def vec(index, size=512):
        return wide(vec_ref[512 * index : 512 * index + size, :], lanes)

    def earlier():
        return pltpu.make_async_copy(
            refs[3].at[pl.ds(0, start), pl.ds(512, 1024)], kv_ref.at[pl.ds(0, start)], sem
        )

    @pl.when(step == 0)
    def _():
        kv_ref[start:] = jnp.zeros_like(kv_ref[start:])
        if start:
            earlier().start()

    x0 = load_frame(own_ref, halo_ref)
    xhat0, rstd0, a0 = norm(x0, vec(0), vec(1))
    r2_ref[0, A0 : A0 + 512, :] = a0
    r2_ref[0, XHAT0 : XHAT0 + 512, :] = xhat0.astype(BF16)
    qkv = mm(wqkv_ref[0], a0, TN).astype(BF16)
    r2_ref[0, QKV0 : QKV0 + 1536, :] = qkv
    keys = qkv[512:1024].T
    left = half_mask((64, 128))
    units = [(pair, hp) for pair in range(lanes // 128) for hp in range(HEADS // 2)]
    for n, (pair, hp) in enumerate(units):
        query = blocks_of(unit_lanes(qkv[:512], pair, hp), left, BY_ROWS)
        scores = mm(unit_rows(keys, pair, hp), query) * SCALE
        scores_ref[n] = jnp.where(mask_ref[pair % mask_ref.shape[0]] > 0.5, scores, NEG)
    for n in range(len(units)):
        scores = scores_ref[n]
        exponent = jnp.exp(scores - jnp.max(scores, axis=0, keepdims=True))
        weights = exponent * (1.0 / jnp.sum(exponent, axis=0, keepdims=True))
        r2_ref[(0, *unit_slot(n))] = weights.astype(BF16)
    for n, (pair, hp) in enumerate(units):
        weights = blocks_of(r2_ref[(0, *unit_slot(n))], left, BY_LANES)
        mixed = mm(unit_lanes(qkv[1024:], pair, hp), weights).astype(BF16)
        put_unit(r2_ref.at[0], O0, pair, hp, mixed)
    x1 = x0 + mm(wproj_ref[0], r2_ref[0, O0 : O0 + 512, :], TN) + vec(2)

    xhat1, rstd1, c1 = norm(x1, vec(3), vec(4))
    r3_ref[0, C1 : C1 + 512, :] = c1
    r3_ref[0, XHAT1 : XHAT1 + 512, :] = xhat1.astype(BF16)
    for k in range(wup_ref.shape[2] // CHUNK):
        pre = mm(wup_ref[0, :, CHUNK * k : CHUNK * (k + 1)], c1, TN)
        pre = pre + wide(vec_ref[512 * 9 + CHUNK * k : 512 * 9 + CHUNK * (k + 1), :], lanes)
        act, slope = gelu_parts(pre)
        r3_ref[0, ACT0 + CHUNK * k : ACT0 + CHUNK * (k + 1), :] = act
        r3_ref[0, SLOPE0 + CHUNK * k : SLOPE0 + CHUNK * (k + 1), :] = slope
    x2 = x1 + vec(5) + mm(wdown_ref[0], r3_ref[0, ACT0:SLOPE0, :], TN)

    xhat2, rstd2, a2 = norm(x2, vec(6), vec(7))
    r1_ref[0, A2 : A2 + 512, :] = a2
    r1_ref[0, XHAT2 : XHAT2 + 512, :] = xhat2.astype(BF16)
    qkv = mm(wqkv_ref[1], a2, TN).astype(BF16)
    qkv2_ref[0] = qkv
    kv_ref[frame] = qkv[512:]
    if start:

        @pl.when(step == 0)
        def _():
            earlier().wait()

    query = qkv[:512] * BF16(SCALE)
    count = kv_ref.shape[0]
    products = jnp.concatenate([query * kv_ref[u, :512, :] for u in range(count)], axis=1)
    products = mm(head_rows(feats), products)
    scores = []
    for u in range(count):
        score = products[:HEADS, lanes * u : lanes * (u + 1)]
        scores.append(jnp.where(u <= frame, score, NEG))
    top = functools.reduce(jnp.maximum, scores)
    exponents = [jnp.exp(s - top) for s in scores]
    scale = 1.0 / sum(exponents)
    o2 = jnp.zeros((feats, lanes), BF16)
    for u in range(count):
        weight = exponents[u] * scale
        p2_ref[0, u] = weight
        o2 = o2 + head_spread(weight) * kv_ref[u, 512:, :]
    r1_ref[0, O2 : O2 + 512, :] = o2
    is_video = item_row([info[2 + i].astype(F32) for i in range(items)], lanes)
    x3_ref[0] = x2 + is_video * (mm(wproj_ref[1], o2, TN) + vec(8))
    stat_ref[0] = jnp.concatenate([rstd0, rstd1, rstd2, jnp.zeros((5, lanes), F32)], axis=0)


def last_kernel(
    info,
    x3_ref,
    cot_own_ref,
    cot_halo_ref,
    vec_ref,
    wup_ref,
    wdown_ref,
    out_own_ref,
    out_halo_ref,
    g3_ref,
    keep_ref,
    send_ref,
    sums_ref,
    acc_up,
    acc_down,
    acc_vec,
    act_ref,
    slope_ref,
    *,
    items,
):
    frame, frames = pl.program_id(0), pl.num_programs(0)
    feats, lanes = g3_ref.shape[1:]

    def vec(index, size=512):
        return wide(vec_ref[512 * index : 512 * index + size, :], lanes)

    @pl.when(frame == 0)
    def _():
        for acc in (acc_up, acc_down, acc_vec):
            acc[...] = jnp.zeros_like(acc)

    counts = [info[2 + items + i] for i in range(items)]
    is_valid = item_row([jnp.where(frame < c, 1.0, 0.0) for c in counts], lanes)
    g4 = load_frame(cot_own_ref, cot_halo_ref) * is_valid
    grad_low = g4.astype(BF16)
    x3 = x3_ref[0]
    xhat3, rstd3, c3 = norm(x3, vec(0), vec(1))
    chunks = [slice(CHUNK * k, CHUNK * (k + 1)) for k in range(wup_ref.shape[2] // CHUNK)]
    for part in chunks:
        pre = mm(wup_ref[0, :, part], c3, TN)
        pre = pre + wide(vec_ref[1536 + part.start : 1536 + part.stop, :], lanes)
        act_ref[part, :], slope_ref[part, :] = gelu_parts(pre)
    x4 = x3 + vec(2) + mm(wdown_ref[0], act_ref[...], TN)
    store_frame(x4 * is_valid, out_own_ref, out_halo_ref)
    for part in chunks:
        d_pre = (mm(wdown_ref[0, part, :], grad_low) * slope_ref[part, :]).astype(BF16)
        slope_ref[part, :] = d_pre
        rows = slice(1536 + part.start, 1536 + part.stop)
        acc_vec[rows, :] += lane_sum(d_pre.astype(F32))
    d_norm = mm(wup_ref[0], slope_ref[...])
    acc_up[...] += mm(c3, slope_ref[...], NT)
    acc_down[...] += mm(act_ref[...], grad_low, NT)
    d_hidden, gain_part, bias_part = norm_back(d_norm, xhat3, rstd3, vec(0))
    acc_vec[0:512, :] += gain_part
    acc_vec[512:1024, :] += bias_part
    acc_vec[1024:1536, :] += lane_sum(g4)
    g3_ref[0] = g4 + d_hidden

    @pl.when(frame == frames - 1)
    def _():
        pack(info, [(acc_up, 16), (acc_down, 64)], core_first(keep_ref, send_ref))
        sums_ref[...] = row_sums(acc_vec[...])


def time_step(t, qkv2_ref, p2_ref, grad_ref, weight_ref, score_ref, dqkv_ref):
    frames, _, lanes = qkv2_ref.shape
    feats = grad_ref.shape[1]
    grad = grad_ref[t]
    products = jnp.concatenate([grad * qkv2_ref[u, 1024:, :] for u in range(t + 1)], axis=1)
    products = mm(head_rows(feats), products)
    weights = [p2_ref[0, u] for u in range(t + 1)]
    d_weights = [products[:HEADS, lanes * u : lanes * (u + 1)] for u in range(t + 1)]
    inner = sum(w * d for w, d in zip(weights, d_weights))
    d_query = jnp.zeros((feats, lanes), BF16)
    for u in range(t + 1):
        d_score = (weights[u] * (d_weights[u] - inner)).astype(BF16).astype(F32)
        score_ref[t, u] = d_score
        weight_ref[t, u] = weights[u]
        d_query = d_query + head_spread(d_score) * qkv2_ref[u, 512:1024, :]
    dqkv_ref[:512, :] = d_query * BF16(SCALE)
    d_key = jnp.zeros((feats, lanes), BF16)
    d_value = jnp.zeros((feats, lanes), BF16)
    for v in range(t, frames):
        d_key = d_key + head_spread(score_ref[v, t]) * qkv2_ref[v, :512, :]
        d_value = d_value + head_spread(weight_ref[v, t]) * grad_ref[v]
    dqkv_ref[512:1024, :] = d_key * BF16(SCALE)
    dqkv_ref[1024:, :] = d_value


def time_kernel(
    info,
    g3_ref,
    r1_ref,
    qkv2_ref,
    p2_ref,
    stat_ref,
    vec_ref,
    wqkv_ref,
    wproj_ref,
    g2_ref,
    keep_ref,
    send_ref,
    sums_ref,
    acc_qkv,
    acc_proj,
    acc_vec,
    grad_ref,
    weight_ref,
    score_ref,
    dqkv_ref,
    *,
    items,
):
    step, frames = pl.program_id(0), pl.num_programs(0)
    frame = frames - 1 - step
    feats, lanes = g2_ref.shape[1:]

    @pl.when(step == 0)
    def _():
        for acc in (acc_qkv, acc_proj, acc_vec):
            acc[...] = jnp.zeros_like(acc)

    g3 = g3_ref[0]
    is_video = item_row([info[2 + i].astype(F32) for i in range(items)], lanes)
    d_attn = (g3 * is_video).astype(BF16)
    acc_proj[...] += mm(r1_ref[0, O2 : O2 + 512, :], d_attn, NT)
    acc_vec[0:512, :] += lane_sum(d_attn.astype(F32))
    grad_ref[frame] = mm(wproj_ref[0], d_attn).astype(BF16)
    for t in range(qkv2_ref.shape[0]):

        @pl.when(frame == t)
        def _():
            time_step(t, qkv2_ref, p2_ref, grad_ref, weight_ref, score_ref, dqkv_ref)

    d_qkv = dqkv_ref[...]
    acc_qkv[...] += mm(r1_ref[0, A2 : A2 + 512, :], d_qkv, NT)
    d_norm = mm(wqkv_ref[0], d_qkv)
    xhat = r1_ref[0, XHAT2 : XHAT2 + 512, :].astype(F32)
    gain = wide(vec_ref[...], lanes)
    d_hidden, gain_part, bias_part = norm_back(d_norm, xhat, stat_ref[0, 2:3, :], gain)
    acc_vec[512:1024, :] += gain_part
    acc_vec[1024:1536, :] += bias_part
    g2_ref[0] = g3 + d_hidden

    @pl.when(step == frames - 1)
    def _():
        pack(info, [(acc_qkv, 16), (acc_proj, 16)], core_first(keep_ref, send_ref))
        sums_ref[...] = row_sums(acc_vec[...])


def feed_kernel(info, g2_ref, r3_ref, stat_ref, vec_ref, wup_ref, wdown_ref, *refs, passes):
    back_ref, refs = refs[passes], refs[passes + 1 :]
    g1_ref, keep_ref, send_ref, sums_ref = refs[:4]
    acc_up, acc_down, acc_vec, sem = refs[-4:]
    own_ref = refs[3 + passes]
    put_back = pltpu.make_async_copy(back_ref, own_ref.at[:, :, : back_ref.shape[2]], sem)
    step, steps = pl.program_id(0), pl.num_programs(0)
    lanes = g1_ref.shape[2]

    @pl.when(step == 0)
    def _():
        put_back.start()
        for acc in (acc_up, acc_down, acc_vec):
            acc[...] = jnp.zeros_like(acc)

    g2 = g2_ref[0]
    grad_low = g2.astype(BF16)
    acc_vec[0:512, :] += lane_sum(grad_low.astype(F32))
    c1 = r3_ref[0, C1 : C1 + 512, :]
    d_norm = jnp.zeros(g2.shape, F32)
    size = 1024
    for k in range(wup_ref.shape[2] // size):
        part = slice(size * k, size * (k + 1))
        d_pre = mm(wdown_ref[0, part, :], grad_low)
        d_pre = (d_pre * r3_ref[0, SLOPE0 + size * k : SLOPE0 + size * (k + 1), :]).astype(BF16)
        d_norm = d_norm + mm(wup_ref[0, :, part], d_pre)
        acc_up[:, part] += mm(c1, d_pre, NT)
        acc_down[part, :] += mm(
            r3_ref[0, ACT0 + size * k : ACT0 + size * (k + 1), :], grad_low, NT
        )
        acc_vec[1536 + size * k : 1536 + size * (k + 1), :] += lane_sum(d_pre.astype(F32))
    xhat = r3_ref[0, XHAT1 : XHAT1 + 512, :].astype(F32)
    gain = wide(vec_ref[...], lanes)
    d_hidden, gain_part, bias_part = norm_back(d_norm, xhat, stat_ref[0, 1:2, :], gain)
    acc_vec[512:1024, :] += gain_part
    acc_vec[1024:1536, :] += bias_part
    g1_ref[0] = g2 + d_hidden

    @pl.when(step == steps - 1)
    def _():
        put_back.wait()
        pack(info, [(acc_up, 16), (acc_down, 64)], core_first(keep_ref, send_ref))
        sums_ref[...] = row_sums(acc_vec[...])


def core_first(keep_ref, send_ref):
    def place(j, c, z, rows, value):
        (send_ref if c else keep_ref)[j, z, rows, :] = value

    return place


def space_kernel(info, g1_ref, r2_ref, stat_ref, vec_ref, wqkv_ref, wproj_ref, *refs, first, last, passes):
    *refs, dqkv_ref, scores_ref, slope_ref = refs
    if not first:
        (qkv_in, proj_in, vec_in, _), refs = refs[:4], refs[4:]
    if last:
        (last_sums, time_sums, feed_sums), refs = refs[:3], refs[3:]
    out_own_ref, out_halo_ref, *refs = refs[passes:]
    if last:
        keep_ref, send_ref, *refs = refs
        *refs, vec_pieces = refs[passes:]
    acc_qkv, acc_proj, acc_vec = refs[:3]
    frame = pl.program_id(0)
    frames = pl.num_programs(0)
    lanes = r2_ref.shape[2]

    @pl.when(frame == 0)
    def _():
        for k, acc in enumerate((acc_qkv, acc_proj, acc_vec)):
            acc[...] = jnp.zeros_like(acc) if first else (qkv_in, proj_in, vec_in)[k][...]

    g1 = g1_ref[0]
    d_attn = g1.astype(BF16)
    acc_proj[...] += mm(r2_ref[0, O0 : O0 + 512, :], d_attn, NT)
    acc_vec[0:512, :] += lane_sum(d_attn.astype(F32))
    d_mixed = mm(wproj_ref[0], d_attn).astype(BF16)
    values = r2_ref[0, QKV0 + 1024 : QKV0 + 1536, :].T
    left = half_mask((64, 128))
    units = [(pair, hp) for pair in range(lanes // 128) for hp in range(HEADS // 2)]
    for n, (pair, hp) in enumerate(units):
        grad = blocks_of(unit_lanes(d_mixed, pair, hp), left, BY_ROWS)
        scores_ref[n] = mm(unit_rows(values, pair, hp), grad)
    for n, (pair, hp) in enumerate(units):
        d_weights = scores_ref[n]
        weights = r2_ref[(0, *unit_slot(n))].astype(F32)
        inner = jnp.sum(weights * d_weights, axis=0, keepdims=True)
        slope_ref[n] = (weights * (d_weights - inner)).astype(BF16)
    for n, (pair, hp) in enumerate(units):
        slope = blocks_of(slope_ref[n], left, BY_LANES)
        soft = blocks_of(r2_ref[(0, *unit_slot(n))], left, BY_LANES)
        grad = unit_lanes(d_mixed, pair, hp)
        query = unit_lanes(r2_ref[0, QKV0 : QKV0 + 512, :], pair, hp)
        key = unit_lanes(r2_ref[0, QKV0 + 512 : QKV0 + 1024, :], pair, hp)
        put_unit(dqkv_ref, 0, pair, hp, (mm(key, slope) * SCALE).astype(BF16))
        put_unit(dqkv_ref, 512, pair, hp, (mm(query, slope, NT) * SCALE).astype(BF16))
        put_unit(dqkv_ref, 1024, pair, hp, mm(grad, soft, NT).astype(BF16))
    d_qkv = dqkv_ref[...]
    acc_qkv[...] += mm(r2_ref[0, A0 : A0 + 512, :], d_qkv, NT)
    d_norm = mm(wqkv_ref[0], d_qkv)
    xhat = r2_ref[0, XHAT0 : XHAT0 + 512, :].astype(F32)
    gain = wide(vec_ref[...], lanes)
    d_hidden, gain_part, bias_part = norm_back(d_norm, xhat, stat_ref[0, 0:1, :], gain)
    acc_vec[512:1024, :] += gain_part
    acc_vec[1024:1536, :] += bias_part
    store_frame(g1 + d_hidden, out_own_ref, out_halo_ref)

    if last:

        @pl.when(frame == frames - 1)
        def _():
            spread_vectors(
                vec_pieces, row_sums(acc_vec[...]), feed_sums[...], time_sums[...], last_sums[...]
            )
            place = core_first(keep_ref, send_ref)
            pack(info, [(acc_qkv, 16), (acc_proj, 16)], place, vec_pieces)


PARTS = ((0, 16), (64, 64), (128, 16), (176, 16))
VECTOR_ROWS = 192


def unpack_kernel(info, mine_ref, other_ref, *refs, vectors):
    outs = refs[-9:-5] if vectors else refs
    for q in range(8):
        place = (q % 4) ^ info[1]
        own = info[0] == q // 4
        for out_ref, (base, depth) in zip(outs, PARTS):
            for k in range(out_ref.shape[2] // 512):
                rows = slice(base + depth * k, base + depth * (k + 1))
                value = jnp.where(own, mine_ref[place, rows, :], other_ref[place, rows, :])
                out_ref[0, depth * q : depth * (q + 1), 512 * k : 512 * (k + 1)] = value.astype(F32)
        if vectors:
            rows = slice(VECTOR_ROWS, VECTOR_ROWS + 16)
            value = jnp.where(own, mine_ref[place, rows, :128], other_ref[place, rows, :128])
            refs[-1][q] = value.astype(F32)
    if vectors:
        *small, upb_ref, vec_ref = refs[-5:]
        for k, ref in enumerate(small):
            for n in range(4):
                r = 4 * k + n
                ref[n : n + 1, :] = vec_ref[r // 3, r % 3 : r % 3 + 1, :]
        for k in range(2):
            for m in range(4):
                r = 12 + 4 * k + m
                upb_ref[k : k + 1, 128 * m : 128 * m + 128] = vec_ref[r // 3, r % 3 : r % 3 + 1, :]


def near_kernel(far_ref, near_ref, keep_ref, taken_ref, keep_out, send_out):
    depth = far_ref.shape[0]
    for k, (early, out) in enumerate(((far_ref, keep_out), (near_ref, send_out))):
        out[:depth, :] = early[...]
        out[depth:, :] = (keep_ref[k].astype(F32) + taken_ref[k].astype(F32)).astype(BF16)


def split_sum_kernel(groups, *refs):
    counts = [(len(g), g[0].shape[0]) for g in groups]
    ins, outs = refs[: sum(c for c, _ in counts)], refs[sum(c for c, _ in counts) :]
    for count, pieces in counts:
        for k in range(pieces):
            total = ins[0][k].astype(F32)
            for ref in ins[1:count]:
                total = total + ref[k].astype(F32)
            outs[k][...] = total.astype(BF16)
        ins, outs = ins[count:], outs[pieces:]


def join_sum_kernel(counts, *refs):
    base = 0
    for count in counts:
        total = refs[0][...].astype(F32)
        for ref in refs[1:count]:
            total = total + ref[...].astype(F32)
        refs[-1][base : base + total.shape[0], :] = total.astype(BF16)
        base += total.shape[0]
        refs = refs[count:]


def stack_kernel(*refs):
    for k, ref in enumerate(refs[:-1]):
        refs[-1][k] = ref[...]


def whole_spec(shape, single=True):
    mode = pl.Buffered(1) if single else None
    return pl.BlockSpec(shape, lambda *_: (0,) * len(shape), pipeline_mode=mode)


def part_spec(shape, index):
    def place(*_):
        return (index,) + (0,) * (len(shape) - 1)

    return pl.BlockSpec((1,) + tuple(shape[1:]), place, pipeline_mode=pl.Buffered(1))


def params(axes, limit=56 * MIB):
    return pltpu.CompilerParams(
        dimension_semantics=("arbitrary",) * axes, vmem_limit_bytes=limit
    )


def cost(flops, moved):
    return pl.CostEstimate(flops=int(flops), bytes_accessed=int(moved), transcendentals=0)


def sds(shape, dtype):
    return jax.ShapeDtypeStruct(shape, dtype)


ANY = pl.BlockSpec(memory_space=pl.ANY)


def run_state(info, start, tokens, halo, mask, vecs, weights, before):
    wqkv, wproj, wup, wdown = weights
    items, frames, grid_rows, cols, feats = tokens.shape
    lanes = items * grid_rows * cols
    half = (items, 1, SHIFT, cols, feats)

    def plane_spec(*shape):
        return pl.BlockSpec((1,) + shape, lambda t, info: (start + t,) + (0,) * len(shape))

    shapes = [
        (R1_ROWS, lanes, BF16),
        (R2_ROWS, lanes, BF16),
        (R3_ROWS, lanes, BF16),
        (3 * feats, lanes, BF16),
        (frames, HEADS, lanes, F32),
        (8, lanes, F32),
        (feats, lanes, F32),
    ]
    operands = [info, tokens, halo, mask, vecs, wqkv, wproj, wup, wdown]
    return pl.pallas_call(
        functools.partial(state_kernel, start=start, items=items),
        grid_spec=pltpu.PrefetchScalarGridSpec(
            num_scalar_prefetch=1,
            grid=(halo.shape[1],),
            in_specs=[
                pl.BlockSpec(half, lambda t, info: (0, start + t, 1, 0, 0)),
                pl.BlockSpec(half, lambda t, info: (0, t, 0, 0, 0)),
                whole_spec(mask.shape),
                whole_spec(vecs.shape),
                whole_spec(wqkv.shape),
                whole_spec(wproj.shape),
                part_spec(wup.shape, 0),
                part_spec(wdown.shape, 0),
            ]
            + [ANY] * len(before),
            out_specs=[plane_spec(*s[:-1]) for s in shapes],
            scratch_shapes=[
                pltpu.VMEM((frames, 2 * feats, lanes), BF16),
                pltpu.VMEM((lanes // 128 * (HEADS // 2), 64, 256), F32),
                pltpu.SemaphoreType.DMA(()),
            ],
        ),
        out_shape=[sds((frames,) + s[:-1], s[-1]) for s in shapes],
        input_output_aliases={len(operands) + k: k for k in range(len(before))},
        compiler_params=params(1, 60 * MIB),
        cost_estimate=cost(4.5e9 * 2 * halo.shape[1], 20e6 * halo.shape[1]),
        name="state",
    )(*operands, *before)


def run_last(info, x3, cotangent, cot_halo, vecs, weights):
    wup, wdown = weights
    items, frames, grid_rows, cols, feats = cotangent.shape
    lanes = x3.shape[2]
    hidden = wup.shape[2]
    half = (items, 1, SHIFT, cols, feats)
    own_spec = pl.BlockSpec(half, lambda t, info: (0, t, 1, 0, 0))
    halo_spec = pl.BlockSpec(half, lambda t, info: (0, t, 0, 0, 0))
    plane = pl.BlockSpec((1, feats, lanes), lambda t, info: (t, 0, 0))
    return pl.pallas_call(
        functools.partial(last_kernel, items=items),
        grid_spec=pltpu.PrefetchScalarGridSpec(
            num_scalar_prefetch=1,
            grid=(frames,),
            in_specs=[
                plane,
                own_spec,
                halo_spec,
                whole_spec(vecs.shape),
                part_spec(wup.shape, 1),
                part_spec(wdown.shape, 1),
            ],
            out_specs=[own_spec, halo_spec, plane]
            + [whole_spec((4, 4, 128, 512))] * 2
            + [whole_spec((8, 3584))],
            scratch_shapes=[
                pltpu.VMEM((feats, hidden), F32),
                pltpu.VMEM((hidden, feats), F32),
                pltpu.VMEM((3584, 128), F32),
                pltpu.VMEM((hidden, lanes), BF16),
                pltpu.VMEM((hidden, lanes), BF16),
            ],
        ),
        out_shape=[
            sds(cotangent.shape, BF16),
            sds(cot_halo.shape, BF16),
            sds((frames, feats, lanes), F32),
        ]
        + [sds((4, 4, 128, 512), BF16)] * 2
        + [sds((8, 3584), F32)],
        compiler_params=params(1, 50 * MIB),
        cost_estimate=cost(32e9 * 1.2, 40e6),
        name="last",
    )(info, x3, cotangent, cot_halo, vecs, wup, wdown)


def run_time(info, g3, r1, qkv2, p2, stats, vecs, weights, items):
    wqkv, wproj = weights
    frames, feats, lanes = g3.shape

    def plane_spec(*shape):
        return pl.BlockSpec(
            (1,) + shape,
            lambda s, info: (frames - 1 - s,) + (0,) * len(shape),
        )

    return pl.pallas_call(
        functools.partial(time_kernel, items=items),
        grid_spec=pltpu.PrefetchScalarGridSpec(
            num_scalar_prefetch=1,
            grid=(frames,),
            in_specs=[
                plane_spec(feats, lanes),
                plane_spec(R1_ROWS, lanes),
                whole_spec(qkv2.shape),
                plane_spec(frames, HEADS, lanes),
                plane_spec(8, lanes),
                whole_spec(vecs.shape),
                part_spec(wqkv.shape, 1),
                part_spec(wproj.shape, 1),
            ],
            out_specs=[
                plane_spec(feats, lanes),
                whole_spec((4, 4, 64, 512)),
                whole_spec((4, 4, 64, 512)),
                whole_spec((8, 1536)),
            ],
            scratch_shapes=[
                pltpu.VMEM((feats, 3 * feats), F32),
                pltpu.VMEM((feats, feats), F32),
                pltpu.VMEM((1536, 128), F32),
                pltpu.VMEM((frames, feats, lanes), BF16),
                pltpu.VMEM((frames, frames, HEADS, lanes), F32),
                pltpu.VMEM((frames, frames, HEADS, lanes), F32),
                pltpu.VMEM((3 * feats, lanes), BF16),
            ],
        ),
        out_shape=[
            sds((frames, feats, lanes), F32),
            sds((4, 4, 64, 512), BF16),
            sds((4, 4, 64, 512), BF16),
            sds((8, 1536), F32),
        ],
        compiler_params=params(1, 50 * MIB),
        cost_estimate=cost(30e9, 40e6),
        name="time",
    )(info, g3, r1, qkv2, p2, stats, vecs, wqkv, wproj)


def run_feed(info, g2, r3, stats, vecs, weights, passes, back):
    wup, wdown = weights
    planes, feats, lanes = g2.shape
    hidden = wup.shape[2]

    def plane_spec(*shape):
        return pl.BlockSpec((1,) + shape, lambda n, info: (n,) + (0,) * len(shape))

    return pl.pallas_call(
        functools.partial(feed_kernel, passes=len(passes)),
        grid_spec=pltpu.PrefetchScalarGridSpec(
            num_scalar_prefetch=1,
            grid=(planes,),
            in_specs=[
                plane_spec(feats, lanes),
                plane_spec(R3_ROWS, lanes),
                plane_spec(8, lanes),
                whole_spec(vecs.shape),
                part_spec(wup.shape, 0),
                part_spec(wdown.shape, 0),
            ]
            + [ANY] * (len(passes) + 1),
            out_specs=[
                plane_spec(feats, lanes),
                whole_spec((4, 4, 128, 512)),
                whole_spec((4, 4, 128, 512)),
                whole_spec((8, 3584)),
            ]
            + [ANY] * len(passes),
            scratch_shapes=[
                pltpu.VMEM((feats, hidden), F32),
                pltpu.VMEM((hidden, feats), F32),
                pltpu.VMEM((3584, 128), F32),
                pltpu.SemaphoreType.DMA(()),
            ],
        ),
        out_shape=[
            sds((planes, feats, lanes), F32),
            sds((4, 4, 128, 512), BF16),
            sds((4, 4, 128, 512), BF16),
            sds((8, 3584), F32),
        ]
        + [sds(p.shape, p.dtype) for p in passes],
        input_output_aliases={7 + k: 4 + k for k in range(len(passes))},
        compiler_params=params(1, 44 * MIB),
        cost_estimate=cost(30e9, 40e6),
        name="feed",
    )(info, g2, r3, stats, vecs, wup, wdown, *passes, back)


def run_space(info, start, count, g1, r2, stats, vecs, weights, shape, before, sums, passes):
    wqkv, wproj = weights
    items, frames, grid_rows, cols, feats = shape
    lanes = g1.shape[2]
    half = (items, 1, SHIFT, cols, feats)
    first, last = start == 0, start + count == frames

    def plane_spec(*tail):
        return pl.BlockSpec(
            (1,) + tail, lambda t, info: (start + t,) + (0,) * len(tail)
        )

    accs = [(feats, 3 * feats), (feats, feats), (1536, 128)]
    halves = [(4, 4, 80, 512), (4, 4, 80, 512)]
    in_specs = [
        plane_spec(feats, lanes),
        plane_spec(R2_ROWS, lanes),
        plane_spec(8, lanes),
        whole_spec(vecs.shape),
        part_spec(wqkv.shape, 0),
        part_spec(wproj.shape, 0),
    ]
    operands = [info, g1, r2, stats, vecs, wqkv, wproj]
    aliases = {}
    if not first:
        in_specs += [whole_spec(a) for a in accs] + [ANY]
        aliases = {len(operands) + 3: 0}
    in_specs += [whole_spec(v.shape) for v in sums]
    base = len(in_specs) + 1
    in_specs += [ANY] * len(passes)
    out_specs = [
        pl.BlockSpec(half, lambda t, info: (0, start + t, 1, 0, 0)),
        pl.BlockSpec(half, lambda t, info: (0, t, 0, 0, 0)),
    ]
    out_shape = [sds(shape, BF16), sds((items, count, SHIFT, cols, feats), BF16)]
    scratch = []
    if last:
        out_specs += [whole_spec(h) for h in halves]
        out_shape += [sds(h, BF16) for h in halves]
        scratch += [pltpu.VMEM(a, F32) for a in accs] + [pltpu.VMEM((32, 16, 128), F32)]
    else:
        out_specs += [whole_spec(a) for a in accs]
        out_shape += [sds(a, F32) for a in accs]
    aliases.update({base + k: len(out_specs) + k for k in range(len(passes))})
    out_specs += [ANY] * len(passes)
    out_shape += [sds(p.shape, p.dtype) for p in passes]
    return pl.pallas_call(
        functools.partial(space_kernel, first=first, last=last, passes=len(passes)),
        grid_spec=pltpu.PrefetchScalarGridSpec(
            num_scalar_prefetch=1,
            grid=(count,),
            in_specs=in_specs,
            out_specs=out_specs,
            scratch_shapes=scratch
            + [
                pltpu.VMEM((3 * feats, lanes), BF16),
                pltpu.VMEM((lanes // 128 * (HEADS // 2), 64, 256), F32),
                pltpu.VMEM((lanes // 128 * (HEADS // 2), 64, 256), BF16),
            ],
        ),
        out_shape=out_shape,
        input_output_aliases=aliases,
        compiler_params=params(1, 44 * MIB),
        cost_estimate=cost(7e9 * 2, 30e6),
        name="space",
    )(*operands, *before, *sums, *passes)


GRADS = [(2, 128, 2048), (2, 512, 512), (2, 128, 1536), (2, 128, 512)]


def grad_specs(slot):
    return [pl.BlockSpec((1,) + a[1:], lambda *_: (slot, 0, 0)) for a in GRADS]


def run_unpack(info, chip, other, outs):
    small = [(4, 128), (4, 128), (4, 128), (2, 512)] if outs else []
    return pl.pallas_call(
        functools.partial(unpack_kernel, vectors=bool(outs)),
        grid_spec=pltpu.PrefetchScalarGridSpec(
            num_scalar_prefetch=1,
            grid=(1,),
            in_specs=[whole_spec(chip.shape), whole_spec(other.shape)] + [ANY] * len(outs),
            out_specs=grad_specs(0 if outs else 1) + [whole_spec(a) for a in small],
            scratch_shapes=[pltpu.VMEM((8, 16, 128), F32)] if outs else [],
        ),
        out_shape=[sds(a, F32) for a in GRADS + small],
        input_output_aliases={3 + k: k for k in range(len(outs))},
        compiler_params=params(1, 24 * MIB),
        cost_estimate=cost(0, 6e6),
        name="unpack",
    )(info, chip, other, *outs)


def run_near(far, near, keep, taken):
    rows = far.shape[0] + keep.shape[1]
    return pl.pallas_call(
        near_kernel,
        out_shape=[sds((rows, 512), BF16)] * 2,
        compiler_params=params(0, 16 * MIB),
        name="near",
    )(far, near, keep, taken)


def split_sum(*groups):
    size = sum(a.size for g in groups for a in g)
    depths = [g[0].shape[-2] for g in groups]
    steps = next(n for n in (5, 4, 1) if all(d % (16 * n) == 0 for d in depths))

    def spec(shape):
        block = shape[:-2] + (shape[-2] // steps, shape[-1])
        return pl.BlockSpec(block, lambda i: (0,) * (len(shape) - 2) + (i, 0))

    ins = [a for g in groups for a in g]
    outs = [g[0].shape[1:] for g in groups for _ in range(g[0].shape[0])]
    flat = pl.pallas_call(
        functools.partial(split_sum_kernel, groups),
        grid=(steps,),
        in_specs=[spec(a.shape) for a in ins],
        out_specs=[spec(o) for o in outs],
        out_shape=[sds(o, BF16) for o in outs],
        compiler_params=params(1, 24 * MIB),
        cost_estimate=cost(size, 3 * size),
        name="split_sum",
    )(*ins)
    result = []
    for g in groups:
        result.append(flat[: g[0].shape[0]])
        flat = flat[g[0].shape[0] :]
    return result


def join_sum(*groups):
    ins = [a for g in groups for a in g]
    rows = sum(g[0].shape[0] for g in groups)
    return pl.pallas_call(
        functools.partial(join_sum_kernel, [len(g) for g in groups]),
        out_shape=sds((rows, 512), BF16),
        compiler_params=params(0, 16 * MIB),
        name="join_sum",
    )(*ins)


def run_stack(*arrays):
    shape = (len(arrays),) + arrays[0].shape
    return pl.pallas_call(
        stack_kernel, out_shape=sds(shape, BF16), compiler_params=params(0, 16 * MIB), name="stack"
    )(*arrays)


def after(values, *others):
    count = len(values)
    return pl.pallas_call(
        lambda *refs: None,
        in_specs=[ANY] * (count + len(others)),
        out_specs=[ANY] * count,
        out_shape=[sds(v.shape, v.dtype) for v in values],
        input_output_aliases={k: k for k in range(count)},
        compiler_params=params(0, 1 * MIB),
        name="after",
    )(*values, *others)


def shift(block, axis, distance):
    size = lax.axis_size(axis)
    return lax.ppermute(block, axis, [(i, (i + distance) % size) for i in range(size)])


def swap(block, axis, bits):
    return lax.ppermute(block, axis, [(i, i ^ bits) for i in range(lax.axis_size(axis))])


def upper_bits(total):
    bit = 8
    while bit < lax.axis_size("dp"):
        total = (total.astype(F32) + swap(total, "dp", bit).astype(F32)).astype(BF16)
        bit *= 2
    return total


def region_label(index, extent):
    return jnp.where(index < extent - WIN, 0, jnp.where(index < extent - SHIFT, 1, 2))


def tile_mask(cols):
    height = lax.axis_size("rows") * WIN
    row_label = region_label(lax.axis_index("rows") * WIN + jnp.arange(WIN), height)
    place = (jnp.arange(WIN) + SHIFT) % WIN
    col_label = region_label(jnp.arange(0, cols, WIN)[:, None] + place, cols)
    label = (row_label[None, :, None] * 3 + col_label[:, None, :]).reshape(-1, WIN * WIN)
    same = (label[:, :, None] == label[:, None, :]).astype(F32)
    pairs = same.reshape(-1, 2, WIN * WIN, WIN * WIN).transpose(0, 2, 1, 3)
    pairs = pairs.reshape(-1, WIN * WIN, 2 * WIN * WIN)
    return jnp.concatenate([pairs, pairs], axis=2)


def gather(mine):
    chip = run_stack(mine, *[swap(mine, "dp", 2 * j) for j in range(1, 4)])
    return chip, swap(chip, "dp", 1)


def on_device(
    tokens,
    video_flag,
    frame_count,
    norm_gain,
    norm_bias,
    w_qkv,
    w_proj,
    w_up,
    w_down,
    out_bias,
    up_bias,
    cotangent,
):
    items, frames, grid_rows, cols, feats = tokens.shape
    place = lax.rem(lax.axis_index("dp"), 8)
    row = lax.axis_index("rows")
    info = jnp.concatenate([jnp.stack([place, row]), video_flag, frame_count]).astype(jnp.int32)
    unpack_info = jnp.stack([lax.rem(place, 2), lax.div(place, 2)]).astype(jnp.int32)

    def column(*parts):
        flat = jnp.concatenate([p.reshape(-1) for p in parts])
        return jnp.broadcast_to(flat[:, None], (flat.shape[0], 128))

    early = (frames - 1) // 2
    halo = shift(tokens[:, :early, :SHIFT], "rows", -1)
    mask = tile_mask(cols)
    state_vecs = column(
        *[v[n] for n in range(3) for v in (norm_gain, norm_bias, out_bias)], up_bias[0]
    )
    last_vecs = column(norm_gain[3], norm_bias[3], out_bias[3], up_bias[1])
    time_vecs = column(norm_gain[2])
    feed_vecs = column(norm_gain[1])
    space_vecs = column(norm_gain[0])
    weights = (w_qkv, w_proj, w_up, w_down)
    (ahead,) = after([tokens[:, early:, :SHIFT]], state_vecs, mask)
    late_halo = shift(ahead, "rows", -1)
    kept = run_state(info, 0, tokens, halo, mask, state_vecs, weights, ())
    (ahead,) = after([cotangent[:, :, :SHIFT]], late_halo)
    cot_halo = shift(ahead, "rows", -1)
    kept = run_state(info, early, tokens, late_halo, mask, state_vecs, weights, kept)
    r1, r2, r3, qkv2, p2, stats, x3 = kept
    out_own, out_halo, g3, keep1, send1, sums1 = run_last(
        info, x3, cotangent, cot_halo, last_vecs, (w_up, w_down)
    )

    def cells(array, *taken):
        return list(split_sum([array, *taken])[0])

    def halves(array):
        return array.reshape((2, 2) + array.shape[1:])

    out_back = shift(out_halo, "rows", 1)
    core1 = swap(send1, "dp", 1)
    g2, keept, sendt, sumst = run_time(
        info, g3, r1, qkv2, p2, stats, time_vecs, (w_qkv, w_proj), items
    )
    cells1 = cells(keep1, core1)
    (sendt,) = after([sendt], cells1[0], out_back)

    across1 = [swap(cells1[j], "dp", 2 * j) for j in range(1, 4)]
    coret = swap(sendt, "dp", 1)
    g1, keep0, send0, sums0, mine1, layer_out = run_feed(
        info, g2, r3, stats, feed_vecs, (w_up, w_down), [cells1[0], out_own], out_back
    )
    rows1, cellst = split_sum([halves(mine1), *[halves(a) for a in across1]], [keept, coret])
    (send0,) = after([send0], rows1[0], cellst[0])

    along1 = swap(rows1[1], "rows", 2)
    acrosst = [swap(cellst[j], "dp", 2 * j) for j in range(1, 4)]
    core0 = swap(send0, "dp", 1)
    grad_own, back0, *accs, mine1, minet = run_space(
        info, 0, early, g1, r2, stats, space_vecs, (w_qkv, w_proj), tokens.shape, (), (),
        [rows1[0], cellst[0]],
    )
    rows1, rowst, cells0 = split_sum(
        [mine1, along1], [halves(minet), *[halves(a) for a in acrosst]], [keep0, core0]
    )
    (back0,) = after([back0], rows1[0], rowst[0], cells0[0])

    alongt = swap(rowst[1], "rows", 2)
    across0 = [swap(cells0[j], "dp", 2 * j) for j in range(1, 4)]
    backs = [shift(back0, "rows", 1)]
    grad_own, back1, keeps, sends, mine1, minet, mine0 = run_space(
        info, early, frames - early, g1, r2, stats, space_vecs, (w_qkv, w_proj), tokens.shape,
        accs + [grad_own], (sums1, sumst, sums0), [rows1[0], rowst[0], cells0[0]],
    )
    (rows0,) = split_sum([halves(mine0), *[halves(a) for a in across0]])
    keep_early, send_early = run_near(mine1, rows1[1], minet, alongt)
    (sends,) = after([sends], rows0[0], keep_early, backs[0])

    cores = swap(sends, "dp", 1)
    near = swap(send_early, "rows", 1)
    along0 = swap(rows0[1], "rows", 2)
    cellss = cells(keeps, cores)
    acrosss = [swap(cellss[j], "dp", 2 * j) for j in range(1, 4)]
    (near,) = after([near], cellss[0])
    sums_early = upper_bits(join_sum([keep_early, near]))
    pair_early = run_stack(sums_early, swap(sums_early, "dp", 2))
    rowss, rows0 = split_sum([cellss[0], *acrosss], [rows0[0], along0])
    alongs = [swap(rowss[z], "rows", z) for z in range(1, 4)]
    near0 = swap(rows0[1], "rows", 1)
    (pair_early,) = after([pair_early], rowss[0])
    other_pair = swap(pair_early, "dp", 4)
    late = upper_bits(join_sum([rows0[0], near0], [rowss[0], *alongs]))
    back1, other_pair = after([back1, other_pair], late)
    backs.append(shift(back1, "rows", 1))
    early_chip = run_stack(pair_early, other_pair)
    early_chip = early_chip.reshape((4,) + sums_early.shape)
    early_other = swap(early_chip, "dp", 1)
    late_chip, late_other = gather(late)
    grad_tokens = lax.dynamic_update_slice(grad_own, backs[0], (0, 0, 0, 0, 0))
    grad_tokens = lax.dynamic_update_slice(grad_tokens, backs[1], (0, early, 0, 0, 0))
    outs = run_unpack(unpack_info, early_chip, early_other, ())
    up, down, qkv, proj, gain, bias, outb, upb = run_unpack(
        unpack_info, late_chip, late_other, outs
    )
    return layer_out, grad_tokens, gain, bias, qkv, proj, up, down, outb, upb


def solution(mesh):
    split = P("dp", None, "rows", None, None)
    in_specs = (split, P("dp"), P("dp")) + (P(),) * 8 + (split,)
    out_specs = (
        split,
        split,
        P(None, "rows"),
        P(None, "rows"),
        P(None, "rows", None),
        P(None, "rows", None),
        P(None, "rows", None),
        P(None, "rows", None),
        P(None, "rows"),
        P(None, "rows"),
    )
    return jax.shard_map(
        on_device, mesh=mesh, in_specs=in_specs, out_specs=out_specs, check_vma=False
    )
```

```python
import functools
import math

import jax
import jax.numpy as jnp
from jax import lax
from jax.experimental import pallas as pl
from jax.experimental.pallas import tpu as pltpu
from jax.sharding import PartitionSpec as P

HEADS = 8
HEAD_DIM = 64
WIN = 8
SHIFT = 4
EPS = 1e-05
NEG = -1e30
SCALE = HEAD_DIM ** (-0.5)
BF16 = jnp.bfloat16
F32 = jnp.float32
NN = (((1,), (0,)), ((), ()))
NT = (((1,), (1,)), ((), ()))
TN = (((0,), (0,)), ((), ()))
CHUNK = 512
MIB = 1 << 20


def mm(left, right, dims=NN):
    return lax.dot_general(left, right, dims, preferred_element_type=F32)


def wide(column, lanes):
    return jnp.concatenate([column] * (lanes // column.shape[1]), axis=1)


def lane_sum(x):
    total = x[:, :128]
    for k in range(1, x.shape[1] // 128):
        total = total + x[:, 128 * k : 128 * (k + 1)]
    return total


def half_mask(shape):
    return lax.rem(lax.broadcasted_iota(jnp.int32, shape, len(shape) - 1), 128) < 64


def load_frame(own_ref, halo_ref):
    items = []
    for i in range(own_ref.shape[0]):
        grid = jnp.concatenate([own_ref[i, 0], halo_ref[i, 0]], axis=0).astype(F32)
        rows, cols, feats = grid.shape
        blocks = grid.reshape(rows, cols // WIN, WIN, feats)
        after = jnp.concatenate([blocks[:, 1:], blocks[:, :1]], axis=1)
        first = lax.broadcasted_iota(jnp.int32, blocks.shape, 2) < SHIFT
        tiles = jnp.where(first, after, blocks).transpose(1, 0, 2, 3)
        items.append(tiles.reshape(rows * cols, feats).astype(BF16).T)
    return jnp.concatenate(items, axis=1).astype(F32)


def store_frame(value, own_ref, halo_ref):
    count, _, half, cols, feats = own_ref.shape
    rows = 2 * half
    for i in range(count):
        part = value[:, rows * cols * i : rows * cols * (i + 1)]
        flat = part.astype(BF16).T.astype(F32)
        tiles = flat.reshape(cols // WIN, rows, WIN, feats).transpose(1, 0, 2, 3)
        before = jnp.concatenate([tiles[:, -1:], tiles[:, :-1]], axis=1)
        first = lax.broadcasted_iota(jnp.int32, tiles.shape, 2) < SHIFT
        grid = jnp.where(first, before, tiles).reshape(rows, cols, feats).astype(BF16)
        own_ref[i, 0] = grid[:half]
        halo_ref[i, 0] = grid[half:]


def item_row(values, lanes):
    size = lanes // len(values)
    return jnp.concatenate([jnp.full((1, size), v, F32) for v in values], axis=1)


def norm(x, gain, bias):
    center = x - jnp.mean(x, axis=0, keepdims=True)
    spread = jnp.mean(center * center, axis=0, keepdims=True)
    rstd = lax.rsqrt(spread + EPS)
    xhat = center * rstd
    return xhat, rstd, (xhat * gain + bias).astype(BF16)


def norm_back(d_norm, xhat, rstd, gain):
    grad_gain = d_norm * xhat
    e_mean = jnp.mean(d_norm * gain, axis=0, keepdims=True)
    x_mean = jnp.mean(grad_gain * gain, axis=0, keepdims=True)
    d_hidden = (d_norm * gain - e_mean - xhat * x_mean) * rstd
    return d_hidden, lane_sum(grad_gain), lane_sum(d_norm)


def gelu_parts(pre):
    low = pre.astype(BF16)
    upper = BF16(0.5) + BF16(0.5) * lax.erf(low * BF16(0.5**0.5))
    density = jnp.exp2(low * low * BF16(-0.5 / math.log(2))) * BF16(0.3989422804014327)
    return low * upper, upper + low * density


def head_rows(feats):
    row = lax.broadcasted_iota(jnp.int32, (16, feats), 0)
    head = lax.div(lax.broadcasted_iota(jnp.int32, (16, feats), 1), HEAD_DIM)
    return jnp.where(row == head, 1.0, 0.0).astype(BF16)


def head_spread(p):
    rows = []
    for h in range(HEADS):
        row = jnp.broadcast_to(p[h : h + 1, :], (16, p.shape[1])).astype(BF16)
        rows += [row] * (HEAD_DIM // 16)
    return jnp.concatenate(rows, axis=0)


def blocks_of(x, left, places):
    zero = jnp.zeros((HEAD_DIM, 128), x.dtype)
    halves = (x[:, :128], x[:, 128:])
    rows = []
    for place in places:
        half = halves[place // 2]
        kept = jnp.where(left, zero, half) if place % 2 else jnp.where(left, half, zero)
        rows.append(jnp.concatenate([zero, kept] if place // 2 else [kept, zero], axis=1))
    return jnp.concatenate(rows, axis=0)


BY_LANES = (0, 1, 2, 3)
BY_ROWS = (0, 2, 1, 3)


def unit_lanes(x, pair, hp):
    cols = slice(128 * pair, 128 * pair + 128)
    first = 128 * hp
    return jnp.concatenate([x[first : first + 64, cols], x[first + 64 : first + 128, cols]], axis=1)


def unit_rows(x, pair, hp):
    dims = slice(128 * hp, 128 * hp + 128)
    first = 128 * pair
    return jnp.concatenate([x[first : first + 64, dims], x[first + 64 : first + 128, dims]], axis=1)


def unit_slot(n):
    return slice(P0 + 64 * (n // 2), P0 + 64 * (n // 2) + 64), slice(256 * (n % 2), 256 * (n % 2) + 256)


def put_unit(ref, base, pair, hp, value):
    cols = slice(128 * pair, 128 * pair + 128)
    first = base + 128 * hp
    ref[first : first + 64, cols] = value[:, :128]
    ref[first + 64 : first + 128, cols] = value[:, 128:]


def spread_vectors(pieces_ref, space, feed, time, last):
    pieces_ref[...] = jnp.zeros_like(pieces_ref)
    starts = (512, 1024, 0)
    sources = [
        (part, first)
        for kind, first in enumerate(starts)
        for part, first in (
            (space, first),
            (feed, first),
            (time, first),
            (last, (0, 512, 1024)[kind]),
        )
    ]
    for z in range(4):
        rows = [part[0:1, first + 128 * z : first + 128 * z + 128] for part, first in sources]
        for part in (feed, last):
            for m in range(4):
                first = 1536 + 512 * z + 128 * m
                rows.append(part[0:1, first : first + 128])
        for r, row in enumerate(rows):
            pieces_ref[8 * z + r // 3, r % 3 : r % 3 + 1, :] = row


def pack(info, pieces, place, vectors=None):
    me, row = info[0], info[1]
    core, cell = lax.rem(me, 2), lax.div(me, 2)

    def step(z, carry):
        for c in range(2):
            for j in range(4):
                side = (core ^ c) * 4 + (cell ^ j)
                base = 0
                for acc_ref, depth in pieces:
                    first = pl.multiple_of((z ^ row) * (8 * depth) + side * depth, 16)
                    for k in range(acc_ref.shape[1] // 512):
                        part = acc_ref[pl.ds(first, depth), 512 * k : 512 * (k + 1)]
                        place(j, c, z, slice(base, base + depth), part.astype(BF16))
                        base += depth
                if vectors is not None:
                    part = vectors[(z ^ row) * 8 + side].astype(BF16)
                    part = jnp.concatenate([part, jnp.zeros((16, 384), BF16)], axis=1)
                    place(j, c, z, slice(base, base + 16), part)
        return carry

    lax.fori_loop(0, 4, step, 0)


def row_sums(acc):
    return lax.dot_general(
        jnp.ones((8, 128), F32), acc, NT, precision=lax.Precision.HIGHEST, preferred_element_type=F32
    )


A2, XHAT2, O2, R1_ROWS = 0, 512, 1024, 1536
C1, XHAT1, ACT0, SLOPE0, R3_ROWS = 0, 512, 1024, 3072, 5120
A0, XHAT0, O0, QKV0, P0, R2_ROWS = 0, 512, 1024, 1536, 3072, 3584


def state_kernel(
    info, own_ref, halo_ref, mask_ref, vec_ref, wqkv_ref, wproj_ref, wup_ref, wdown_ref, *refs, start, items
):
    r1_ref, r2_ref, r3_ref, qkv2_ref, p2_ref, stat_ref, x3_ref, kv_ref, scores_ref, sem = refs[-10:]
    step = pl.program_id(0)
    frame = start + step
    lanes = r1_ref.shape[2]
    feats = wqkv_ref.shape[1]

    def vec(index, size=512):
        return wide(vec_ref[512 * index : 512 * index + size, :], lanes)

    def earlier():
        return pltpu.make_async_copy(
            refs[3].at[pl.ds(0, start), pl.ds(512, 1024)], kv_ref.at[pl.ds(0, start)], sem
        )

    @pl.when(step == 0)
    def _():
        kv_ref[start:] = jnp.zeros_like(kv_ref[start:])
        if start:
            earlier().start()

    x0 = load_frame(own_ref, halo_ref)
    xhat0, rstd0, a0 = norm(x0, vec(0), vec(3))
    r2_ref[0, A0 : A0 + 512, :] = a0
    r2_ref[0, XHAT0 : XHAT0 + 512, :] = xhat0.astype(BF16)
    qkv = mm(wqkv_ref[0], a0, TN).astype(BF16)
    r2_ref[0, QKV0 : QKV0 + 1536, :] = qkv
    keys = qkv[512:1024].T
    left = half_mask((64, 128))
    units = [(pair, hp) for pair in range(lanes // 128) for hp in range(HEADS // 2)]
    for n, (pair, hp) in enumerate(units):
        query = blocks_of(unit_lanes(qkv[:512], pair, hp), left, BY_ROWS)
        scores = mm(unit_rows(keys, pair, hp), query) * SCALE
        scores_ref[n] = jnp.where(mask_ref[pair % mask_ref.shape[0]] > 0.5, scores, NEG)
    for n in range(len(units)):
        scores = scores_ref[n]
        exponent = jnp.exp(scores - jnp.max(scores, axis=0, keepdims=True))
        weights = exponent * (1.0 / jnp.sum(exponent, axis=0, keepdims=True))
        r2_ref[(0, *unit_slot(n))] = weights.astype(BF16)
    for n, (pair, hp) in enumerate(units):
        weights = blocks_of(r2_ref[(0, *unit_slot(n))], left, BY_LANES)
        mixed = mm(unit_lanes(qkv[1024:], pair, hp), weights).astype(BF16)
        put_unit(r2_ref.at[0], O0, pair, hp, mixed)
    x1 = x0 + mm(wproj_ref[0], r2_ref[0, O0 : O0 + 512, :], TN) + vec(6)

    xhat1, rstd1, c1 = norm(x1, vec(1), vec(4))
    r3_ref[0, C1 : C1 + 512, :] = c1
    r3_ref[0, XHAT1 : XHAT1 + 512, :] = xhat1.astype(BF16)
    for k in range(wup_ref.shape[2] // CHUNK):
        pre = mm(wup_ref[0, :, CHUNK * k : CHUNK * (k + 1)], c1, TN)
        pre = pre + wide(vec_ref[512 * 9 + CHUNK * k : 512 * 9 + CHUNK * (k + 1), :], lanes)
        act, slope = gelu_parts(pre)
        r3_ref[0, ACT0 + CHUNK * k : ACT0 + CHUNK * (k + 1), :] = act
        r3_ref[0, SLOPE0 + CHUNK * k : SLOPE0 + CHUNK * (k + 1), :] = slope
    x2 = x1 + vec(7) + mm(wdown_ref[0], r3_ref[0, ACT0:SLOPE0, :], TN)

    xhat2, rstd2, a2 = norm(x2, vec(2), vec(5))
    r1_ref[0, A2 : A2 + 512, :] = a2
    r1_ref[0, XHAT2 : XHAT2 + 512, :] = xhat2.astype(BF16)
    qkv = mm(wqkv_ref[1], a2, TN).astype(BF16)
    qkv2_ref[0] = qkv
    kv_ref[frame] = qkv[512:]
    if start:

        @pl.when(step == 0)
        def _():
            earlier().wait()

    query = qkv[:512] * BF16(SCALE)
    count = kv_ref.shape[0]
    products = jnp.concatenate([query * kv_ref[u, :512, :] for u in range(count)], axis=1)
    products = mm(head_rows(feats), products)
    scores = []
    for u in range(count):
        score = products[:HEADS, lanes * u : lanes * (u + 1)]
        scores.append(jnp.where(u <= frame, score, NEG))
    top = functools.reduce(jnp.maximum, scores)
    exponents = [jnp.exp(s - top) for s in scores]
    scale = 1.0 / sum(exponents)
    o2 = jnp.zeros((feats, lanes), BF16)
    for u in range(count):
        weight = exponents[u] * scale
        p2_ref[0, u] = weight
        o2 = o2 + head_spread(weight) * kv_ref[u, 512:, :]
    r1_ref[0, O2 : O2 + 512, :] = o2
    is_video = item_row([info[2 + i].astype(F32) for i in range(items)], lanes)
    x3_ref[0] = x2 + is_video * (mm(wproj_ref[1], o2, TN) + vec(8))
    stat_ref[0] = jnp.concatenate([rstd0, rstd1, rstd2, jnp.zeros((5, lanes), F32)], axis=0)


def last_kernel(
    info,
    x3_ref,
    cot_own_ref,
    cot_halo_ref,
    vec_ref,
    wup_ref,
    wdown_ref,
    out_own_ref,
    out_halo_ref,
    g3_ref,
    keep_ref,
    send_ref,
    sums_ref,
    acc_up,
    acc_down,
    acc_vec,
    act_ref,
    slope_ref,
    *,
    items,
):
    frame, frames = pl.program_id(0), pl.num_programs(0)
    feats, lanes = g3_ref.shape[1:]

    def vec(index, size=512):
        return wide(vec_ref[512 * index : 512 * index + size, :], lanes)

    @pl.when(frame == 0)
    def _():
        for acc in (acc_up, acc_down, acc_vec):
            acc[...] = jnp.zeros_like(acc)

    counts = [info[2 + items + i] for i in range(items)]
    is_valid = item_row([jnp.where(frame < c, 1.0, 0.0) for c in counts], lanes)
    g4 = load_frame(cot_own_ref, cot_halo_ref) * is_valid
    grad_low = g4.astype(BF16)
    x3 = x3_ref[0]
    xhat3, rstd3, c3 = norm(x3, vec(0), vec(1))
    chunks = [slice(CHUNK * k, CHUNK * (k + 1)) for k in range(wup_ref.shape[2] // CHUNK)]
    for part in chunks:
        pre = mm(wup_ref[0, :, part], c3, TN)
        pre = pre + wide(vec_ref[1536 + part.start : 1536 + part.stop, :], lanes)
        act_ref[part, :], slope_ref[part, :] = gelu_parts(pre)
    x4 = x3 + vec(2) + mm(wdown_ref[0], act_ref[...], TN)
    store_frame(x4 * is_valid, out_own_ref, out_halo_ref)
    for part in chunks:
        d_pre = (mm(wdown_ref[0, part, :], grad_low) * slope_ref[part, :]).astype(BF16)
        slope_ref[part, :] = d_pre
        rows = slice(1536 + part.start, 1536 + part.stop)
        acc_vec[rows, :] += lane_sum(d_pre.astype(F32))
    d_norm = mm(wup_ref[0], slope_ref[...])
    acc_up[...] += mm(c3, slope_ref[...], NT)
    acc_down[...] += mm(act_ref[...], grad_low, NT)
    d_hidden, gain_part, bias_part = norm_back(d_norm, xhat3, rstd3, vec(0))
    acc_vec[0:512, :] += gain_part
    acc_vec[512:1024, :] += bias_part
    acc_vec[1024:1536, :] += lane_sum(g4)
    g3_ref[0] = g4 + d_hidden

    @pl.when(frame == frames - 1)
    def _():
        pack(info, [(acc_up, 16), (acc_down, 64)], core_first(keep_ref, send_ref))
        sums_ref[...] = row_sums(acc_vec[...])


def time_step(t, qkv2_ref, p2_ref, grad_ref, weight_ref, score_ref, dqkv_ref):
    frames, _, lanes = qkv2_ref.shape
    feats = grad_ref.shape[1]
    grad = grad_ref[t]
    products = jnp.concatenate([grad * qkv2_ref[u, 1024:, :] for u in range(t + 1)], axis=1)
    products = mm(head_rows(feats), products)
    weights = [p2_ref[0, u] for u in range(t + 1)]
    d_weights = [products[:HEADS, lanes * u : lanes * (u + 1)] for u in range(t + 1)]
    inner = sum(w * d for w, d in zip(weights, d_weights))
    d_query = jnp.zeros((feats, lanes), BF16)
    for u in range(t + 1):
        d_score = (weights[u] * (d_weights[u] - inner)).astype(BF16).astype(F32)
        score_ref[t, u] = d_score
        weight_ref[t, u] = weights[u]
        d_query = d_query + head_spread(d_score) * qkv2_ref[u, 512:1024, :]
    dqkv_ref[:512, :] = d_query * BF16(SCALE)
    d_key = jnp.zeros((feats, lanes), BF16)
    d_value = jnp.zeros((feats, lanes), BF16)
    for v in range(t, frames):
        d_key = d_key + head_spread(score_ref[v, t]) * qkv2_ref[v, :512, :]
        d_value = d_value + head_spread(weight_ref[v, t]) * grad_ref[v]
    dqkv_ref[512:1024, :] = d_key * BF16(SCALE)
    dqkv_ref[1024:, :] = d_value


def time_kernel(
    info,
    g3_ref,
    r1_ref,
    qkv2_ref,
    p2_ref,
    stat_ref,
    vec_ref,
    wqkv_ref,
    wproj_ref,
    g2_ref,
    keep_ref,
    send_ref,
    sums_ref,
    acc_qkv,
    acc_proj,
    acc_vec,
    grad_ref,
    weight_ref,
    score_ref,
    dqkv_ref,
    *,
    items,
):
    step, frames = pl.program_id(0), pl.num_programs(0)
    frame = frames - 1 - step
    feats, lanes = g2_ref.shape[1:]

    @pl.when(step == 0)
    def _():
        for acc in (acc_qkv, acc_proj, acc_vec):
            acc[...] = jnp.zeros_like(acc)

    g3 = g3_ref[0]
    is_video = item_row([info[2 + i].astype(F32) for i in range(items)], lanes)
    d_attn = (g3 * is_video).astype(BF16)
    acc_proj[...] += mm(r1_ref[0, O2 : O2 + 512, :], d_attn, NT)
    acc_vec[0:512, :] += lane_sum(d_attn.astype(F32))
    grad_ref[frame] = mm(wproj_ref[0], d_attn).astype(BF16)
    for t in range(qkv2_ref.shape[0]):

        @pl.when(frame == t)
        def _():
            time_step(t, qkv2_ref, p2_ref, grad_ref, weight_ref, score_ref, dqkv_ref)

    d_qkv = dqkv_ref[...]
    acc_qkv[...] += mm(r1_ref[0, A2 : A2 + 512, :], d_qkv, NT)
    d_norm = mm(wqkv_ref[0], d_qkv)
    xhat = r1_ref[0, XHAT2 : XHAT2 + 512, :].astype(F32)
    gain = wide(vec_ref[...], lanes)
    d_hidden, gain_part, bias_part = norm_back(d_norm, xhat, stat_ref[0, 2:3, :], gain)
    acc_vec[512:1024, :] += gain_part
    acc_vec[1024:1536, :] += bias_part
    g2_ref[0] = g3 + d_hidden

    @pl.when(step == frames - 1)
    def _():
        pack(info, [(acc_qkv, 16), (acc_proj, 16)], core_first(keep_ref, send_ref))
        sums_ref[...] = row_sums(acc_vec[...])


def feed_kernel(info, g2_ref, r3_ref, stat_ref, vec_ref, wup_ref, wdown_ref, *refs, passes):
    back_ref, refs = refs[passes], refs[passes + 1 :]
    g1_ref, keep_ref, send_ref, sums_ref = refs[:4]
    acc_up, acc_down, acc_vec, sem = refs[-4:]
    own_ref = refs[3 + passes]
    put_back = pltpu.make_async_copy(back_ref, own_ref.at[:, :, : back_ref.shape[2]], sem)
    step, steps = pl.program_id(0), pl.num_programs(0)
    lanes = g1_ref.shape[2]

    @pl.when(step == 0)
    def _():
        put_back.start()
        for acc in (acc_up, acc_down, acc_vec):
            acc[...] = jnp.zeros_like(acc)

    g2 = g2_ref[0]
    grad_low = g2.astype(BF16)
    acc_vec[0:512, :] += lane_sum(grad_low.astype(F32))
    c1 = r3_ref[0, C1 : C1 + 512, :]
    d_norm = jnp.zeros(g2.shape, F32)
    size = 1024
    for k in range(wup_ref.shape[2] // size):
        part = slice(size * k, size * (k + 1))
        d_pre = mm(wdown_ref[0, part, :], grad_low)
        d_pre = (d_pre * r3_ref[0, SLOPE0 + size * k : SLOPE0 + size * (k + 1), :]).astype(BF16)
        d_norm = d_norm + mm(wup_ref[0, :, part], d_pre)
        acc_up[:, part] += mm(c1, d_pre, NT)
        acc_down[part, :] += mm(
            r3_ref[0, ACT0 + size * k : ACT0 + size * (k + 1), :], grad_low, NT
        )
        acc_vec[1536 + size * k : 1536 + size * (k + 1), :] += lane_sum(d_pre.astype(F32))
    xhat = r3_ref[0, XHAT1 : XHAT1 + 512, :].astype(F32)
    gain = wide(vec_ref[...], lanes)
    d_hidden, gain_part, bias_part = norm_back(d_norm, xhat, stat_ref[0, 1:2, :], gain)
    acc_vec[512:1024, :] += gain_part
    acc_vec[1024:1536, :] += bias_part
    g1_ref[0] = g2 + d_hidden

    @pl.when(step == steps - 1)
    def _():
        put_back.wait()
        pack(info, [(acc_up, 16), (acc_down, 64)], core_first(keep_ref, send_ref))
        sums_ref[...] = row_sums(acc_vec[...])


def core_first(keep_ref, send_ref):
    def place(j, c, z, rows, value):
        (send_ref if c else keep_ref)[j, z, rows, :] = value

    return place


def space_kernel(info, g1_ref, r2_ref, stat_ref, vec_ref, wqkv_ref, wproj_ref, *refs, first, last, passes):
    *refs, dqkv_ref, scores_ref, slope_ref = refs
    if not first:
        (qkv_in, proj_in, vec_in, _), refs = refs[:4], refs[4:]
    if last:
        (last_sums, time_sums, feed_sums), refs = refs[:3], refs[3:]
    out_own_ref, out_halo_ref, *refs = refs[passes:]
    if last:
        keep_ref, send_ref, *refs = refs
        *refs, vec_pieces = refs[passes:]
    acc_qkv, acc_proj, acc_vec = refs[:3]
    frame = pl.program_id(0)
    frames = pl.num_programs(0)
    lanes = r2_ref.shape[2]

    @pl.when(frame == 0)
    def _():
        for k, acc in enumerate((acc_qkv, acc_proj, acc_vec)):
            acc[...] = jnp.zeros_like(acc) if first else (qkv_in, proj_in, vec_in)[k][...]

    g1 = g1_ref[0]
    d_attn = g1.astype(BF16)
    acc_proj[...] += mm(r2_ref[0, O0 : O0 + 512, :], d_attn, NT)
    acc_vec[0:512, :] += lane_sum(d_attn.astype(F32))
    d_mixed = mm(wproj_ref[0], d_attn).astype(BF16)
    values = r2_ref[0, QKV0 + 1024 : QKV0 + 1536, :].T
    left = half_mask((64, 128))
    units = [(pair, hp) for pair in range(lanes // 128) for hp in range(HEADS // 2)]
    for n, (pair, hp) in enumerate(units):
        grad = blocks_of(unit_lanes(d_mixed, pair, hp), left, BY_ROWS)
        scores_ref[n] = mm(unit_rows(values, pair, hp), grad)
    for n, (pair, hp) in enumerate(units):
        d_weights = scores_ref[n]
        weights = r2_ref[(0, *unit_slot(n))].astype(F32)
        inner = jnp.sum(weights * d_weights, axis=0, keepdims=True)
        slope_ref[n] = (weights * (d_weights - inner)).astype(BF16)
    for n, (pair, hp) in enumerate(units):
        slope = blocks_of(slope_ref[n], left, BY_LANES)
        soft = blocks_of(r2_ref[(0, *unit_slot(n))], left, BY_LANES)
        grad = unit_lanes(d_mixed, pair, hp)
        query = unit_lanes(r2_ref[0, QKV0 : QKV0 + 512, :], pair, hp)
        key = unit_lanes(r2_ref[0, QKV0 + 512 : QKV0 + 1024, :], pair, hp)
        put_unit(dqkv_ref, 0, pair, hp, (mm(key, slope) * SCALE).astype(BF16))
        put_unit(dqkv_ref, 512, pair, hp, (mm(query, slope, NT) * SCALE).astype(BF16))
        put_unit(dqkv_ref, 1024, pair, hp, mm(grad, soft, NT).astype(BF16))
    d_qkv = dqkv_ref[...]
    acc_qkv[...] += mm(r2_ref[0, A0 : A0 + 512, :], d_qkv, NT)
    d_norm = mm(wqkv_ref[0], d_qkv)
    xhat = r2_ref[0, XHAT0 : XHAT0 + 512, :].astype(F32)
    gain = wide(vec_ref[...], lanes)
    d_hidden, gain_part, bias_part = norm_back(d_norm, xhat, stat_ref[0, 0:1, :], gain)
    acc_vec[512:1024, :] += gain_part
    acc_vec[1024:1536, :] += bias_part
    store_frame(g1 + d_hidden, out_own_ref, out_halo_ref)

    if last:

        @pl.when(frame == frames - 1)
        def _():
            spread_vectors(
                vec_pieces, row_sums(acc_vec[...]), feed_sums[...], time_sums[...], last_sums[...]
            )
            place = core_first(keep_ref, send_ref)
            pack(info, [(acc_qkv, 16), (acc_proj, 16)], place, vec_pieces)


PARTS = ((0, 16), (64, 64), (128, 16), (176, 16))
VECTOR_ROWS = 192


def unpack_kernel(info, mine_ref, other_ref, *refs, vectors):
    outs = refs[-9:-5] if vectors else refs
    for q in range(8):
        place = (q % 4) ^ info[1]
        own = info[0] == q // 4
        for out_ref, (base, depth) in zip(outs, PARTS):
            for k in range(out_ref.shape[2] // 512):
                rows = slice(base + depth * k, base + depth * (k + 1))
                value = jnp.where(own, mine_ref[place, rows, :], other_ref[place, rows, :])
                out_ref[0, depth * q : depth * (q + 1), 512 * k : 512 * (k + 1)] = value.astype(F32)
        if vectors:
            rows = slice(VECTOR_ROWS, VECTOR_ROWS + 16)
            value = jnp.where(own, mine_ref[place, rows, :128], other_ref[place, rows, :128])
            refs[-1][q] = value.astype(F32)
    if vectors:
        *small, upb_ref, vec_ref = refs[-5:]
        for k, ref in enumerate(small):
            for n in range(4):
                r = 4 * k + n
                ref[n : n + 1, :] = vec_ref[r // 3, r % 3 : r % 3 + 1, :]
        for k in range(2):
            for m in range(4):
                r = 12 + 4 * k + m
                upb_ref[k : k + 1, 128 * m : 128 * m + 128] = vec_ref[r // 3, r % 3 : r % 3 + 1, :]


def near_kernel(far_ref, near_ref, keep_ref, taken_ref, keep_out, send_out):
    depth = far_ref.shape[0]
    for k, (early, out) in enumerate(((far_ref, keep_out), (near_ref, send_out))):
        out[:depth, :] = early[...]
        out[depth:, :] = (keep_ref[k].astype(F32) + taken_ref[k].astype(F32)).astype(BF16)


def split_sum_kernel(groups, *refs):
    counts = [(len(g), g[0].shape[0]) for g in groups]
    ins, outs = refs[: sum(c for c, _ in counts)], refs[sum(c for c, _ in counts) :]
    for count, pieces in counts:
        for k in range(pieces):
            total = ins[0][k].astype(F32)
            for ref in ins[1:count]:
                total = total + ref[k].astype(F32)
            outs[k][...] = total.astype(BF16)
        ins, outs = ins[count:], outs[pieces:]


def join_sum_kernel(counts, *refs):
    base = 0
    for count in counts:
        total = refs[0][...].astype(F32)
        for ref in refs[1:count]:
            total = total + ref[...].astype(F32)
        refs[-1][base : base + total.shape[0], :] = total.astype(BF16)
        base += total.shape[0]
        refs = refs[count:]


def stack_kernel(*refs):
    for k, ref in enumerate(refs[:-1]):
        refs[-1][k] = ref[...]


def whole_spec(shape, single=True):
    mode = pl.Buffered(1) if single else None
    return pl.BlockSpec(shape, lambda *_: (0,) * len(shape), pipeline_mode=mode)


def part_spec(shape, index):
    def place(*_):
        return (index,) + (0,) * (len(shape) - 1)

    return pl.BlockSpec((1,) + tuple(shape[1:]), place, pipeline_mode=pl.Buffered(1))


def params(axes, limit=56 * MIB):
    return pltpu.CompilerParams(
        dimension_semantics=("arbitrary",) * axes, vmem_limit_bytes=limit
    )


def cost(flops, moved):
    return pl.CostEstimate(flops=int(flops), bytes_accessed=int(moved), transcendentals=0)


def sds(shape, dtype):
    return jax.ShapeDtypeStruct(shape, dtype)


ANY = pl.BlockSpec(memory_space=pl.ANY)


def run_state(info, start, tokens, halo, mask, vecs, weights, before):
    wqkv, wproj, wup, wdown = weights
    items, frames, grid_rows, cols, feats = tokens.shape
    lanes = items * grid_rows * cols
    half = (items, 1, SHIFT, cols, feats)

    def plane_spec(*shape):
        return pl.BlockSpec((1,) + shape, lambda t, info: (start + t,) + (0,) * len(shape))

    shapes = [
        (R1_ROWS, lanes, BF16),
        (R2_ROWS, lanes, BF16),
        (R3_ROWS, lanes, BF16),
        (3 * feats, lanes, BF16),
        (frames, HEADS, lanes, F32),
        (8, lanes, F32),
        (feats, lanes, F32),
    ]
    operands = [info, tokens, halo, mask, vecs, wqkv, wproj, wup, wdown]
    return pl.pallas_call(
        functools.partial(state_kernel, start=start, items=items),
        grid_spec=pltpu.PrefetchScalarGridSpec(
            num_scalar_prefetch=1,
            grid=(halo.shape[1],),
            in_specs=[
                pl.BlockSpec(half, lambda t, info: (0, start + t, 1, 0, 0)),
                pl.BlockSpec(half, lambda t, info: (0, t, 0, 0, 0)),
                whole_spec(mask.shape),
                whole_spec(vecs.shape),
                whole_spec(wqkv.shape),
                whole_spec(wproj.shape),
                part_spec(wup.shape, 0),
                part_spec(wdown.shape, 0),
            ]
            + [ANY] * len(before),
            out_specs=[plane_spec(*s[:-1]) for s in shapes],
            scratch_shapes=[
                pltpu.VMEM((frames, 2 * feats, lanes), BF16),
                pltpu.VMEM((lanes // 128 * (HEADS // 2), 64, 256), F32),
                pltpu.SemaphoreType.DMA(()),
            ],
        ),
        out_shape=[sds((frames,) + s[:-1], s[-1]) for s in shapes],
        input_output_aliases={len(operands) + k: k for k in range(len(before))},
        compiler_params=params(1, 60 * MIB),
        cost_estimate=cost(4.5e9 * 2 * halo.shape[1], 20e6 * halo.shape[1]),
        name="state",
    )(*operands, *before)


def run_last(info, x3, cotangent, cot_halo, vecs, weights):
    wup, wdown = weights
    items, frames, grid_rows, cols, feats = cotangent.shape
    lanes = x3.shape[2]
    hidden = wup.shape[2]
    half = (items, 1, SHIFT, cols, feats)
    own_spec = pl.BlockSpec(half, lambda t, info: (0, t, 1, 0, 0))
    halo_spec = pl.BlockSpec(half, lambda t, info: (0, t, 0, 0, 0))
    plane = pl.BlockSpec((1, feats, lanes), lambda t, info: (t, 0, 0))
    return pl.pallas_call(
        functools.partial(last_kernel, items=items),
        grid_spec=pltpu.PrefetchScalarGridSpec(
            num_scalar_prefetch=1,
            grid=(frames,),
            in_specs=[
                plane,
                own_spec,
                halo_spec,
                whole_spec(vecs.shape),
                part_spec(wup.shape, 1),
                part_spec(wdown.shape, 1),
            ],
            out_specs=[own_spec, halo_spec, plane]
            + [whole_spec((4, 4, 128, 512))] * 2
            + [whole_spec((8, 3584))],
            scratch_shapes=[
                pltpu.VMEM((feats, hidden), F32),
                pltpu.VMEM((hidden, feats), F32),
                pltpu.VMEM((3584, 128), F32),
                pltpu.VMEM((hidden, lanes), BF16),
                pltpu.VMEM((hidden, lanes), BF16),
            ],
        ),
        out_shape=[
            sds(cotangent.shape, BF16),
            sds(cot_halo.shape, BF16),
            sds((frames, feats, lanes), F32),
        ]
        + [sds((4, 4, 128, 512), BF16)] * 2
        + [sds((8, 3584), F32)],
        compiler_params=params(1, 40 * MIB),
        cost_estimate=cost(32e9 * 1.2, 40e6),
        name="last",
    )(info, x3, cotangent, cot_halo, vecs, wup, wdown)


def run_time(info, g3, r1, qkv2, p2, stats, vecs, weights, items):
    wqkv, wproj = weights
    frames, feats, lanes = g3.shape

    def plane_spec(*shape):
        return pl.BlockSpec(
            (1,) + shape,
            lambda s, info: (frames - 1 - s,) + (0,) * len(shape),
        )

    return pl.pallas_call(
        functools.partial(time_kernel, items=items),
        grid_spec=pltpu.PrefetchScalarGridSpec(
            num_scalar_prefetch=1,
            grid=(frames,),
            in_specs=[
                plane_spec(feats, lanes),
                plane_spec(R1_ROWS, lanes),
                whole_spec(qkv2.shape),
                plane_spec(frames, HEADS, lanes),
                plane_spec(8, lanes),
                whole_spec(vecs.shape),
                part_spec(wqkv.shape, 1),
                part_spec(wproj.shape, 1),
            ],
            out_specs=[
                plane_spec(feats, lanes),
                whole_spec((4, 4, 64, 512)),
                whole_spec((4, 4, 64, 512)),
                whole_spec((8, 1536)),
            ],
            scratch_shapes=[
                pltpu.VMEM((feats, 3 * feats), F32),
                pltpu.VMEM((feats, feats), F32),
                pltpu.VMEM((1536, 128), F32),
                pltpu.VMEM((frames, feats, lanes), BF16),
                pltpu.VMEM((frames, frames, HEADS, lanes), F32),
                pltpu.VMEM((frames, frames, HEADS, lanes), F32),
                pltpu.VMEM((3 * feats, lanes), BF16),
            ],
        ),
        out_shape=[
            sds((frames, feats, lanes), F32),
            sds((4, 4, 64, 512), BF16),
            sds((4, 4, 64, 512), BF16),
            sds((8, 1536), F32),
        ],
        compiler_params=params(1, 40 * MIB),
        cost_estimate=cost(30e9, 40e6),
        name="time",
    )(info, g3, r1, qkv2, p2, stats, vecs, wqkv, wproj)


def run_feed(info, g2, r3, stats, vecs, weights, passes, back):
    wup, wdown = weights
    planes, feats, lanes = g2.shape
    hidden = wup.shape[2]

    def plane_spec(*shape):
        return pl.BlockSpec((1,) + shape, lambda n, info: (n,) + (0,) * len(shape))

    return pl.pallas_call(
        functools.partial(feed_kernel, passes=len(passes)),
        grid_spec=pltpu.PrefetchScalarGridSpec(
            num_scalar_prefetch=1,
            grid=(planes,),
            in_specs=[
                plane_spec(feats, lanes),
                plane_spec(R3_ROWS, lanes),
                plane_spec(8, lanes),
                whole_spec(vecs.shape),
                part_spec(wup.shape, 0),
                part_spec(wdown.shape, 0),
            ]
            + [ANY] * (len(passes) + 1),
            out_specs=[
                plane_spec(feats, lanes),
                whole_spec((4, 4, 128, 512)),
                whole_spec((4, 4, 128, 512)),
                whole_spec((8, 3584)),
            ]
            + [ANY] * len(passes),
            scratch_shapes=[
                pltpu.VMEM((feats, hidden), F32),
                pltpu.VMEM((hidden, feats), F32),
                pltpu.VMEM((3584, 128), F32),
                pltpu.SemaphoreType.DMA(()),
            ],
        ),
        out_shape=[
            sds((planes, feats, lanes), F32),
            sds((4, 4, 128, 512), BF16),
            sds((4, 4, 128, 512), BF16),
            sds((8, 3584), F32),
        ]
        + [sds(p.shape, p.dtype) for p in passes],
        input_output_aliases={7 + k: 4 + k for k in range(len(passes))},
        compiler_params=params(1, 36 * MIB),
        cost_estimate=cost(30e9, 40e6),
        name="feed",
    )(info, g2, r3, stats, vecs, wup, wdown, *passes, back)


def run_space(info, start, count, g1, r2, stats, vecs, weights, shape, before, sums, passes):
    wqkv, wproj = weights
    items, frames, grid_rows, cols, feats = shape
    lanes = g1.shape[2]
    half = (items, 1, SHIFT, cols, feats)
    first, last = start == 0, start + count == frames

    def plane_spec(*tail):
        return pl.BlockSpec(
            (1,) + tail, lambda t, info: (start + t,) + (0,) * len(tail)
        )

    accs = [(feats, 3 * feats), (feats, feats), (1536, 128)]
    halves = [(4, 4, 80, 512), (4, 4, 80, 512)]
    in_specs = [
        plane_spec(feats, lanes),
        plane_spec(R2_ROWS, lanes),
        plane_spec(8, lanes),
        whole_spec(vecs.shape),
        part_spec(wqkv.shape, 0),
        part_spec(wproj.shape, 0),
    ]
    operands = [info, g1, r2, stats, vecs, wqkv, wproj]
    aliases = {}
    if not first:
        in_specs += [whole_spec(a) for a in accs] + [ANY]
        aliases = {len(operands) + 3: 0}
    in_specs += [whole_spec(v.shape) for v in sums]
    base = len(in_specs) + 1
    in_specs += [ANY] * len(passes)
    out_specs = [
        pl.BlockSpec(half, lambda t, info: (0, start + t, 1, 0, 0)),
        pl.BlockSpec(half, lambda t, info: (0, t, 0, 0, 0)),
    ]
    out_shape = [sds(shape, BF16), sds((items, count, SHIFT, cols, feats), BF16)]
    scratch = []
    if last:
        out_specs += [whole_spec(h) for h in halves]
        out_shape += [sds(h, BF16) for h in halves]
        scratch += [pltpu.VMEM(a, F32) for a in accs] + [pltpu.VMEM((32, 16, 128), F32)]
    else:
        out_specs += [whole_spec(a) for a in accs]
        out_shape += [sds(a, F32) for a in accs]
    aliases.update({base + k: len(out_specs) + k for k in range(len(passes))})
    out_specs += [ANY] * len(passes)
    out_shape += [sds(p.shape, p.dtype) for p in passes]
    return pl.pallas_call(
        functools.partial(space_kernel, first=first, last=last, passes=len(passes)),
        grid_spec=pltpu.PrefetchScalarGridSpec(
            num_scalar_prefetch=1,
            grid=(count,),
            in_specs=in_specs,
            out_specs=out_specs,
            scratch_shapes=scratch
            + [
                pltpu.VMEM((3 * feats, lanes), BF16),
                pltpu.VMEM((lanes // 128 * (HEADS // 2), 64, 256), F32),
                pltpu.VMEM((lanes // 128 * (HEADS // 2), 64, 256), BF16),
            ],
        ),
        out_shape=out_shape,
        input_output_aliases=aliases,
        compiler_params=params(1, 40 * MIB),
        cost_estimate=cost(7e9 * 2, 30e6),
        name="space",
    )(*operands, *before, *sums, *passes)


GRADS = [(2, 128, 2048), (2, 512, 512), (2, 128, 1536), (2, 128, 512)]


def grad_specs(slot):
    return [pl.BlockSpec((1,) + a[1:], lambda *_: (slot, 0, 0)) for a in GRADS]


def run_unpack(info, chip, other, outs):
    small = [(4, 128), (4, 128), (4, 128), (2, 512)] if outs else []
    return pl.pallas_call(
        functools.partial(unpack_kernel, vectors=bool(outs)),
        grid_spec=pltpu.PrefetchScalarGridSpec(
            num_scalar_prefetch=1,
            grid=(1,),
            in_specs=[whole_spec(chip.shape), whole_spec(other.shape)] + [ANY] * len(outs),
            out_specs=grad_specs(0 if outs else 1) + [whole_spec(a) for a in small],
            scratch_shapes=[pltpu.VMEM((8, 16, 128), F32)] if outs else [],
        ),
        out_shape=[sds(a, F32) for a in GRADS + small],
        input_output_aliases={3 + k: k for k in range(len(outs))},
        compiler_params=params(1, 24 * MIB),
        cost_estimate=cost(0, 6e6),
        name="unpack",
    )(info, chip, other, *outs)


def run_near(far, near, keep, taken):
    rows = far.shape[0] + keep.shape[1]
    return pl.pallas_call(
        near_kernel,
        out_shape=[sds((rows, 512), BF16)] * 2,
        compiler_params=params(0, 16 * MIB),
        name="near",
    )(far, near, keep, taken)


def split_sum(*groups):
    size = sum(a.size for g in groups for a in g)
    depths = [g[0].shape[-2] for g in groups]
    steps = next(n for n in (5, 4, 1) if all(d % (16 * n) == 0 for d in depths))

    def spec(shape):
        block = shape[:-2] + (shape[-2] // steps, shape[-1])
        return pl.BlockSpec(block, lambda i: (0,) * (len(shape) - 2) + (i, 0))

    ins = [a for g in groups for a in g]
    outs = [g[0].shape[1:] for g in groups for _ in range(g[0].shape[0])]
    flat = pl.pallas_call(
        functools.partial(split_sum_kernel, groups),
        grid=(steps,),
        in_specs=[spec(a.shape) for a in ins],
        out_specs=[spec(o) for o in outs],
        out_shape=[sds(o, BF16) for o in outs],
        compiler_params=params(1, 24 * MIB),
        cost_estimate=cost(size, 3 * size),
        name="split_sum",
    )(*ins)
    result = []
    for g in groups:
        result.append(flat[: g[0].shape[0]])
        flat = flat[g[0].shape[0] :]
    return result


def join_sum(*groups):
    ins = [a for g in groups for a in g]
    rows = sum(g[0].shape[0] for g in groups)
    return pl.pallas_call(
        functools.partial(join_sum_kernel, [len(g) for g in groups]),
        out_shape=sds((rows, 512), BF16),
        compiler_params=params(0, 16 * MIB),
        name="join_sum",
    )(*ins)


def run_stack(*arrays):
    shape = (len(arrays),) + arrays[0].shape
    return pl.pallas_call(
        stack_kernel, out_shape=sds(shape, BF16), compiler_params=params(0, 16 * MIB), name="stack"
    )(*arrays)


def after(values, *others):
    count = len(values)
    return pl.pallas_call(
        lambda *refs: None,
        in_specs=[ANY] * (count + len(others)),
        out_specs=[ANY] * count,
        out_shape=[sds(v.shape, v.dtype) for v in values],
        input_output_aliases={k: k for k in range(count)},
        compiler_params=params(0, 1 * MIB),
        name="after",
    )(*values, *others)


def shift(block, axis, distance):
    size = lax.axis_size(axis)
    return lax.ppermute(block, axis, [(i, (i + distance) % size) for i in range(size)])


def swap(block, axis, bits):
    return lax.ppermute(block, axis, [(i, i ^ bits) for i in range(lax.axis_size(axis))])


def upper_bits(total):
    bit = 8
    while bit < lax.axis_size("dp"):
        total = (total.astype(F32) + swap(total, "dp", bit).astype(F32)).astype(BF16)
        bit *= 2
    return total


def region_label(index, extent):
    return jnp.where(index < extent - WIN, 0, jnp.where(index < extent - SHIFT, 1, 2))


def tile_mask(cols):
    height = lax.axis_size("rows") * WIN
    row_label = region_label(lax.axis_index("rows") * WIN + jnp.arange(WIN), height)
    place = (jnp.arange(WIN) + SHIFT) % WIN
    col_label = region_label(jnp.arange(0, cols, WIN)[:, None] + place, cols)
    label = (row_label[None, :, None] * 3 + col_label[:, None, :]).reshape(-1, WIN * WIN)
    same = (label[:, :, None] == label[:, None, :]).astype(F32)
    pairs = same.reshape(-1, 2, WIN * WIN, WIN * WIN).transpose(0, 2, 1, 3)
    pairs = pairs.reshape(-1, WIN * WIN, 2 * WIN * WIN)
    return jnp.concatenate([pairs, pairs], axis=2)


def gather(mine):
    chip = run_stack(mine, *[swap(mine, "dp", 2 * j) for j in range(1, 4)])
    return chip, swap(chip, "dp", 1)


def on_device(
    tokens,
    video_flag,
    frame_count,
    norm_gain,
    norm_bias,
    w_qkv,
    w_proj,
    w_up,
    w_down,
    out_bias,
    up_bias,
    cotangent,
):
    items, frames, grid_rows, cols, feats = tokens.shape
    place = lax.rem(lax.axis_index("dp"), 8)
    row = lax.axis_index("rows")
    info = jnp.concatenate([jnp.stack([place, row]), video_flag, frame_count]).astype(jnp.int32)
    unpack_info = jnp.stack([lax.rem(place, 2), lax.div(place, 2)]).astype(jnp.int32)

    def column(*parts):
        rows = jnp.concatenate([p.reshape(-1, feats) for p in parts])
        rows = lax.optimization_barrier(rows)
        return jnp.broadcast_to(rows[:, :, None], rows.shape + (128,)).reshape(-1, 128)

    early = (frames - 1) // 2
    halo = shift(tokens[:, :early, :SHIFT], "rows", -1)
    mask = tile_mask(cols)
    state_vecs = column(norm_gain[:3], norm_bias[:3], out_bias[:3], up_bias[:1])
    last_vecs = column(norm_gain[3:], norm_bias[3:], out_bias[3:], up_bias[1:])
    time_vecs, feed_vecs, space_vecs = [column(norm_gain[n : n + 1]) for n in (2, 1, 0)]
    weights = (w_qkv, w_proj, w_up, w_down)
    (ahead,) = after([tokens[:, early:, :SHIFT]], state_vecs, mask)
    late_halo = shift(ahead, "rows", -1)
    kept = run_state(info, 0, tokens, halo, mask, state_vecs, weights, ())
    (ahead,) = after([cotangent[:, :, :SHIFT]], late_halo)
    cot_halo = shift(ahead, "rows", -1)
    kept = run_state(info, early, tokens, late_halo, mask, state_vecs, weights, kept)
    r1, r2, r3, qkv2, p2, stats, x3 = kept
    out_own, out_halo, g3, keep1, send1, sums1 = run_last(
        info, x3, cotangent, cot_halo, last_vecs, (w_up, w_down)
    )

    def cells(array, *taken):
        return list(split_sum([array, *taken])[0])

    def halves(array):
        return array.reshape((2, 2) + array.shape[1:])

    out_back = shift(out_halo, "rows", 1)
    core1 = swap(send1, "dp", 1)
    g2, keept, sendt, sumst = run_time(
        info, g3, r1, qkv2, p2, stats, time_vecs, (w_qkv, w_proj), items
    )
    cells1 = cells(keep1, core1)
    (sendt,) = after([sendt], cells1[0], out_back)

    across1 = [swap(cells1[j], "dp", 2 * j) for j in range(1, 4)]
    coret = swap(sendt, "dp", 1)
    g1, keep0, send0, sums0, mine1, layer_out = run_feed(
        info, g2, r3, stats, feed_vecs, (w_up, w_down), [cells1[0], out_own], out_back
    )
    rows1, cellst = split_sum([halves(mine1), *[halves(a) for a in across1]], [keept, coret])
    (send0,) = after([send0], rows1[0], cellst[0])

    along1 = swap(rows1[1], "rows", 2)
    acrosst = [swap(cellst[j], "dp", 2 * j) for j in range(1, 4)]
    core0 = swap(send0, "dp", 1)
    grad_own, back0, *accs, mine1, minet = run_space(
        info, 0, early, g1, r2, stats, space_vecs, (w_qkv, w_proj), tokens.shape, (), (),
        [rows1[0], cellst[0]],
    )
    rows1, rowst, cells0 = split_sum(
        [mine1, along1], [halves(minet), *[halves(a) for a in acrosst]], [keep0, core0]
    )
    (back0,) = after([back0], rows1[0], rowst[0], cells0[0])

    alongt = swap(rowst[1], "rows", 2)
    across0 = [swap(cells0[j], "dp", 2 * j) for j in range(1, 4)]
    backs = [shift(back0, "rows", 1)]
    grad_own, back1, keeps, sends, mine1, minet, mine0 = run_space(
        info, early, frames - early, g1, r2, stats, space_vecs, (w_qkv, w_proj), tokens.shape,
        accs + [grad_own], (sums1, sumst, sums0), [rows1[0], rowst[0], cells0[0]],
    )
    (rows0,) = split_sum([halves(mine0), *[halves(a) for a in across0]])
    keep_early, send_early = run_near(mine1, rows1[1], minet, alongt)
    (sends,) = after([sends], rows0[0], keep_early, backs[0])

    cores = swap(sends, "dp", 1)
    near = swap(send_early, "rows", 1)
    along0 = swap(rows0[1], "rows", 2)
    cellss = cells(keeps, cores)
    acrosss = [swap(cellss[j], "dp", 2 * j) for j in range(1, 4)]
    (near,) = after([near], cellss[0])
    sums_early = upper_bits(join_sum([keep_early, near]))
    pair_early = run_stack(sums_early, swap(sums_early, "dp", 2))
    rowss, rows0 = split_sum([cellss[0], *acrosss], [rows0[0], along0])
    alongs = [swap(rowss[z], "rows", z) for z in range(1, 4)]
    near0 = swap(rows0[1], "rows", 1)
    (back1,) = after([back1], rowss[0])
    backs.append(shift(back1, "rows", 1))
    other_pair = swap(pair_early, "dp", 4)
    late = upper_bits(join_sum([rows0[0], near0], [rowss[0], *alongs]))
    (other_pair,) = after([other_pair], late)
    early_chip = run_stack(pair_early, other_pair)
    early_chip = early_chip.reshape((4,) + sums_early.shape)
    early_other = swap(early_chip, "dp", 1)
    late_chip, late_other = gather(late)
    grad_tokens = lax.dynamic_update_slice(grad_own, backs[0], (0, 0, 0, 0, 0))
    grad_tokens = lax.dynamic_update_slice(grad_tokens, backs[1], (0, early, 0, 0, 0))
    outs = run_unpack(unpack_info, early_chip, early_other, ())
    up, down, qkv, proj, gain, bias, outb, upb = run_unpack(
        unpack_info, late_chip, late_other, outs
    )
    return layer_out, grad_tokens, gain, bias, qkv, proj, up, down, outb, upb


def solution(mesh):
    split = P("dp", None, "rows", None, None)
    in_specs = (split, P("dp"), P("dp")) + (P(),) * 8 + (split,)
    out_specs = (
        split,
        split,
        P(None, "rows"),
        P(None, "rows"),
        P(None, "rows", None),
        P(None, "rows", None),
        P(None, "rows", None),
        P(None, "rows", None),
        P(None, "rows"),
        P(None, "rows"),
    )
    return jax.shard_map(
        on_device, mesh=mesh, in_specs=in_specs, out_specs=out_specs, check_vma=False
    )
```

```python
import functools
import math

import jax
import jax.numpy as jnp
from jax import lax
from jax.experimental import pallas as pl
from jax.experimental.pallas import tpu as pltpu
from jax.sharding import PartitionSpec as P

HEADS = 8
HEAD_DIM = 64
WIN = 8
SHIFT = 4
EPS = 1e-05
NEG = -1e30
SCALE = HEAD_DIM ** (-0.5)
BF16 = jnp.bfloat16
F32 = jnp.float32
NN = (((1,), (0,)), ((), ()))
NT = (((1,), (1,)), ((), ()))
TN = (((0,), (0,)), ((), ()))
CHUNK = 512
MIB = 1 << 20


def mm(left, right, dims=NN):
    return lax.dot_general(left, right, dims, preferred_element_type=F32)


def wide(column, lanes):
    return jnp.concatenate([column] * (lanes // column.shape[1]), axis=1)


def lane_sum(x):
    total = x[:, :128]
    for k in range(1, x.shape[1] // 128):
        total = total + x[:, 128 * k : 128 * (k + 1)]
    return total


def half_mask(shape):
    return lax.rem(lax.broadcasted_iota(jnp.int32, shape, len(shape) - 1), 128) < 64


def load_frame(own_ref, halo_ref):
    items = []
    for i in range(own_ref.shape[0]):
        grid = jnp.concatenate([own_ref[i, 0], halo_ref[i, 0]], axis=0).astype(F32)
        rows, cols, feats = grid.shape
        blocks = grid.reshape(rows, cols // WIN, WIN, feats)
        after = jnp.concatenate([blocks[:, 1:], blocks[:, :1]], axis=1)
        first = lax.broadcasted_iota(jnp.int32, blocks.shape, 2) < SHIFT
        tiles = jnp.where(first, after, blocks).transpose(1, 0, 2, 3)
        items.append(tiles.reshape(rows * cols, feats).astype(BF16).T)
    return jnp.concatenate(items, axis=1).astype(F32)


def store_frame(value, own_ref, halo_ref):
    count, _, half, cols, feats = own_ref.shape
    rows = 2 * half
    for i in range(count):
        part = value[:, rows * cols * i : rows * cols * (i + 1)]
        flat = part.astype(BF16).T.astype(F32)
        tiles = flat.reshape(cols // WIN, rows, WIN, feats).transpose(1, 0, 2, 3)
        before = jnp.concatenate([tiles[:, -1:], tiles[:, :-1]], axis=1)
        first = lax.broadcasted_iota(jnp.int32, tiles.shape, 2) < SHIFT
        grid = jnp.where(first, before, tiles).reshape(rows, cols, feats).astype(BF16)
        own_ref[i, 0] = grid[:half]
        halo_ref[i, 0] = grid[half:]


def item_row(values, lanes):
    size = lanes // len(values)
    return jnp.concatenate([jnp.full((1, size), v, F32) for v in values], axis=1)


def norm(x, gain, bias):
    center = x - jnp.mean(x, axis=0, keepdims=True)
    spread = jnp.mean(center * center, axis=0, keepdims=True)
    rstd = lax.rsqrt(spread + EPS)
    xhat = center * rstd
    return xhat, rstd, (xhat * gain + bias).astype(BF16)


def norm_back(d_norm, xhat, rstd, gain):
    grad_gain = d_norm * xhat
    e_mean = jnp.mean(d_norm * gain, axis=0, keepdims=True)
    x_mean = jnp.mean(grad_gain * gain, axis=0, keepdims=True)
    d_hidden = (d_norm * gain - e_mean - xhat * x_mean) * rstd
    return d_hidden, lane_sum(grad_gain), lane_sum(d_norm)


def gelu_parts(pre):
    low = pre.astype(BF16)
    upper = BF16(0.5) + BF16(0.5) * lax.erf(low * BF16(0.5**0.5))
    density = jnp.exp2(low * low * BF16(-0.5 / math.log(2))) * BF16(0.3989422804014327)
    return low * upper, upper + low * density


def head_rows(feats):
    row = lax.broadcasted_iota(jnp.int32, (16, feats), 0)
    head = lax.div(lax.broadcasted_iota(jnp.int32, (16, feats), 1), HEAD_DIM)
    return jnp.where(row == head, 1.0, 0.0).astype(BF16)


def head_spread(p):
    rows = []
    for h in range(HEADS):
        row = jnp.broadcast_to(p[h : h + 1, :], (16, p.shape[1])).astype(BF16)
        rows += [row] * (HEAD_DIM // 16)
    return jnp.concatenate(rows, axis=0)


def blocks_of(x, left, places):
    zero = jnp.zeros((HEAD_DIM, 128), x.dtype)
    halves = (x[:, :128], x[:, 128:])
    rows = []
    for place in places:
        half = halves[place // 2]
        kept = jnp.where(left, zero, half) if place % 2 else jnp.where(left, half, zero)
        rows.append(jnp.concatenate([zero, kept] if place // 2 else [kept, zero], axis=1))
    return jnp.concatenate(rows, axis=0)


BY_LANES = (0, 1, 2, 3)
BY_ROWS = (0, 2, 1, 3)


def unit_lanes(x, pair, hp):
    cols = slice(128 * pair, 128 * pair + 128)
    first = 128 * hp
    return jnp.concatenate([x[first : first + 64, cols], x[first + 64 : first + 128, cols]], axis=1)


def unit_rows(x, pair, hp):
    dims = slice(128 * hp, 128 * hp + 128)
    first = 128 * pair
    return jnp.concatenate([x[first : first + 64, dims], x[first + 64 : first + 128, dims]], axis=1)


def unit_slot(n):
    return slice(P0 + 64 * (n // 2), P0 + 64 * (n // 2) + 64), slice(256 * (n % 2), 256 * (n % 2) + 256)


def put_unit(ref, base, pair, hp, value):
    cols = slice(128 * pair, 128 * pair + 128)
    first = base + 128 * hp
    ref[first : first + 64, cols] = value[:, :128]
    ref[first + 64 : first + 128, cols] = value[:, 128:]


def spread_vectors(pieces_ref, space, feed, time, last):
    pieces_ref[...] = jnp.zeros_like(pieces_ref)
    starts = (512, 1024, 0)
    sources = [
        (part, first)
        for kind, first in enumerate(starts)
        for part, first in (
            (space, first),
            (feed, first),
            (time, first),
            (last, (0, 512, 1024)[kind]),
        )
    ]
    for z in range(4):
        rows = [part[0:1, first + 128 * z : first + 128 * z + 128] for part, first in sources]
        for part in (feed, last):
            for m in range(4):
                first = 1536 + 512 * z + 128 * m
                rows.append(part[0:1, first : first + 128])
        for r, row in enumerate(rows):
            pieces_ref[8 * z + r // 3, r % 3 : r % 3 + 1, :] = row


def pack(info, pieces, place, vectors=None):
    me, row = info[0], info[1]
    core, cell = lax.rem(me, 2), lax.div(me, 2)

    def step(z, carry):
        for c in range(2):
            for j in range(4):
                side = (core ^ c) * 4 + (cell ^ j)
                base = 0
                for acc_ref, depth in pieces:
                    first = pl.multiple_of((z ^ row) * (8 * depth) + side * depth, 16)
                    for k in range(acc_ref.shape[1] // 512):
                        part = acc_ref[pl.ds(first, depth), 512 * k : 512 * (k + 1)]
                        place(j, c, z, slice(base, base + depth), part.astype(BF16))
                        base += depth
                if vectors is not None:
                    part = vectors[(z ^ row) * 8 + side].astype(BF16)
                    part = jnp.concatenate([part, jnp.zeros((16, 384), BF16)], axis=1)
                    place(j, c, z, slice(base, base + 16), part)
        return carry

    lax.fori_loop(0, 4, step, 0)


def row_sums(acc):
    return lax.dot_general(
        jnp.ones((8, 128), F32), acc, NT, precision=lax.Precision.HIGHEST, preferred_element_type=F32
    )


A2, XHAT2, O2, R1_ROWS = 0, 512, 1024, 1536
C1, XHAT1, ACT0, SLOPE0, R3_ROWS = 0, 512, 1024, 3072, 5120
A0, XHAT0, O0, QKV0, P0, R2_ROWS = 0, 512, 1024, 1536, 3072, 3584


def state_kernel(
    info, own_ref, halo_ref, mask_ref, vec_ref, wqkv_ref, wproj_ref, wup_ref, wdown_ref, *refs, start, items
):
    r1_ref, r2_ref, r3_ref, qkv2_ref, p2_ref, stat_ref, x3_ref, kv_ref, scores_ref, sem = refs[-10:]
    step = pl.program_id(0)
    frame = start + step
    lanes = r1_ref.shape[2]
    feats = wqkv_ref.shape[1]

    def vec(index, size=512):
        return wide(vec_ref[512 * index : 512 * index + size, :], lanes)

    def earlier():
        return pltpu.make_async_copy(
            refs[3].at[pl.ds(0, start), pl.ds(512, 1024)], kv_ref.at[pl.ds(0, start)], sem
        )

    @pl.when(step == 0)
    def _():
        kv_ref[start:] = jnp.zeros_like(kv_ref[start:])
        if start:
            earlier().start()

    x0 = load_frame(own_ref, halo_ref)
    xhat0, rstd0, a0 = norm(x0, vec(0), vec(3))
    r2_ref[0, A0 : A0 + 512, :] = a0
    r2_ref[0, XHAT0 : XHAT0 + 512, :] = xhat0.astype(BF16)
    qkv = mm(wqkv_ref[0], a0, TN).astype(BF16)
    r2_ref[0, QKV0 : QKV0 + 1536, :] = qkv
    keys = qkv[512:1024].T
    left = half_mask((64, 128))
    units = [(pair, hp) for pair in range(lanes // 128) for hp in range(HEADS // 2)]
    for n, (pair, hp) in enumerate(units):
        query = blocks_of(unit_lanes(qkv[:512], pair, hp), left, BY_ROWS)
        scores = mm(unit_rows(keys, pair, hp), query) * SCALE
        scores_ref[n] = jnp.where(mask_ref[pair % mask_ref.shape[0]] > 0.5, scores, NEG)
    for n in range(len(units)):
        scores = scores_ref[n]
        exponent = jnp.exp(scores - jnp.max(scores, axis=0, keepdims=True))
        weights = exponent * (1.0 / jnp.sum(exponent, axis=0, keepdims=True))
        r2_ref[(0, *unit_slot(n))] = weights.astype(BF16)
    for n, (pair, hp) in enumerate(units):
        weights = blocks_of(r2_ref[(0, *unit_slot(n))], left, BY_LANES)
        mixed = mm(unit_lanes(qkv[1024:], pair, hp), weights).astype(BF16)
        put_unit(r2_ref.at[0], O0, pair, hp, mixed)
    x1 = x0 + mm(wproj_ref[0], r2_ref[0, O0 : O0 + 512, :], TN) + vec(6)

    xhat1, rstd1, c1 = norm(x1, vec(1), vec(4))
    r3_ref[0, C1 : C1 + 512, :] = c1
    r3_ref[0, XHAT1 : XHAT1 + 512, :] = xhat1.astype(BF16)
    for k in range(wup_ref.shape[2] // CHUNK):
        pre = mm(wup_ref[0, :, CHUNK * k : CHUNK * (k + 1)], c1, TN)
        pre = pre + wide(vec_ref[512 * 9 + CHUNK * k : 512 * 9 + CHUNK * (k + 1), :], lanes)
        act, slope = gelu_parts(pre)
        r3_ref[0, ACT0 + CHUNK * k : ACT0 + CHUNK * (k + 1), :] = act
        r3_ref[0, SLOPE0 + CHUNK * k : SLOPE0 + CHUNK * (k + 1), :] = slope
    x2 = x1 + vec(7) + mm(wdown_ref[0], r3_ref[0, ACT0:SLOPE0, :], TN)

    xhat2, rstd2, a2 = norm(x2, vec(2), vec(5))
    r1_ref[0, A2 : A2 + 512, :] = a2
    r1_ref[0, XHAT2 : XHAT2 + 512, :] = xhat2.astype(BF16)
    qkv = mm(wqkv_ref[1], a2, TN).astype(BF16)
    qkv2_ref[0] = qkv
    kv_ref[frame] = qkv[512:]
    if start:

        @pl.when(step == 0)
        def _():
            earlier().wait()

    query = qkv[:512] * BF16(SCALE)
    count = kv_ref.shape[0]
    products = jnp.concatenate([query * kv_ref[u, :512, :] for u in range(count)], axis=1)
    products = mm(head_rows(feats), products)
    scores = []
    for u in range(count):
        score = products[:HEADS, lanes * u : lanes * (u + 1)]
        scores.append(jnp.where(u <= frame, score, NEG))
    top = functools.reduce(jnp.maximum, scores)
    exponents = [jnp.exp(s - top) for s in scores]
    scale = 1.0 / sum(exponents)
    o2 = jnp.zeros((feats, lanes), BF16)
    for u in range(count):
        weight = exponents[u] * scale
        p2_ref[0, u] = weight
        o2 = o2 + head_spread(weight) * kv_ref[u, 512:, :]
    r1_ref[0, O2 : O2 + 512, :] = o2
    is_video = item_row([info[2 + i].astype(F32) for i in range(items)], lanes)
    x3_ref[0] = x2 + is_video * (mm(wproj_ref[1], o2, TN) + vec(8))
    stat_ref[0] = jnp.concatenate([rstd0, rstd1, rstd2, jnp.zeros((5, lanes), F32)], axis=0)


def last_kernel(
    info,
    x3_ref,
    cot_own_ref,
    cot_halo_ref,
    vec_ref,
    wup_ref,
    wdown_ref,
    out_own_ref,
    out_halo_ref,
    g3_ref,
    keep_ref,
    send_ref,
    sums_ref,
    acc_up,
    acc_down,
    acc_vec,
    act_ref,
    slope_ref,
    *,
    items,
):
    frame, frames = pl.program_id(0), pl.num_programs(0)
    feats, lanes = g3_ref.shape[1:]

    def vec(index, size=512):
        return wide(vec_ref[512 * index : 512 * index + size, :], lanes)

    @pl.when(frame == 0)
    def _():
        for acc in (acc_up, acc_down, acc_vec):
            acc[...] = jnp.zeros_like(acc)

    counts = [info[2 + items + i] for i in range(items)]
    is_valid = item_row([jnp.where(frame < c, 1.0, 0.0) for c in counts], lanes)
    g4 = load_frame(cot_own_ref, cot_halo_ref) * is_valid
    grad_low = g4.astype(BF16)
    x3 = x3_ref[0]
    xhat3, rstd3, c3 = norm(x3, vec(0), vec(1))
    chunks = [slice(CHUNK * k, CHUNK * (k + 1)) for k in range(wup_ref.shape[2] // CHUNK)]
    for part in chunks:
        pre = mm(wup_ref[0, :, part], c3, TN)
        pre = pre + wide(vec_ref[1536 + part.start : 1536 + part.stop, :], lanes)
        act_ref[part, :], slope_ref[part, :] = gelu_parts(pre)
    x4 = x3 + vec(2) + mm(wdown_ref[0], act_ref[...], TN)
    store_frame(x4 * is_valid, out_own_ref, out_halo_ref)
    for part in chunks:
        d_pre = (mm(wdown_ref[0, part, :], grad_low) * slope_ref[part, :]).astype(BF16)
        slope_ref[part, :] = d_pre
        rows = slice(1536 + part.start, 1536 + part.stop)
        acc_vec[rows, :] += lane_sum(d_pre.astype(F32))
    d_norm = mm(wup_ref[0], slope_ref[...])
    acc_up[...] += mm(c3, slope_ref[...], NT)
    acc_down[...] += mm(act_ref[...], grad_low, NT)
    d_hidden, gain_part, bias_part = norm_back(d_norm, xhat3, rstd3, vec(0))
    acc_vec[0:512, :] += gain_part
    acc_vec[512:1024, :] += bias_part
    acc_vec[1024:1536, :] += lane_sum(g4)
    g3_ref[0] = g4 + d_hidden

    @pl.when(frame == frames - 1)
    def _():
        pack(info, [(acc_up, 16), (acc_down, 64)], core_first(keep_ref, send_ref))
        sums_ref[...] = row_sums(acc_vec[...])


def time_step(t, qkv2_ref, p2_ref, grad_ref, weight_ref, score_ref, dqkv_ref):
    frames, _, lanes = qkv2_ref.shape
    feats = grad_ref.shape[1]
    grad = grad_ref[t]
    products = jnp.concatenate([grad * qkv2_ref[u, 1024:, :] for u in range(t + 1)], axis=1)
    products = mm(head_rows(feats), products)
    weights = [p2_ref[0, u] for u in range(t + 1)]
    d_weights = [products[:HEADS, lanes * u : lanes * (u + 1)] for u in range(t + 1)]
    inner = sum(w * d for w, d in zip(weights, d_weights))
    d_query = jnp.zeros((feats, lanes), BF16)
    for u in range(t + 1):
        d_score = (weights[u] * (d_weights[u] - inner)).astype(BF16).astype(F32)
        score_ref[t, u] = d_score
        weight_ref[t, u] = weights[u]
        d_query = d_query + head_spread(d_score) * qkv2_ref[u, 512:1024, :]
    dqkv_ref[:512, :] = d_query * BF16(SCALE)
    d_key = jnp.zeros((feats, lanes), BF16)
    d_value = jnp.zeros((feats, lanes), BF16)
    for v in range(t, frames):
        d_key = d_key + head_spread(score_ref[v, t]) * qkv2_ref[v, :512, :]
        d_value = d_value + head_spread(weight_ref[v, t]) * grad_ref[v]
    dqkv_ref[512:1024, :] = d_key * BF16(SCALE)
    dqkv_ref[1024:, :] = d_value


def time_kernel(
    info,
    g3_ref,
    r1_ref,
    qkv2_ref,
    p2_ref,
    stat_ref,
    vec_ref,
    wqkv_ref,
    wproj_ref,
    g2_ref,
    keep_ref,
    send_ref,
    sums_ref,
    acc_qkv,
    acc_proj,
    acc_vec,
    grad_ref,
    weight_ref,
    score_ref,
    dqkv_ref,
    *,
    items,
):
    step, frames = pl.program_id(0), pl.num_programs(0)
    frame = frames - 1 - step
    feats, lanes = g2_ref.shape[1:]

    @pl.when(step == 0)
    def _():
        for acc in (acc_qkv, acc_proj, acc_vec):
            acc[...] = jnp.zeros_like(acc)

    g3 = g3_ref[0]
    is_video = item_row([info[2 + i].astype(F32) for i in range(items)], lanes)
    d_attn = (g3 * is_video).astype(BF16)
    acc_proj[...] += mm(r1_ref[0, O2 : O2 + 512, :], d_attn, NT)
    acc_vec[0:512, :] += lane_sum(d_attn.astype(F32))
    grad_ref[frame] = mm(wproj_ref[0], d_attn).astype(BF16)
    for t in range(qkv2_ref.shape[0]):

        @pl.when(frame == t)
        def _():
            time_step(t, qkv2_ref, p2_ref, grad_ref, weight_ref, score_ref, dqkv_ref)

    d_qkv = dqkv_ref[...]
    acc_qkv[...] += mm(r1_ref[0, A2 : A2 + 512, :], d_qkv, NT)
    d_norm = mm(wqkv_ref[0], d_qkv)
    xhat = r1_ref[0, XHAT2 : XHAT2 + 512, :].astype(F32)
    gain = wide(vec_ref[...], lanes)
    d_hidden, gain_part, bias_part = norm_back(d_norm, xhat, stat_ref[0, 2:3, :], gain)
    acc_vec[512:1024, :] += gain_part
    acc_vec[1024:1536, :] += bias_part
    g2_ref[0] = g3 + d_hidden

    @pl.when(step == frames - 1)
    def _():
        pack(info, [(acc_qkv, 16), (acc_proj, 16)], core_first(keep_ref, send_ref))
        sums_ref[...] = row_sums(acc_vec[...])


def feed_kernel(info, g2_ref, r3_ref, stat_ref, vec_ref, wup_ref, wdown_ref, *refs, passes):
    back_ref, refs = refs[passes], refs[passes + 1 :]
    g1_ref, keep_ref, send_ref, sums_ref = refs[:4]
    acc_up, acc_down, acc_vec, sem = refs[-4:]
    own_ref = refs[3 + passes]
    put_back = pltpu.make_async_copy(back_ref, own_ref.at[:, :, : back_ref.shape[2]], sem)
    step, steps = pl.program_id(0), pl.num_programs(0)
    lanes = g1_ref.shape[2]

    @pl.when(step == 0)
    def _():
        put_back.start()
        for acc in (acc_up, acc_down, acc_vec):
            acc[...] = jnp.zeros_like(acc)

    g2 = g2_ref[0]
    grad_low = g2.astype(BF16)
    acc_vec[0:512, :] += lane_sum(grad_low.astype(F32))
    c1 = r3_ref[0, C1 : C1 + 512, :]
    d_norm = jnp.zeros(g2.shape, F32)
    size = 1024
    for k in range(wup_ref.shape[2] // size):
        part = slice(size * k, size * (k + 1))
        d_pre = mm(wdown_ref[0, part, :], grad_low)
        d_pre = (d_pre * r3_ref[0, SLOPE0 + size * k : SLOPE0 + size * (k + 1), :]).astype(BF16)
        d_norm = d_norm + mm(wup_ref[0, :, part], d_pre)
        acc_up[:, part] += mm(c1, d_pre, NT)
        acc_down[part, :] += mm(
            r3_ref[0, ACT0 + size * k : ACT0 + size * (k + 1), :], grad_low, NT
        )
        acc_vec[1536 + size * k : 1536 + size * (k + 1), :] += lane_sum(d_pre.astype(F32))
    xhat = r3_ref[0, XHAT1 : XHAT1 + 512, :].astype(F32)
    gain = wide(vec_ref[...], lanes)
    d_hidden, gain_part, bias_part = norm_back(d_norm, xhat, stat_ref[0, 1:2, :], gain)
    acc_vec[512:1024, :] += gain_part
    acc_vec[1024:1536, :] += bias_part
    g1_ref[0] = g2 + d_hidden

    @pl.when(step == steps - 1)
    def _():
        put_back.wait()
        pack(info, [(acc_up, 16), (acc_down, 64)], core_first(keep_ref, send_ref))
        sums_ref[...] = row_sums(acc_vec[...])


def core_first(keep_ref, send_ref):
    def place(j, c, z, rows, value):
        (send_ref if c else keep_ref)[j, z, rows, :] = value

    return place


def space_kernel(info, g1_ref, r2_ref, stat_ref, vec_ref, wqkv_ref, wproj_ref, *refs, first, last, passes):
    *refs, dqkv_ref, scores_ref, slope_ref = refs
    if not first:
        (qkv_in, proj_in, vec_in, _), refs = refs[:4], refs[4:]
    if last:
        (last_sums, time_sums, feed_sums), refs = refs[:3], refs[3:]
    out_own_ref, out_halo_ref, *refs = refs[passes:]
    if last:
        keep_ref, send_ref, *refs = refs
        *refs, vec_pieces = refs[passes:]
    acc_qkv, acc_proj, acc_vec = refs[:3]
    frame = pl.program_id(0)
    frames = pl.num_programs(0)
    lanes = r2_ref.shape[2]

    @pl.when(frame == 0)
    def _():
        for k, acc in enumerate((acc_qkv, acc_proj, acc_vec)):
            acc[...] = jnp.zeros_like(acc) if first else (qkv_in, proj_in, vec_in)[k][...]

    g1 = g1_ref[0]
    d_attn = g1.astype(BF16)
    acc_proj[...] += mm(r2_ref[0, O0 : O0 + 512, :], d_attn, NT)
    acc_vec[0:512, :] += lane_sum(d_attn.astype(F32))
    d_mixed = mm(wproj_ref[0], d_attn).astype(BF16)
    values = r2_ref[0, QKV0 + 1024 : QKV0 + 1536, :].T
    left = half_mask((64, 128))
    units = [(pair, hp) for pair in range(lanes // 128) for hp in range(HEADS // 2)]
    for n, (pair, hp) in enumerate(units):
        grad = blocks_of(unit_lanes(d_mixed, pair, hp), left, BY_ROWS)
        scores_ref[n] = mm(unit_rows(values, pair, hp), grad)
    for n, (pair, hp) in enumerate(units):
        d_weights = scores_ref[n]
        weights = r2_ref[(0, *unit_slot(n))].astype(F32)
        inner = jnp.sum(weights * d_weights, axis=0, keepdims=True)
        slope_ref[n] = (weights * (d_weights - inner)).astype(BF16)
    for n, (pair, hp) in enumerate(units):
        slope = blocks_of(slope_ref[n], left, BY_LANES)
        soft = blocks_of(r2_ref[(0, *unit_slot(n))], left, BY_LANES)
        grad = unit_lanes(d_mixed, pair, hp)
        query = unit_lanes(r2_ref[0, QKV0 : QKV0 + 512, :], pair, hp)
        key = unit_lanes(r2_ref[0, QKV0 + 512 : QKV0 + 1024, :], pair, hp)
        put_unit(dqkv_ref, 0, pair, hp, (mm(key, slope) * SCALE).astype(BF16))
        put_unit(dqkv_ref, 512, pair, hp, (mm(query, slope, NT) * SCALE).astype(BF16))
        put_unit(dqkv_ref, 1024, pair, hp, mm(grad, soft, NT).astype(BF16))
    d_qkv = dqkv_ref[...]
    acc_qkv[...] += mm(r2_ref[0, A0 : A0 + 512, :], d_qkv, NT)
    d_norm = mm(wqkv_ref[0], d_qkv)
    xhat = r2_ref[0, XHAT0 : XHAT0 + 512, :].astype(F32)
    gain = wide(vec_ref[...], lanes)
    d_hidden, gain_part, bias_part = norm_back(d_norm, xhat, stat_ref[0, 0:1, :], gain)
    acc_vec[512:1024, :] += gain_part
    acc_vec[1024:1536, :] += bias_part
    store_frame(g1 + d_hidden, out_own_ref, out_halo_ref)

    if last:

        @pl.when(frame == frames - 1)
        def _():
            spread_vectors(
                vec_pieces, row_sums(acc_vec[...]), feed_sums[...], time_sums[...], last_sums[...]
            )
            place = core_first(keep_ref, send_ref)
            pack(info, [(acc_qkv, 16), (acc_proj, 16)], place, vec_pieces)


PARTS = ((0, 16), (64, 64), (128, 16), (176, 16))
VECTOR_ROWS = 192


def unpack_kernel(info, mine_ref, other_ref, *refs, vectors):
    outs = refs[-9:-5] if vectors else refs
    for q in range(8):
        place = (q % 4) ^ info[1]
        own = info[0] == q // 4
        for out_ref, (base, depth) in zip(outs, PARTS):
            for k in range(out_ref.shape[2] // 512):
                rows = slice(base + depth * k, base + depth * (k + 1))
                value = jnp.where(own, mine_ref[place, rows, :], other_ref[place, rows, :])
                out_ref[0, depth * q : depth * (q + 1), 512 * k : 512 * (k + 1)] = value.astype(F32)
        if vectors:
            rows = slice(VECTOR_ROWS, VECTOR_ROWS + 16)
            value = jnp.where(own, mine_ref[place, rows, :128], other_ref[place, rows, :128])
            refs[-1][q] = value.astype(F32)
    if vectors:
        *small, upb_ref, vec_ref = refs[-5:]
        for k, ref in enumerate(small):
            for n in range(4):
                r = 4 * k + n
                ref[n : n + 1, :] = vec_ref[r // 3, r % 3 : r % 3 + 1, :]
        for k in range(2):
            for m in range(4):
                r = 12 + 4 * k + m
                upb_ref[k : k + 1, 128 * m : 128 * m + 128] = vec_ref[r // 3, r % 3 : r % 3 + 1, :]


def near_kernel(far_ref, near_ref, keep_ref, taken_ref, keep_out, send_out):
    depth = far_ref.shape[0]
    for k, (early, out) in enumerate(((far_ref, keep_out), (near_ref, send_out))):
        out[:depth, :] = early[...]
        out[depth:, :] = (keep_ref[k].astype(F32) + taken_ref[k].astype(F32)).astype(BF16)


def split_sum_kernel(groups, *refs):
    counts = [(len(g), g[0].shape[0]) for g in groups]
    ins, outs = refs[: sum(c for c, _ in counts)], refs[sum(c for c, _ in counts) :]
    for count, pieces in counts:
        for k in range(pieces):
            total = ins[0][k].astype(F32)
            for ref in ins[1:count]:
                total = total + ref[k].astype(F32)
            outs[k][...] = total.astype(BF16)
        ins, outs = ins[count:], outs[pieces:]


def join_sum_kernel(counts, *refs):
    base = 0
    for count in counts:
        total = refs[0][...].astype(F32)
        for ref in refs[1:count]:
            total = total + ref[...].astype(F32)
        refs[-1][base : base + total.shape[0], :] = total.astype(BF16)
        base += total.shape[0]
        refs = refs[count:]


def stack_kernel(*refs):
    for k, ref in enumerate(refs[:-1]):
        refs[-1][k] = ref[...]


def whole_spec(shape, single=True):
    mode = pl.Buffered(1) if single else None
    return pl.BlockSpec(shape, lambda *_: (0,) * len(shape), pipeline_mode=mode)


def part_spec(shape, index):
    def place(*_):
        return (index,) + (0,) * (len(shape) - 1)

    return pl.BlockSpec((1,) + tuple(shape[1:]), place, pipeline_mode=pl.Buffered(1))


def params(axes, limit=56 * MIB):
    return pltpu.CompilerParams(
        dimension_semantics=("arbitrary",) * axes, vmem_limit_bytes=limit
    )


def cost(flops, moved):
    return pl.CostEstimate(flops=int(flops), bytes_accessed=int(moved), transcendentals=0)


def sds(shape, dtype):
    return jax.ShapeDtypeStruct(shape, dtype)


ANY = pl.BlockSpec(memory_space=pl.ANY)


def run_state(info, start, tokens, halo, mask, vecs, weights, before):
    wqkv, wproj, wup, wdown = weights
    items, frames, grid_rows, cols, feats = tokens.shape
    lanes = items * grid_rows * cols
    half = (items, 1, SHIFT, cols, feats)

    def plane_spec(*shape):
        return pl.BlockSpec((1,) + shape, lambda t, info: (start + t,) + (0,) * len(shape))

    shapes = [
        (R1_ROWS, lanes, BF16),
        (R2_ROWS, lanes, BF16),
        (R3_ROWS, lanes, BF16),
        (3 * feats, lanes, BF16),
        (frames, HEADS, lanes, F32),
        (8, lanes, F32),
        (feats, lanes, F32),
    ]
    operands = [info, tokens, halo, mask, vecs, wqkv, wproj, wup, wdown]
    return pl.pallas_call(
        functools.partial(state_kernel, start=start, items=items),
        grid_spec=pltpu.PrefetchScalarGridSpec(
            num_scalar_prefetch=1,
            grid=(halo.shape[1],),
            in_specs=[
                pl.BlockSpec(half, lambda t, info: (0, start + t, 1, 0, 0)),
                pl.BlockSpec(half, lambda t, info: (0, t, 0, 0, 0)),
                whole_spec(mask.shape),
                whole_spec(vecs.shape),
                whole_spec(wqkv.shape),
                whole_spec(wproj.shape),
                part_spec(wup.shape, 0),
                part_spec(wdown.shape, 0),
            ]
            + [ANY] * len(before),
            out_specs=[plane_spec(*s[:-1]) for s in shapes],
            scratch_shapes=[
                pltpu.VMEM((frames, 2 * feats, lanes), BF16),
                pltpu.VMEM((lanes // 128 * (HEADS // 2), 64, 256), F32),
                pltpu.SemaphoreType.DMA(()),
            ],
        ),
        out_shape=[sds((frames,) + s[:-1], s[-1]) for s in shapes],
        input_output_aliases={len(operands) + k: k for k in range(len(before))},
        compiler_params=params(1, 60 * MIB),
        cost_estimate=cost(4.5e9 * 2 * halo.shape[1], 20e6 * halo.shape[1]),
        name="state",
    )(*operands, *before)


def run_last(info, x3, cotangent, cot_halo, vecs, weights):
    wup, wdown = weights
    items, frames, grid_rows, cols, feats = cotangent.shape
    lanes = x3.shape[2]
    hidden = wup.shape[2]
    half = (items, 1, SHIFT, cols, feats)
    own_spec = pl.BlockSpec(half, lambda t, info: (0, t, 1, 0, 0))
    halo_spec = pl.BlockSpec(half, lambda t, info: (0, t, 0, 0, 0))
    plane = pl.BlockSpec((1, feats, lanes), lambda t, info: (t, 0, 0))
    return pl.pallas_call(
        functools.partial(last_kernel, items=items),
        grid_spec=pltpu.PrefetchScalarGridSpec(
            num_scalar_prefetch=1,
            grid=(frames,),
            in_specs=[
                plane,
                own_spec,
                halo_spec,
                whole_spec(vecs.shape),
                part_spec(wup.shape, 1),
                part_spec(wdown.shape, 1),
            ],
            out_specs=[own_spec, halo_spec, plane]
            + [whole_spec((4, 4, 128, 512))] * 2
            + [whole_spec((8, 3584))],
            scratch_shapes=[
                pltpu.VMEM((feats, hidden), F32),
                pltpu.VMEM((hidden, feats), F32),
                pltpu.VMEM((3584, 128), F32),
                pltpu.VMEM((hidden, lanes), BF16),
                pltpu.VMEM((hidden, lanes), BF16),
            ],
        ),
        out_shape=[
            sds(cotangent.shape, BF16),
            sds(cot_halo.shape, BF16),
            sds((frames, feats, lanes), F32),
        ]
        + [sds((4, 4, 128, 512), BF16)] * 2
        + [sds((8, 3584), F32)],
        compiler_params=params(1, 40 * MIB),
        cost_estimate=cost(32e9 * 1.2, 40e6),
        name="last",
    )(info, x3, cotangent, cot_halo, vecs, wup, wdown)


def run_time(info, g3, r1, qkv2, p2, stats, vecs, weights, items):
    wqkv, wproj = weights
    frames, feats, lanes = g3.shape

    def plane_spec(*shape):
        return pl.BlockSpec(
            (1,) + shape,
            lambda s, info: (frames - 1 - s,) + (0,) * len(shape),
        )

    return pl.pallas_call(
        functools.partial(time_kernel, items=items),
        grid_spec=pltpu.PrefetchScalarGridSpec(
            num_scalar_prefetch=1,
            grid=(frames,),
            in_specs=[
                plane_spec(feats, lanes),
                plane_spec(R1_ROWS, lanes),
                whole_spec(qkv2.shape),
                plane_spec(frames, HEADS, lanes),
                plane_spec(8, lanes),
                whole_spec(vecs.shape),
                part_spec(wqkv.shape, 1),
                part_spec(wproj.shape, 1),
            ],
            out_specs=[
                plane_spec(feats, lanes),
                whole_spec((4, 4, 64, 512)),
                whole_spec((4, 4, 64, 512)),
                whole_spec((8, 1536)),
            ],
            scratch_shapes=[
                pltpu.VMEM((feats, 3 * feats), F32),
                pltpu.VMEM((feats, feats), F32),
                pltpu.VMEM((1536, 128), F32),
                pltpu.VMEM((frames, feats, lanes), BF16),
                pltpu.VMEM((frames, frames, HEADS, lanes), F32),
                pltpu.VMEM((frames, frames, HEADS, lanes), F32),
                pltpu.VMEM((3 * feats, lanes), BF16),
            ],
        ),
        out_shape=[
            sds((frames, feats, lanes), F32),
            sds((4, 4, 64, 512), BF16),
            sds((4, 4, 64, 512), BF16),
            sds((8, 1536), F32),
        ],
        compiler_params=params(1, 40 * MIB),
        cost_estimate=cost(30e9, 40e6),
        name="time",
    )(info, g3, r1, qkv2, p2, stats, vecs, wqkv, wproj)


def run_feed(info, g2, r3, stats, vecs, weights, passes, back):
    wup, wdown = weights
    planes, feats, lanes = g2.shape
    hidden = wup.shape[2]

    def plane_spec(*shape):
        return pl.BlockSpec((1,) + shape, lambda n, info: (n,) + (0,) * len(shape))

    return pl.pallas_call(
        functools.partial(feed_kernel, passes=len(passes)),
        grid_spec=pltpu.PrefetchScalarGridSpec(
            num_scalar_prefetch=1,
            grid=(planes,),
            in_specs=[
                plane_spec(feats, lanes),
                plane_spec(R3_ROWS, lanes),
                plane_spec(8, lanes),
                whole_spec(vecs.shape),
                part_spec(wup.shape, 0),
                part_spec(wdown.shape, 0),
            ]
            + [ANY] * (len(passes) + 1),
            out_specs=[
                plane_spec(feats, lanes),
                whole_spec((4, 4, 128, 512)),
                whole_spec((4, 4, 128, 512)),
                whole_spec((8, 3584)),
            ]
            + [ANY] * len(passes),
            scratch_shapes=[
                pltpu.VMEM((feats, hidden), F32),
                pltpu.VMEM((hidden, feats), F32),
                pltpu.VMEM((3584, 128), F32),
                pltpu.SemaphoreType.DMA(()),
            ],
        ),
        out_shape=[
            sds((planes, feats, lanes), F32),
            sds((4, 4, 128, 512), BF16),
            sds((4, 4, 128, 512), BF16),
            sds((8, 3584), F32),
        ]
        + [sds(p.shape, p.dtype) for p in passes],
        input_output_aliases={7 + k: 4 + k for k in range(len(passes))},
        compiler_params=params(1, 36 * MIB),
        cost_estimate=cost(30e9, 40e6),
        name="feed",
    )(info, g2, r3, stats, vecs, wup, wdown, *passes, back)


def run_space(info, start, count, g1, r2, stats, vecs, weights, shape, before, sums, passes):
    wqkv, wproj = weights
    items, frames, grid_rows, cols, feats = shape
    lanes = g1.shape[2]
    half = (items, 1, SHIFT, cols, feats)
    first, last = start == 0, start + count == frames

    def plane_spec(*tail):
        return pl.BlockSpec(
            (1,) + tail, lambda t, info: (start + t,) + (0,) * len(tail)
        )

    accs = [(feats, 3 * feats), (feats, feats), (1536, 128)]
    halves = [(4, 4, 80, 512), (4, 4, 80, 512)]
    in_specs = [
        plane_spec(feats, lanes),
        plane_spec(R2_ROWS, lanes),
        plane_spec(8, lanes),
        whole_spec(vecs.shape),
        part_spec(wqkv.shape, 0),
        part_spec(wproj.shape, 0),
    ]
    operands = [info, g1, r2, stats, vecs, wqkv, wproj]
    aliases = {}
    if not first:
        in_specs += [whole_spec(a) for a in accs] + [ANY]
        aliases = {len(operands) + 3: 0}
    in_specs += [whole_spec(v.shape) for v in sums]
    base = len(in_specs) + 1
    in_specs += [ANY] * len(passes)
    out_specs = [
        pl.BlockSpec(half, lambda t, info: (0, start + t, 1, 0, 0)),
        pl.BlockSpec(half, lambda t, info: (0, t, 0, 0, 0)),
    ]
    out_shape = [sds(shape, BF16), sds((items, count, SHIFT, cols, feats), BF16)]
    scratch = []
    if last:
        out_specs += [whole_spec(h) for h in halves]
        out_shape += [sds(h, BF16) for h in halves]
        scratch += [pltpu.VMEM(a, F32) for a in accs] + [pltpu.VMEM((32, 16, 128), F32)]
    else:
        out_specs += [whole_spec(a) for a in accs]
        out_shape += [sds(a, F32) for a in accs]
    aliases.update({base + k: len(out_specs) + k for k in range(len(passes))})
    out_specs += [ANY] * len(passes)
    out_shape += [sds(p.shape, p.dtype) for p in passes]
    return pl.pallas_call(
        functools.partial(space_kernel, first=first, last=last, passes=len(passes)),
        grid_spec=pltpu.PrefetchScalarGridSpec(
            num_scalar_prefetch=1,
            grid=(count,),
            in_specs=in_specs,
            out_specs=out_specs,
            scratch_shapes=scratch
            + [
                pltpu.VMEM((3 * feats, lanes), BF16),
                pltpu.VMEM((lanes // 128 * (HEADS // 2), 64, 256), F32),
                pltpu.VMEM((lanes // 128 * (HEADS // 2), 64, 256), BF16),
            ],
        ),
        out_shape=out_shape,
        input_output_aliases=aliases,
        compiler_params=params(1, 40 * MIB),
        cost_estimate=cost(7e9 * 2, 30e6),
        name="space",
    )(*operands, *before, *sums, *passes)


GRADS = [(2, 128, 2048), (2, 512, 512), (2, 128, 1536), (2, 128, 512)]


def grad_specs(slot):
    return [pl.BlockSpec((1,) + a[1:], lambda *_: (slot, 0, 0)) for a in GRADS]


def run_unpack(info, chip, other, outs):
    small = [(4, 128), (4, 128), (4, 128), (2, 512)] if outs else []
    return pl.pallas_call(
        functools.partial(unpack_kernel, vectors=bool(outs)),
        grid_spec=pltpu.PrefetchScalarGridSpec(
            num_scalar_prefetch=1,
            grid=(1,),
            in_specs=[whole_spec(chip.shape), whole_spec(other.shape)] + [ANY] * len(outs),
            out_specs=grad_specs(0 if outs else 1) + [whole_spec(a) for a in small],
            scratch_shapes=[pltpu.VMEM((8, 16, 128), F32)] if outs else [],
        ),
        out_shape=[sds(a, F32) for a in GRADS + small],
        input_output_aliases={3 + k: k for k in range(len(outs))},
        compiler_params=params(1, 24 * MIB),
        cost_estimate=cost(0, 0),
        name="unpack",
    )(info, chip, other, *outs)


def run_near(far, near, keep, taken):
    rows = far.shape[0] + keep.shape[1]
    return pl.pallas_call(
        near_kernel,
        out_shape=[sds((rows, 512), BF16)] * 2,
        compiler_params=params(0, 16 * MIB),
        name="near",
    )(far, near, keep, taken)


def split_sum(*groups):
    size = sum(a.size for g in groups for a in g)
    depths = [g[0].shape[-2] for g in groups]
    steps = next(n for n in (5, 4, 1) if all(d % (16 * n) == 0 for d in depths))

    def spec(shape):
        block = shape[:-2] + (shape[-2] // steps, shape[-1])
        return pl.BlockSpec(block, lambda i: (0,) * (len(shape) - 2) + (i, 0))

    ins = [a for g in groups for a in g]
    outs = [g[0].shape[1:] for g in groups for _ in range(g[0].shape[0])]
    flat = pl.pallas_call(
        functools.partial(split_sum_kernel, groups),
        grid=(steps,),
        in_specs=[spec(a.shape) for a in ins],
        out_specs=[spec(o) for o in outs],
        out_shape=[sds(o, BF16) for o in outs],
        compiler_params=params(1, 24 * MIB),
        cost_estimate=cost(size, 3 * size),
        name="split_sum",
    )(*ins)
    result = []
    for g in groups:
        result.append(flat[: g[0].shape[0]])
        flat = flat[g[0].shape[0] :]
    return result


def join_sum(*groups):
    ins = [a for g in groups for a in g]
    rows = sum(g[0].shape[0] for g in groups)
    return pl.pallas_call(
        functools.partial(join_sum_kernel, [len(g) for g in groups]),
        out_shape=sds((rows, 512), BF16),
        compiler_params=params(0, 16 * MIB),
        name="join_sum",
    )(*ins)


def run_stack(*arrays):
    shape = (len(arrays),) + arrays[0].shape
    return pl.pallas_call(
        stack_kernel, out_shape=sds(shape, BF16), compiler_params=params(0, 16 * MIB), name="stack"
    )(*arrays)


def after(values, *others):
    count = len(values)
    return pl.pallas_call(
        lambda *refs: None,
        in_specs=[ANY] * (count + len(others)),
        out_specs=[ANY] * count,
        out_shape=[sds(v.shape, v.dtype) for v in values],
        input_output_aliases={k: k for k in range(count)},
        compiler_params=params(0, 1 * MIB),
        name="after",
    )(*values, *others)


def shift(block, axis, distance):
    size = lax.axis_size(axis)
    return lax.ppermute(block, axis, [(i, (i + distance) % size) for i in range(size)])


def swap(block, axis, bits):
    return lax.ppermute(block, axis, [(i, i ^ bits) for i in range(lax.axis_size(axis))])


def upper_bits(total):
    bit = 8
    while bit < lax.axis_size("dp"):
        total = (total.astype(F32) + swap(total, "dp", bit).astype(F32)).astype(BF16)
        bit *= 2
    return total


def region_label(index, extent):
    return jnp.where(index < extent - WIN, 0, jnp.where(index < extent - SHIFT, 1, 2))


def tile_mask(cols):
    height = lax.axis_size("rows") * WIN
    row_label = region_label(lax.axis_index("rows") * WIN + jnp.arange(WIN), height)
    place = (jnp.arange(WIN) + SHIFT) % WIN
    col_label = region_label(jnp.arange(0, cols, WIN)[:, None] + place, cols)
    label = (row_label[None, :, None] * 3 + col_label[:, None, :]).reshape(-1, WIN * WIN)
    same = (label[:, :, None] == label[:, None, :]).astype(F32)
    pairs = same.reshape(-1, 2, WIN * WIN, WIN * WIN).transpose(0, 2, 1, 3)
    pairs = pairs.reshape(-1, WIN * WIN, 2 * WIN * WIN)
    return jnp.concatenate([pairs, pairs], axis=2)


def gather(mine):
    chip = run_stack(mine, *[swap(mine, "dp", 2 * j) for j in range(1, 4)])
    return chip, swap(chip, "dp", 1)


def on_device(
    tokens,
    video_flag,
    frame_count,
    norm_gain,
    norm_bias,
    w_qkv,
    w_proj,
    w_up,
    w_down,
    out_bias,
    up_bias,
    cotangent,
):
    items, frames, grid_rows, cols, feats = tokens.shape
    place = lax.rem(lax.axis_index("dp"), 8)
    row = lax.axis_index("rows")
    info = jnp.concatenate([jnp.stack([place, row]), video_flag, frame_count]).astype(jnp.int32)
    unpack_info = jnp.stack([lax.rem(place, 2), lax.div(place, 2)]).astype(jnp.int32)

    def column(*parts):
        rows = jnp.concatenate([p.reshape(-1, feats) for p in parts])
        rows = lax.optimization_barrier(rows)
        return jnp.broadcast_to(rows[:, :, None], rows.shape + (128,)).reshape(-1, 128)

    early = (frames - 1) // 2
    halo = shift(tokens[:, :early, :SHIFT], "rows", -1)
    mask = tile_mask(cols)
    state_vecs = column(norm_gain[:3], norm_bias[:3], out_bias[:3], up_bias[:1])
    last_vecs = column(norm_gain[3:], norm_bias[3:], out_bias[3:], up_bias[1:])
    time_vecs, feed_vecs, space_vecs = [column(norm_gain[n : n + 1]) for n in (2, 1, 0)]
    weights = (w_qkv, w_proj, w_up, w_down)
    (ahead,) = after([tokens[:, early:, :SHIFT]], state_vecs, mask)
    late_halo = shift(ahead, "rows", -1)
    kept = run_state(info, 0, tokens, halo, mask, state_vecs, weights, ())
    (ahead,) = after([cotangent[:, :, :SHIFT]], late_halo)
    cot_halo = shift(ahead, "rows", -1)
    kept = run_state(info, early, tokens, late_halo, mask, state_vecs, weights, kept)
    r1, r2, r3, qkv2, p2, stats, x3 = kept
    out_own, out_halo, g3, keep1, send1, sums1 = run_last(
        info, x3, cotangent, cot_halo, last_vecs, (w_up, w_down)
    )

    def cells(array, *taken):
        return list(split_sum([array, *taken])[0])

    def halves(array):
        return array.reshape((2, 2) + array.shape[1:])

    out_back = shift(out_halo, "rows", 1)
    core1 = swap(send1, "dp", 1)
    g2, keept, sendt, sumst = run_time(
        info, g3, r1, qkv2, p2, stats, time_vecs, (w_qkv, w_proj), items
    )
    cells1 = cells(keep1, core1)
    (sendt,) = after([sendt], cells1[0], out_back)

    across1 = [swap(cells1[j], "dp", 2 * j) for j in range(1, 4)]
    coret = swap(sendt, "dp", 1)
    g1, keep0, send0, sums0, mine1, layer_out = run_feed(
        info, g2, r3, stats, feed_vecs, (w_up, w_down), [cells1[0], out_own], out_back
    )
    rows1, cellst = split_sum([halves(mine1), *[halves(a) for a in across1]], [keept, coret])
    (send0,) = after([send0], rows1[0], cellst[0])

    along1 = swap(rows1[1], "rows", 2)
    acrosst = [swap(cellst[j], "dp", 2 * j) for j in range(1, 4)]
    core0 = swap(send0, "dp", 1)
    grad_own, back0, *accs, mine1, minet = run_space(
        info, 0, early, g1, r2, stats, space_vecs, (w_qkv, w_proj), tokens.shape, (), (),
        [rows1[0], cellst[0]],
    )
    rows1, rowst, cells0 = split_sum(
        [mine1, along1], [halves(minet), *[halves(a) for a in acrosst]], [keep0, core0]
    )
    (back0,) = after([back0], rows1[0], rowst[0], cells0[0])

    alongt = swap(rowst[1], "rows", 2)
    across0 = [swap(cells0[j], "dp", 2 * j) for j in range(1, 4)]
    backs = [shift(back0, "rows", 1)]
    grad_own, back1, keeps, sends, mine1, minet, mine0 = run_space(
        info, early, frames - early, g1, r2, stats, space_vecs, (w_qkv, w_proj), tokens.shape,
        accs + [grad_own], (sums1, sumst, sums0), [rows1[0], rowst[0], cells0[0]],
    )
    (rows0,) = split_sum([halves(mine0), *[halves(a) for a in across0]])
    keep_early, send_early = run_near(mine1, rows1[1], minet, alongt)
    (sends,) = after([sends], rows0[0], keep_early, backs[0])

    cores = swap(sends, "dp", 1)
    near = swap(send_early, "rows", 1)
    along0 = swap(rows0[1], "rows", 2)
    cellss = cells(keeps, cores)
    acrosss = [swap(cellss[j], "dp", 2 * j) for j in range(1, 4)]
    (near,) = after([near], cellss[0])
    sums_early = upper_bits(join_sum([keep_early, near]))
    pair_early = run_stack(sums_early, swap(sums_early, "dp", 2))
    rowss, rows0 = split_sum([cellss[0], *acrosss], [rows0[0], along0])
    alongs = [swap(rowss[z], "rows", z) for z in range(1, 4)]
    near0 = swap(rows0[1], "rows", 1)
    (back1,) = after([back1], rowss[0])
    backs.append(shift(back1, "rows", 1))
    other_pair = swap(pair_early, "dp", 4)
    late = upper_bits(join_sum([rows0[0], near0], [rowss[0], *alongs]))
    (other_pair,) = after([other_pair], late)
    early_chip = run_stack(pair_early, other_pair)
    early_chip = early_chip.reshape((4,) + sums_early.shape)
    early_other = swap(early_chip, "dp", 1)
    late_chip, late_other = gather(late)
    grad_tokens = lax.dynamic_update_slice(grad_own, backs[0], (0, 0, 0, 0, 0))
    outs = run_unpack(unpack_info, early_chip, early_other, ())
    up, down, qkv, proj, gain, bias, outb, upb = run_unpack(
        unpack_info, late_chip, late_other, outs
    )
    (grad_tokens,) = after([grad_tokens], gain)
    grad_tokens = lax.dynamic_update_slice(grad_tokens, backs[1], (0, early, 0, 0, 0))
    return layer_out, grad_tokens, gain, bias, qkv, proj, up, down, outb, upb


def solution(mesh):
    split = P("dp", None, "rows", None, None)
    in_specs = (split, P("dp"), P("dp")) + (P(),) * 8 + (split,)
    out_specs = (
        split,
        split,
        P(None, "rows"),
        P(None, "rows"),
        P(None, "rows", None),
        P(None, "rows", None),
        P(None, "rows", None),
        P(None, "rows", None),
        P(None, "rows"),
        P(None, "rows"),
    )
    return jax.shard_map(
        on_device, mesh=mesh, in_specs=in_specs, out_specs=out_specs, check_vma=False
    )
```
